32 devices in a mesh: lat: 8 (over z, x), head: 4 (over y, core).
Axes of the slice: x: 2, y: 2, z: 4, core: 2. Of those that a mesh axis runs over, the one named last changes fastest.
Arguments:
- level_tokens: bfloat16 [4096, 13, 1024], P('lat'), may hold values from -400 to 400
- ln_gain: float32 [1024], replicated, may hold values from 0.25 to 1.75
- key_weight: bfloat16 [1024, 1024], P(None, 'head'), may hold values from -0.1875 to 0.1875
- value_weight: bfloat16 [1024, 1024], P(None, 'head'), may hold values from -0.1875 to 0.1875
- out_weight: bfloat16 [1024, 1024], P('head'), may hold values from -0.1875 to 0.1875
- ocean_queries: bfloat16 [4096, 4, 1024], P('lat', None, 'head'), may hold values from -600 to 600
- send_slots: int32 [8, 8, 64], P('lat'), may hold values from -1 to 511, as said below
Outputs:
- ocean_out: bfloat16 [4096, 4, 1024], P('lat', None, 'head')
The draws below stay inside these ranges and needn't reach their ends.
Inputs may be any that keep to these rules, and one draw needn't show every extreme that they name: `send_slots`: entry [h, o, k] is a patch index within stripe h, or -1 for an empty slot. The live entries of one stripe are distinct, and in each [h, o] row the live entries come first. In every draw some owner has all 64 slots of every stripe live.
All inputs are finite; a program needn't handle non-finite values.
Results may differ from the reference program's by a relative error of at most 0.013.
The reference program's roundings to bfloat16 on the way count: a program that leaves them out, or rounds other values in their place, can miss the bound.
Values may be sent and summed in bfloat16 or wider, within the bound.
No kernel may reach another device: no remote copies, remote signals or barrier semaphores. Data moves between devices by JAX's collectives and lax.ppermute only.
A program may use at most 128 MiB of HBM per device.

```python
import math
import jax
import jax.numpy as jnp
from jax import lax

D = 1024
HEAD_DIM = 64
LEV = 13
LATENTS = 4
P_DEV = 512
CAPS = 64
PATCHES = 4096
SLOTS = 4096
N_LAT = 8
N_HEAD = 4


def draw_level_tokens(key, part):
    key = jax.random.fold_in(key, 7)
    key_base, key_cols, key_rows = jax.random.split(key, 3)
    col_scale = jnp.exp(jax.random.uniform(key_cols, (D,), jnp.float32, 0.0, math.log(10.0)))
    row_scale = jnp.exp(jax.random.uniform(key_rows, (PATCHES, LEV, 1), jnp.float32, 0.0, math.log(10.0)))
    base = jnp.clip(jax.random.normal(key_base, (PATCHES, LEV, D), jnp.float32), -4.0, 4.0)
    return (base * col_scale * row_scale).astype(jnp.bfloat16)


def draw_ocean_queries(key, part):
    key = jax.random.fold_in(key, 9)
    key_base = jax.random.fold_in(key, 0)
    base = jnp.clip(jax.random.normal(key_base, (SLOTS, LATENTS, D), jnp.float32), -4.0, 4.0)
    return base.astype(jnp.bfloat16)


def draw_send_slots(key, part):
    key = jax.random.fold_in(key, 11)
    full_owner = jax.random.randint(jax.random.fold_in(key, 1), (), 0, N_LAT)
    stripe = jnp.arange(N_LAT, dtype=jnp.int32)
    distance = jnp.abs(2 * stripe + 1 - N_LAT)
    highest = jnp.maximum(CAPS - (CAPS - CAPS // 4) * distance // N_LAT, 1)
    lowest = highest // 2
    raw_counts = jax.random.randint(jax.random.fold_in(key, 2), (N_LAT, N_LAT), 0, 1 << 20)
    counts = lowest[:, None] + raw_counts % (highest - lowest + 1)[:, None]
    owners = jnp.arange(N_LAT, dtype=jnp.int32)
    counts = jnp.where(owners[None, :] == full_owner, CAPS, counts)
    starts = jnp.cumsum(counts, axis=1) - counts
    stripe_keys = jax.random.split(jax.random.fold_in(key, 3), N_LAT)
    orders = jax.vmap(lambda one_key: jax.random.permutation(one_key, P_DEV))(stripe_keys).astype(jnp.int32)
    within = jnp.arange(CAPS, dtype=jnp.int32)
    position = starts[:, :, None] + within[None, None, :]
    live_slots = within[None, None, :] < counts[:, :, None]
    position = jnp.minimum(position, P_DEV - 1).reshape(N_LAT, N_LAT * CAPS)
    chosen = jnp.take_along_axis(orders, position, axis=1).reshape(N_LAT, N_LAT, CAPS)
    return jnp.where(live_slots, chosen, -1).astype(jnp.int32)


def steps_of(own_key, dims, cuts, smallest, top_value):
    def one(dim, shards_of):
        heights = jax.random.uniform(jax.random.fold_in(jax.random.fold_in(own_key, 6), dim), (shards_of,), jnp.float32, smallest / len(cuts), top_value / len(cuts))
        return jnp.repeat(jnp.exp(heights), dims[dim] // shards_of).reshape((-1,) + (1,) * (len(dims) - dim - 1))

    level = one(*cuts[0])
    for cut in cuts[1:]:
        level = level * one(*cut)
    return level


def normal_values(key, shape, deviation, reach, shards=(), kind=jnp.bfloat16):
    array = deviation * jax.random.normal(key, shape, jnp.float32)
    if shards:
        array = array * steps_of(key, shape, shards, -0.22, 0.18)
    return jnp.clip(array, -reach, reach).astype(kind)


def setup_inputs(seed: int = 0) -> dict:
    seeds = jax.random.split(jax.random.key(seed), 8)
    return {
        "level_tokens": draw_level_tokens(jax.random.fold_in(seeds[7], 71), 0),
        "ln_gain": jnp.clip(1.0 + 0.15 * jax.random.normal(seeds[1], (D,), jnp.float32), 0.25, 1.75),
        "key_weight": normal_values(seeds[2], (D, D), D ** -0.5, 0.1875, ((1, 4),)),
        "value_weight": normal_values(seeds[3], (D, D), D ** -0.5, 0.1875, ((1, 4),)),
        "out_weight": normal_values(seeds[4], (D, D), D ** -0.5, 0.1875, ((0, 4),)),
        "ocean_queries": draw_ocean_queries(jax.random.fold_in(seeds[7], 71), 0),
        "send_slots": draw_send_slots(jax.random.fold_in(seeds[7], 71), 0),
    }


def layer_norm(rows, gain):
    value_matrix = rows.astype(jnp.float32)
    center = lax.optimization_barrier(jnp.mean(value_matrix, axis=-1, keepdims=True))
    max_shifted_scores = value_matrix - center
    spread = lax.optimization_barrier(jnp.mean(max_shifted_scores * max_shifted_scores, axis=-1, keepdims=True))
    return (max_shifted_scores * lax.rsqrt(spread + 1e-05) * gain).astype(jnp.bfloat16)

def reference(level_tokens, ln_gain, key_weight, value_weight, out_weight, ocean_queries, send_slots):
    head_count = D // HEAD_DIM
    group_width = D // N_HEAD
    stripe_base = (jnp.arange(N_LAT, dtype=jnp.int32) * P_DEV)[:, None]

    def owner_block(owner):
        slot_rows = send_slots[:, owner, :]
        live_slots = (slot_rows >= 0).reshape(-1)
        picked = (stripe_base + jnp.maximum(slot_rows, 0)).reshape(-1).astype(jnp.int32)
        gathered = jnp.take(level_tokens, picked, axis=0)
        normalized_rows = layer_norm(gathered, ln_gain).reshape(P_DEV * LEV, D)
        key_rows = jnp.dot(normalized_rows, key_weight, preferred_element_type=jnp.float32).astype(jnp.bfloat16)
        key_rows = key_rows.reshape(P_DEV, LEV, head_count, HEAD_DIM)
        value_rows = jnp.dot(normalized_rows, value_weight, preferred_element_type=jnp.float32).astype(jnp.bfloat16)
        value_rows = value_rows.reshape(P_DEV, LEV, head_count, HEAD_DIM)
        queries = lax.dynamic_slice_in_dim(ocean_queries, (owner * P_DEV).astype(jnp.int32), P_DEV, 0)
        queries = queries.reshape(P_DEV, LATENTS, head_count, HEAD_DIM)
        scores = jnp.einsum('sqhe,slhe->shql', queries.astype(jnp.float32), key_rows.astype(jnp.float32)) / math.sqrt(HEAD_DIM)
        highest = lax.optimization_barrier(jnp.max(scores, axis=-1, keepdims=True))
        expo = jnp.exp(scores - highest)
        soft = (expo / lax.optimization_barrier(jnp.sum(expo, axis=-1, keepdims=True))).astype(jnp.bfloat16)
        mixed_heads = jnp.einsum('shql,slhe->sqhe', soft.astype(jnp.float32), value_rows.astype(jnp.float32)).astype(jnp.bfloat16)
        mixed_heads = mixed_heads.reshape(P_DEV * LATENTS, D)
        summed = jnp.zeros((P_DEV * LATENTS, D), jnp.float32)
        for group_index in range(N_HEAD):
            first_row = group_index * group_width
            partial_term = jnp.dot(mixed_heads[:, first_row:first_row + group_width], out_weight[first_row:first_row + group_width], preferred_element_type=jnp.float32).astype(jnp.bfloat16)
            partial_term = lax.optimization_barrier(partial_term)
            summed = summed + partial_term.astype(jnp.float32)
        result = summed.astype(jnp.bfloat16).reshape(P_DEV, LATENTS, D)
        return jnp.where(live_slots[:, None, None], result, jnp.zeros_like(result))
    blocks = lax.map(owner_block, jnp.arange(N_LAT, dtype=jnp.int32))
    return blocks.reshape(SLOTS, LATENTS, D)
```

```python
import functools
import math

import jax
import jax.numpy as jnp
from jax import lax
from jax.experimental import pallas as pl
from jax.experimental.pallas import tpu as pltpu
from jax.sharding import PartitionSpec as P

HEAD_DIM = 64
EPS = 1e-05
GROUP = 16
VMEM_LIMIT = 56 * 1024 * 1024


def params():
    return pltpu.CompilerParams(vmem_limit_bytes=VMEM_LIMIT)


def project_kernel(tokens_ref, gain_ref, key_weight_ref, value_weight_ref, key_ref, value_ref, normed_ref):
    levels, rows, width = tokens_ref.shape
    gain = gain_ref[...]

    def one_level(level, carry):
        tokens = tokens_ref[level].astype(jnp.float32)
        center = jnp.sum(tokens, axis=-1, keepdims=True) * (1.0 / width)
        shifted = tokens - center
        spread = jnp.sum(shifted * shifted, axis=-1, keepdims=True) * (1.0 / width)
        normed = shifted * lax.rsqrt(spread + EPS) * gain
        normed_ref[level] = normed.astype(jnp.bfloat16)
        return carry

    lax.fori_loop(0, levels, one_level, 0)
    normed = normed_ref[...].reshape(levels * rows, width)
    for weight_ref, out_ref in ((key_weight_ref, key_ref), (value_weight_ref, value_ref)):
        product = jnp.dot(normed, weight_ref[...], preferred_element_type=jnp.float32)
        out_ref[...] = product.astype(jnp.bfloat16).reshape(out_ref.shape)


def project(tokens, gain, key_weight, value_weight):
    levels, patches, width = tokens.shape
    local = key_weight.shape[1]
    rows = 64
    out = jax.ShapeDtypeStruct((levels, patches, local), jnp.bfloat16)
    out_spec = pl.BlockSpec((levels, rows, local), lambda i: (0, i, 0))
    whole = lambda i: (0, 0)
    return pl.pallas_call(
        project_kernel,
        grid=(patches // rows,),
        in_specs=[
            pl.BlockSpec((levels, rows, width), lambda i: (0, i, 0)),
            pl.BlockSpec((1, width), whole),
            pl.BlockSpec((width, local), whole),
            pl.BlockSpec((width, local), whole),
        ],
        out_specs=[out_spec, out_spec],
        out_shape=[out, out],
        scratch_shapes=[pltpu.VMEM((levels, rows, width), jnp.bfloat16)],
        compiler_params=params(),
        cost_estimate=pl.CostEstimate(
            flops=4 * levels * patches * width * local,
            bytes_accessed=2 * levels * patches * (width + 2 * local) + 4 * width * local,
            transcendentals=0,
        ),
        name="norm_project",
    )(tokens, gain.reshape(1, width), key_weight, value_weight)


def reorder_kernel(slots_ref, key_ref, value_ref, key_out_ref, value_out_ref):
    slots = slots_ref.shape[0]
    patches = key_ref.shape[1]
    columns = lax.broadcasted_iota(jnp.int32, (slots, patches), 1)
    pick = jnp.where(columns == slots_ref[...], 1.0, 0.0).astype(jnp.bfloat16)
    for in_ref, out_ref in ((key_ref, key_out_ref), (value_ref, value_out_ref)):
        out_ref[0] = jnp.dot(pick, in_ref[0], preferred_element_type=jnp.float32).astype(jnp.bfloat16)


def reorder(slots, keys, values):
    levels, patches, local = keys.shape
    count = slots.shape[0]
    out = jax.ShapeDtypeStruct((levels, count, local), jnp.bfloat16)
    in_spec = pl.BlockSpec((1, patches, local), lambda i: (i, 0, 0))
    out_spec = pl.BlockSpec((1, count, local), lambda i: (i, 0, 0))
    return pl.pallas_call(
        reorder_kernel,
        grid=(levels,),
        in_specs=[pl.BlockSpec((count, 1), lambda i: (0, 0)), in_spec, in_spec],
        out_specs=[out_spec, out_spec],
        out_shape=[out, out],
        compiler_params=params(),
        cost_estimate=pl.CostEstimate(
            flops=4 * levels * patches * count * local,
            bytes_accessed=4 * levels * (patches + count) * local,
            transcendentals=0,
        ),
        name="slot_order",
    )(slots.reshape(count, 1), keys, values)


def attend_kernel(query_ref, key_ref, value_ref, mixed_ref):
    levels, slots, local = key_ref.shape
    latents = query_ref.shape[1]
    heads = local // HEAD_DIM
    rows = GROUP * latents
    columns = levels * GROUP
    lane_head = lax.broadcasted_iota(jnp.int32, (rows, local), 1) // HEAD_DIM
    row_slot = (lax.broadcasted_iota(jnp.int32, (heads * rows, columns), 0) // latents) & (GROUP - 1)
    column_slot = lax.broadcasted_iota(jnp.int32, (heads * rows, columns), 1) & (GROUP - 1)
    same = row_slot - column_slot == 0
    for start in range(0, slots, GROUP):
        part = pl.ds(start, GROUP)
        queries = query_ref[part].reshape(rows, local)
        queries = queries.astype(jnp.float32)
        queries = jnp.concatenate(
            [jnp.where(lane_head == head, queries, 0.0).astype(jnp.bfloat16) for head in range(heads)], axis=0
        )
        keys = key_ref[:, part, :].reshape(columns, local)
        scores = lax.dot_general(
            queries, keys, (((1,), (1,)), ((), ())), preferred_element_type=jnp.float32
        ) * (1.0 / math.sqrt(HEAD_DIM))
        scores = jnp.where(same, scores, -jnp.inf)
        highest = jnp.max(scores, axis=-1, keepdims=True)
        expo = jnp.exp(scores - highest)
        soft = (expo / jnp.sum(expo, axis=-1, keepdims=True)).astype(jnp.bfloat16)
        values = value_ref[:, part, :].reshape(columns, local)
        wide = jnp.dot(soft, values, preferred_element_type=jnp.float32)
        mixed = wide[:rows]
        for head in range(1, heads):
            mixed = jnp.where(lane_head == head, wide[head * rows : (head + 1) * rows], mixed)
        mixed_ref[part] = mixed.astype(jnp.bfloat16).reshape(GROUP, latents, local)


def attend(queries, keys, values):
    slots, latents, local = queries.shape
    levels = keys.shape[0]
    block = 64
    query_spec = pl.BlockSpec((block, latents, local), lambda i: (i, 0, 0))
    key_spec = pl.BlockSpec((levels, block, local), lambda i: (0, i, 0))
    return pl.pallas_call(
        attend_kernel,
        grid=(slots // block,),
        in_specs=[query_spec, key_spec, key_spec],
        out_specs=query_spec,
        out_shape=jax.ShapeDtypeStruct((slots, latents, local), jnp.bfloat16),
        compiler_params=params(),
        cost_estimate=pl.CostEstimate(
            flops=4 * slots * latents * levels * GROUP * local * 4,
            bytes_accessed=4 * slots * (latents + levels) * local,
            transcendentals=0,
        ),
        name="attend_slots",
    )(queries, keys, values)


def combine_kernel(place_ref, first_ref, second_ref, third_ref, fourth_ref, weight_ref, out_ref):
    slots, latents, local = out_ref.shape
    total = None
    for step, mixed_ref in enumerate((first_ref, second_ref, third_ref, fourth_ref)):
        mixed = mixed_ref[...].reshape(slots * latents, local)
        weight = weight_ref[jnp.bitwise_xor(place_ref[0], step)]
        term = jnp.dot(mixed, weight, preferred_element_type=jnp.float32).astype(jnp.bfloat16).astype(jnp.float32)
        total = term if total is None else total + term
    out_ref[...] = total.astype(jnp.bfloat16).reshape(out_ref.shape)


def combine(place, groups, weight):
    slots, latents, local = groups[0].shape
    block = 64
    spec = pl.BlockSpec((block, latents, local), lambda i, place: (i, 0, 0))
    return pl.pallas_call(
        combine_kernel,
        grid_spec=pltpu.PrefetchScalarGridSpec(
            num_scalar_prefetch=1,
            grid=(slots // block,),
            in_specs=[spec] * 4 + [pl.BlockSpec(weight.shape, lambda i, place: (0, 0, 0))],
            out_specs=spec,
        ),
        out_shape=jax.ShapeDtypeStruct((slots, latents, local), jnp.bfloat16),
        compiler_params=params(),
        cost_estimate=pl.CostEstimate(
            flops=8 * slots * latents * local * local,
            bytes_accessed=10 * slots * latents * local,
            transcendentals=0,
        ),
        name="combine_groups",
    )(place, *groups, weight)


def swap(array, axis_name, distance):
    size = lax.axis_size(axis_name)
    return lax.ppermute(array, axis_name, [(i, i ^ distance) for i in range(size)])


def shards(level_tokens, ln_gain, key_weight, value_weight, out_weight, ocean_queries, send_slots):
    stripes = lax.axis_size("lat")
    caps = send_slots.shape[2]
    slots, latents, local = ocean_queries.shape
    by_stripe = (stripes, caps, latents, local)
    queries = lax.all_to_all(ocean_queries.reshape(by_stripe), "lat", split_axis=0, concat_axis=0, tiled=True)
    weight = lax.all_to_all(out_weight, "head", split_axis=1, concat_axis=0, tiled=True)
    weight = weight.reshape(-1, local, local)
    keys, values = project(jnp.transpose(level_tokens, (1, 0, 2)), ln_gain, key_weight, value_weight)
    keys, values = reorder(send_slots.reshape(-1), keys, values)
    mixed = attend(queries.reshape(slots, latents, local), keys, values)
    mixed = lax.all_to_all(mixed.reshape(by_stripe), "lat", split_axis=0, concat_axis=0, tiled=True)
    mixed = mixed.reshape(slots, latents, local)
    second = swap(mixed, "head", 2)
    first = swap(mixed, "head", 1)
    third = swap(second, "head", 1)
    place = lax.axis_index("head").reshape(1)
    return combine(place, (mixed, first, second, third), weight)


def solution(mesh):
    return jax.shard_map(
        shards,
        mesh=mesh,
        in_specs=(
            P("lat", None, None),
            P(),
            P(None, "head"),
            P(None, "head"),
            P("head", None),
            P("lat", None, "head"),
            P("lat", None, None),
        ),
        out_specs=P("lat", None, "head"),
        check_vma=False,
    )
```

```python
import functools
import math

import jax
import jax.numpy as jnp
from jax import lax
from jax.experimental import pallas as pl
from jax.experimental.pallas import tpu as pltpu
from jax.sharding import PartitionSpec as P

HEAD_DIM = 64
EPS = 1e-05
GROUP = 16
ROWS = 32
VMEM_LIMIT = 56 * 1024 * 1024


def params():
    return pltpu.CompilerParams(vmem_limit_bytes=VMEM_LIMIT)


def normalize_rows(tokens, gain):
    width = tokens.shape[-1]
    tokens = tokens.astype(jnp.float32)
    center = jnp.sum(tokens, axis=-1, keepdims=True) * (1.0 / width)
    shifted = tokens - center
    spread = jnp.sum(shifted * shifted, axis=-1, keepdims=True) * (1.0 / width)
    return (shifted * lax.rsqrt(spread + EPS) * gain).astype(jnp.bfloat16)


def project_kernel(
    slots_ref, tokens_ref, gain_ref, key_weight_ref, value_weight_ref, key_ref, value_ref, even_ref, odd_ref, pick_ref
):
    step = pl.program_id(0)
    patches = tokens_ref.shape[1]

    @pl.when(step == 0)
    def _():
        columns = lax.broadcasted_iota(jnp.int32, pick_ref.shape, 1)
        pick_ref[...] = jnp.where(columns == slots_ref[...], 1.0, 0.0).astype(jnp.bfloat16)

    def stage(write_ref, read_ref):
        gain = gain_ref[...]
        for weight_ref, out_ref in ((key_weight_ref, key_ref), (value_weight_ref, value_ref)):
            product = jnp.dot(read_ref[...], weight_ref[...], preferred_element_type=jnp.float32)
            product = product.astype(jnp.bfloat16)
            out_ref[0] = jnp.dot(pick_ref[...], product, preferred_element_type=jnp.float32).astype(jnp.bfloat16)
        for start in range(0, patches, ROWS):
            part = pl.ds(start, ROWS)
            write_ref[part, :] = normalize_rows(tokens_ref[0, part, :], gain)

    @pl.when(step % 2 == 0)
    def _():
        stage(even_ref, odd_ref)

    @pl.when(step % 2 == 1)
    def _():
        stage(odd_ref, even_ref)


def project(slots, tokens, gain, key_weight, value_weight):
    levels, patches, width = tokens.shape
    local = key_weight.shape[1]
    count = slots.shape[0]
    out = jax.ShapeDtypeStruct((levels, count, local), jnp.bfloat16)
    out_spec = pl.BlockSpec((1, count, local), lambda i: (jnp.maximum(i - 1, 0), 0, 0))
    whole = lambda i: (0, 0)
    return pl.pallas_call(
        project_kernel,
        grid=(levels + 1,),
        in_specs=[
            pl.BlockSpec((count, 1), whole),
            pl.BlockSpec((1, patches, width), lambda i: (jnp.minimum(i, levels - 1), 0, 0)),
            pl.BlockSpec((1, width), whole),
            pl.BlockSpec((width, local), whole),
            pl.BlockSpec((width, local), whole),
        ],
        out_specs=[out_spec, out_spec],
        out_shape=[out, out],
        scratch_shapes=[
            pltpu.VMEM((patches, width), jnp.bfloat16),
            pltpu.VMEM((patches, width), jnp.bfloat16),
            pltpu.VMEM((count, patches), jnp.bfloat16),
        ],
        compiler_params=params(),
        cost_estimate=pl.CostEstimate(
            flops=4 * levels * patches * (width + count) * local,
            bytes_accessed=2 * levels * patches * (width + 2 * local) + 4 * width * local,
            transcendentals=0,
        ),
        name="norm_project",
    )(slots.reshape(count, 1), tokens, gain.reshape(1, width), key_weight, value_weight)


def attend_kernel(place_ref, query_ref, key_ref, value_ref, mixed_ref):
    levels, slots, local = key_ref.shape
    latents = query_ref.shape[1]
    heads = local // HEAD_DIM
    rows = GROUP * latents
    columns = levels * GROUP
    lane_head = lax.broadcasted_iota(jnp.int32, (rows, local), 1) // HEAD_DIM
    row_slot = (lax.broadcasted_iota(jnp.int32, (heads * rows, columns), 0) // latents) & (GROUP - 1)
    column_slot = lax.broadcasted_iota(jnp.int32, (heads * rows, columns), 1) & (GROUP - 1)
    same = row_slot - column_slot == 0
    for start in range(0, slots, GROUP):
        part = pl.ds(start, GROUP)
        queries = query_ref[part].reshape(rows, local)
        queries = queries.astype(jnp.float32)
        queries = jnp.concatenate(
            [jnp.where(lane_head == head, queries, 0.0).astype(jnp.bfloat16) for head in range(heads)], axis=0
        )
        keys = key_ref[:, part, :].reshape(columns, local)
        scores = lax.dot_general(
            queries, keys, (((1,), (1,)), ((), ())), preferred_element_type=jnp.float32
        )
        scores = jnp.where(same, scores, -jnp.inf)
        highest = jnp.max(scores, axis=-1, keepdims=True)
        expo = jnp.exp2((scores - highest) * (math.log2(math.e) / math.sqrt(HEAD_DIM)))
        soft = (expo * (1.0 / jnp.sum(expo, axis=-1, keepdims=True))).astype(jnp.bfloat16)
        values = value_ref[:, part, :].reshape(columns, local)
        wide = jnp.dot(soft, values, preferred_element_type=jnp.float32)
        mixed = wide[:rows]
        for head in range(1, heads):
            mixed = jnp.where(lane_head == head, wide[head * rows : (head + 1) * rows], mixed)
        mixed_ref[pl.ds(start * latents, rows), :] = mixed.astype(jnp.bfloat16)


def attend(place, queries, keys, values, distance, block):
    slots, latents, local = queries.shape
    levels = keys.shape[0]
    steps = slots // block if distance is None else 1

    def chunk(i, place):
        return i if distance is None else jnp.bitwise_xor(place[0], distance)

    key_spec = pl.BlockSpec((levels, block, local), lambda i, place: (0, chunk(i, place), 0))
    return pl.pallas_call(
        attend_kernel,
        grid_spec=pltpu.PrefetchScalarGridSpec(
            num_scalar_prefetch=1,
            grid=(steps,),
            in_specs=[
                pl.BlockSpec((block, latents, local), lambda i, place: (chunk(i, place), 0, 0)),
                key_spec,
                key_spec,
            ],
            out_specs=pl.BlockSpec((block * latents, local), lambda i, place: (i, 0)),
        ),
        out_shape=jax.ShapeDtypeStruct((steps * block * latents, local), jnp.bfloat16),
        compiler_params=params(),
        cost_estimate=pl.CostEstimate(
            flops=16 * steps * block * latents * levels * GROUP * local,
            bytes_accessed=4 * steps * block * (latents + levels) * local,
            transcendentals=0,
        ),
        name="attend_slots",
    )(place, queries, keys, values)


def combine_kernel(place_ref, first_ref, second_ref, third_ref, fourth_ref, weight_ref, *refs):
    out_ref = refs[-1]
    total = None
    for step, mixed_ref in enumerate((first_ref, second_ref, third_ref, fourth_ref)):
        weight = weight_ref[jnp.bitwise_xor(place_ref[1], step)]
        term = jnp.dot(mixed_ref[...], weight, preferred_element_type=jnp.float32)
        term = term.astype(jnp.bfloat16).astype(jnp.float32)
        total = term if total is None else total + term
    out_ref[...] = total.astype(jnp.bfloat16).reshape(out_ref.shape)


def combine(place, groups, weight, out, shape, distance, block):
    slots, latents, local = shape
    steps = slots // block if distance is None else 1

    def chunk(i, place):
        return i if distance is None else jnp.bitwise_xor(place[0], distance)

    spec = pl.BlockSpec((block * latents, local), lambda i, place: (i, 0))
    in_specs = [spec] * 4 + [pl.BlockSpec(weight.shape, lambda i, place: (0, 0, 0))]
    operands = [place, *groups, weight]
    aliases = {}
    if out is not None:
        aliases = {len(operands): 0}
        in_specs.append(pl.BlockSpec(memory_space=pl.ANY))
        operands.append(out)
    return pl.pallas_call(
        combine_kernel,
        grid_spec=pltpu.PrefetchScalarGridSpec(
            num_scalar_prefetch=1,
            grid=(steps,),
            in_specs=in_specs,
            out_specs=pl.BlockSpec((block, latents, local), lambda i, place: (chunk(i, place), 0, 0)),
        ),
        out_shape=jax.ShapeDtypeStruct((slots, latents, local), jnp.bfloat16),
        input_output_aliases=aliases,
        compiler_params=params(),
        cost_estimate=pl.CostEstimate(
            flops=8 * steps * block * latents * local * local,
            bytes_accessed=10 * steps * block * latents * local,
            transcendentals=0,
        ),
        name="combine_groups",
    )(*operands)


def swap(array, axis_name, distance):
    size = lax.axis_size(axis_name)
    return lax.ppermute(array, axis_name, [(i, i ^ distance) for i in range(size)])


def spread_heads(mixed):
    second = swap(mixed, "head", 2)
    return mixed, swap(mixed, "head", 1), second, swap(second, "head", 1)


def shards(level_tokens, ln_gain, key_weight, value_weight, out_weight, ocean_queries, send_slots):
    stripes = lax.axis_size("lat")
    caps = send_slots.shape[2]
    shape = ocean_queries.shape
    slots, latents, local = shape
    by_stripe = (stripes, caps, latents, local)
    place = jnp.stack([lax.axis_index("lat"), lax.axis_index("head")]).astype(jnp.int32)
    queries = lax.all_to_all(ocean_queries.reshape(by_stripe), "lat", split_axis=0, concat_axis=0, tiled=True)
    queries = queries.reshape(shape)
    weight = lax.all_to_all(out_weight, "head", split_axis=1, concat_axis=0, tiled=True)
    weight = weight.reshape(-1, local, local)
    tokens = jnp.transpose(level_tokens, (1, 0, 2))
    keys, values = project(send_slots.reshape(-1), tokens, ln_gain, key_weight, value_weight)
    if caps % GROUP:
        mixed = attend(place, queries, keys, values, None, 64)
        mixed = lax.all_to_all(mixed.reshape(stripes, -1, local), "lat", split_axis=0, concat_axis=0, tiled=True)
        return combine(place, spread_heads(mixed.reshape(-1, local)), weight, None, shape, None, 64)
    arrived = []
    for distance in sorted(range(stripes), reverse=True):
        mixed = attend(place, queries, keys, values, distance, caps)
        arrived.append((distance, swap(mixed, "lat", distance) if distance else mixed))
    out = None
    for distance, mixed in arrived:
        out = combine(place, spread_heads(mixed), weight, out, shape, distance, caps)
    return out


def solution(mesh):
    return jax.shard_map(
        shards,
        mesh=mesh,
        in_specs=(
            P("lat", None, None),
            P(),
            P(None, "head"),
            P(None, "head"),
            P("head", None),
            P("lat", None, "head"),
            P("lat", None, None),
        ),
        out_specs=P("lat", None, "head"),
        check_vma=False,
    )
```

```python
import functools
import math

import jax
import jax.numpy as jnp
from jax import lax
from jax.experimental import pallas as pl
from jax.experimental.pallas import tpu as pltpu
from jax.sharding import PartitionSpec as P

HEAD_DIM = 64
EPS = 1e-05
GROUP = 16
ROWS = 32
BATCH = 256
LANES = 128
VMEM_LIMIT = 56 * 1024 * 1024


def params():
    return pltpu.CompilerParams(vmem_limit_bytes=VMEM_LIMIT)


def lane_parts(tokens_ref, row, rows):
    width = tokens_ref.shape[-1]
    for lane in range(0, width, LANES):
        yield lane, tokens_ref[0, pl.ds(row, rows), pl.ds(lane, LANES)].astype(jnp.float32)


def normalize_rows(tokens_ref, start, gain, write_ref):
    width = tokens_ref.shape[-1]
    pieces = range(start, start + BATCH, ROWS)
    sums = []
    for row in pieces:
        total = None
        for _, part in lane_parts(tokens_ref, row, ROWS):
            total = part if total is None else total + part
        sums.append(total)
    centers = [jnp.sum(total, axis=-1, keepdims=True) * (1.0 / width) for total in sums]
    squares = []
    for row, center in zip(pieces, centers):
        total = None
        for _, part in lane_parts(tokens_ref, row, ROWS):
            part = part - center
            total = part * part if total is None else total + part * part
        squares.append(total)
    scales = [lax.rsqrt(jnp.sum(total, axis=-1, keepdims=True) * (1.0 / width) + EPS) for total in squares]
    for row, center, scale in zip(pieces, centers, scales):
        for lane, part in lane_parts(tokens_ref, row, ROWS):
            normed = (part - center) * scale * gain[:, lane : lane + LANES]
            write_ref[pl.ds(row, ROWS), pl.ds(lane, LANES)] = normed.astype(jnp.bfloat16)


def project_kernel(
    slots_ref, tokens_ref, gain_ref, key_weight_ref, value_weight_ref, key_ref, value_ref, even_ref, odd_ref, pick_ref
):
    step = pl.program_id(0)
    patches = tokens_ref.shape[1]

    @pl.when(step == 0)
    def _():
        columns = lax.broadcasted_iota(jnp.int32, pick_ref.shape, 1)
        pick_ref[...] = jnp.where(columns == slots_ref[...], 1.0, 0.0).astype(jnp.bfloat16)

    def stage(write_ref, read_ref):
        gain = gain_ref[...]
        for weight_ref, out_ref in ((key_weight_ref, key_ref), (value_weight_ref, value_ref)):
            product = jnp.dot(read_ref[...], weight_ref[...], preferred_element_type=jnp.float32)
            product = product.astype(jnp.bfloat16)
            out_ref[0] = jnp.dot(pick_ref[...], product, preferred_element_type=jnp.float32).astype(jnp.bfloat16)
        for start in range(0, patches, BATCH):
            normalize_rows(tokens_ref, start, gain, write_ref)

    @pl.when(step % 2 == 0)
    def _():
        stage(even_ref, odd_ref)

    @pl.when(step % 2 == 1)
    def _():
        stage(odd_ref, even_ref)


def project(slots, tokens, gain, key_weight, value_weight):
    levels, patches, width = tokens.shape
    local = key_weight.shape[1]
    count = slots.shape[0]
    out = jax.ShapeDtypeStruct((levels, count, local), jnp.bfloat16)
    out_spec = pl.BlockSpec((1, count, local), lambda i: (jnp.maximum(i - 1, 0), 0, 0))
    whole = lambda i: (0, 0)
    return pl.pallas_call(
        project_kernel,
        grid=(levels + 1,),
        in_specs=[
            pl.BlockSpec((count, 1), whole),
            pl.BlockSpec((1, patches, width), lambda i: (jnp.minimum(i, levels - 1), 0, 0)),
            pl.BlockSpec((1, width), whole),
            pl.BlockSpec((width, local), whole),
            pl.BlockSpec((width, local), whole),
        ],
        out_specs=[out_spec, out_spec],
        out_shape=[out, out],
        scratch_shapes=[
            pltpu.VMEM((patches, width), jnp.bfloat16),
            pltpu.VMEM((patches, width), jnp.bfloat16),
            pltpu.VMEM((count, patches), jnp.bfloat16),
        ],
        compiler_params=params(),
        cost_estimate=pl.CostEstimate(
            flops=4 * levels * patches * (width + count) * local,
            bytes_accessed=2 * levels * patches * (width + 2 * local) + 4 * width * local,
            transcendentals=0,
        ),
        name="norm_project",
    )(slots.reshape(count, 1), tokens, gain.reshape(1, width), key_weight, value_weight)


def attend_kernel(place_ref, query_ref, key_ref, value_ref, *refs):
    out_refs, mixed_ref = refs[:-1], refs[-1]
    levels, slots, local = key_ref.shape
    latents = query_ref.shape[1]
    heads = local // HEAD_DIM
    rows = GROUP * latents
    columns = levels * GROUP
    lane_head = lax.broadcasted_iota(jnp.int32, (rows, local), 1) // HEAD_DIM
    row_slot = (lax.broadcasted_iota(jnp.int32, (heads * rows, columns), 0) // latents) & (GROUP - 1)
    column_slot = lax.broadcasted_iota(jnp.int32, (heads * rows, columns), 1) & (GROUP - 1)
    same = row_slot - column_slot == 0
    ones = jnp.ones((columns, LANES), jnp.bfloat16)

    def by_head(wide):
        mixed = wide[:rows]
        for head in range(1, heads):
            mixed = jnp.where(lane_head == head, wide[head * rows : (head + 1) * rows], mixed)
        return mixed

    starts = range(0, slots, GROUP)
    scores = []
    for start in starts:
        queries = query_ref[pl.ds(start, GROUP)].reshape(rows, local).astype(jnp.float32)
        queries = jnp.concatenate(
            [jnp.where(lane_head == head, queries, 0.0).astype(jnp.bfloat16) for head in range(heads)], axis=0
        )
        keys = key_ref[:, pl.ds(start, GROUP), :].reshape(columns, local)
        product = lax.dot_general(queries, keys, (((1,), (1,)), ((), ())), preferred_element_type=jnp.float32)
        scores.append(jnp.where(same, product, -jnp.inf))
    highest = [jnp.max(product, axis=-1, keepdims=True) for product in scores]
    scale = math.log2(math.e) / math.sqrt(HEAD_DIM)
    expo = [jnp.exp2((product - top) * scale).astype(jnp.bfloat16) for product, top in zip(scores, highest)]
    for start, weights in zip(starts, expo):
        values = value_ref[:, pl.ds(start, GROUP), :].reshape(columns, local)
        wide = jnp.dot(weights, values, preferred_element_type=jnp.float32)
        sums = jnp.dot(weights, ones, preferred_element_type=jnp.float32)
        sums = by_head(jnp.concatenate([sums] * (local // LANES), axis=1))
        mixed = by_head(wide) / sums
        mixed_ref[pl.ds(start * latents, rows), :] = mixed.astype(jnp.bfloat16)
    for step, out_ref in enumerate(out_refs):

        @pl.when(pl.program_id(0) == step)
        def _(out_ref=out_ref):
            out_ref[...] = mixed_ref[...]


def attend(place, queries, keys, values, first, block, steps):
    slots, latents, local = queries.shape
    levels = keys.shape[0]

    def chunk(i, place):
        return jnp.bitwise_xor(place[0], first - i)

    key_spec = pl.BlockSpec((levels, block, local), lambda i, place: (0, chunk(i, place), 0))
    return pl.pallas_call(
        attend_kernel,
        grid_spec=pltpu.PrefetchScalarGridSpec(
            num_scalar_prefetch=1,
            grid=(steps,),
            in_specs=[
                pl.BlockSpec((block, latents, local), lambda i, place: (chunk(i, place), 0, 0)),
                key_spec,
                key_spec,
            ],
            out_specs=[pl.BlockSpec((block * latents, local), lambda i, place: (0, 0))] * steps,
            scratch_shapes=[pltpu.VMEM((block * latents, local), jnp.bfloat16)],
        ),
        out_shape=[jax.ShapeDtypeStruct((block * latents, local), jnp.bfloat16)] * steps,
        compiler_params=params(),
        cost_estimate=pl.CostEstimate(
            flops=16 * steps * block * latents * levels * GROUP * local,
            bytes_accessed=4 * steps * block * (latents + levels) * local,
            transcendentals=0,
        ),
        name="attend_slots",
    )(place, queries, keys, values)


def combine_kernel(place_ref, *refs):
    out_ref = refs[-1]
    total = None
    for mixed_ref, weight_ref in zip(refs[:4], refs[4:8]):
        term = jnp.dot(mixed_ref[...], weight_ref[...], preferred_element_type=jnp.float32)
        term = term.astype(jnp.bfloat16).astype(jnp.float32)
        total = term if total is None else total + term
    out_ref[...] = total.astype(jnp.bfloat16).reshape(out_ref.shape)


def combine(place, groups, weights, out, shape, first, block, steps):
    slots, latents, local = shape
    spec = pl.BlockSpec((block * latents, local), lambda i, place: (i, 0))
    in_specs = [spec] * 4 + [pl.BlockSpec(weights[0].shape, lambda i, place: (0, 0))] * 4
    operands = [place, *groups, *weights]
    aliases = {}
    if out is not None:
        aliases = {len(operands): 0}
        in_specs.append(pl.BlockSpec(memory_space=pl.ANY))
        operands.append(out)
    return pl.pallas_call(
        combine_kernel,
        grid_spec=pltpu.PrefetchScalarGridSpec(
            num_scalar_prefetch=1,
            grid=(steps,),
            in_specs=in_specs,
            out_specs=pl.BlockSpec(
                (block, latents, local), lambda i, place: (jnp.bitwise_xor(place[0], first - i), 0, 0)
            ),
        ),
        out_shape=jax.ShapeDtypeStruct((slots, latents, local), jnp.bfloat16),
        input_output_aliases=aliases,
        compiler_params=params(),
        cost_estimate=pl.CostEstimate(
            flops=8 * steps * block * latents * local * local,
            bytes_accessed=10 * steps * block * latents * local,
            transcendentals=0,
        ),
        name="combine_groups",
    )(*operands)


def swap(array, axis_name, distance):
    size = lax.axis_size(axis_name)
    return lax.ppermute(array, axis_name, [(i, i ^ distance) for i in range(size)])


def spread_heads(mixed):
    second = swap(mixed, "head", 2)
    return mixed, swap(mixed, "head", 1), second, swap(second, "head", 1)


def spread_weight(out_weight, head):
    local = out_weight.shape[0]
    parts = []
    for distance in range(lax.axis_size("head")):
        start = jnp.bitwise_xor(head, distance) * local
        part = lax.dynamic_slice_in_dim(out_weight, start, local, 1)
        parts.append(swap(part, "head", distance) if distance else part)
    return parts


def shards(level_tokens, ln_gain, key_weight, value_weight, out_weight, ocean_queries, send_slots):
    stripes = lax.axis_size("lat")
    caps = send_slots.shape[2]
    shape = ocean_queries.shape
    slots, latents, local = shape
    by_stripe = (stripes, caps, latents, local)
    place = jnp.stack([lax.axis_index("lat"), lax.axis_index("head")]).astype(jnp.int32)
    queries = lax.all_to_all(ocean_queries.reshape(by_stripe), "lat", split_axis=0, concat_axis=0, tiled=True)
    queries = queries.reshape(shape)
    weights = spread_weight(out_weight, place[1])
    tokens = jnp.transpose(level_tokens, (1, 0, 2))
    keys, values = project(send_slots.reshape(-1), tokens, ln_gain, key_weight, value_weight)
    if caps % GROUP:
        still = jnp.zeros_like(place)
        steps = slots // 64
        mixed = jnp.concatenate(attend(still + (steps - 1), queries, keys, values, steps - 1, 64, steps))
        mixed = lax.all_to_all(mixed.reshape(stripes, -1, local), "lat", split_axis=0, concat_axis=0, tiled=True)
        groups = spread_heads(mixed.reshape(-1, local))
        return combine(still + (steps - 1), groups, weights, None, shape, steps - 1, 64, steps)
    half = stripes // 2
    arrived = []
    for first in (stripes - 1, half - 1):
        chunks = attend(place, queries, keys, values, first, caps, half)
        chunks = [swap(chunk, "lat", first - i) if first - i else chunk for i, chunk in enumerate(chunks)]
        arrived.append((first, chunks))
    out = None
    for first, chunks in reversed(arrived):
        groups = spread_heads(jnp.concatenate(chunks))
        out = combine(place, groups, weights, out, shape, first, caps, half)
    return out


def solution(mesh):
    return jax.shard_map(
        shards,
        mesh=mesh,
        in_specs=(
            P("lat", None, None),
            P(),
            P(None, "head"),
            P(None, "head"),
            P("head", None),
            P("lat", None, "head"),
            P("lat", None, None),
        ),
        out_specs=P("lat", None, "head"),
        check_vma=False,
    )
```

```python
import functools
import math

import jax
import jax.numpy as jnp
from jax import lax
from jax.experimental import pallas as pl
from jax.experimental.pallas import tpu as pltpu
from jax.sharding import PartitionSpec as P

HEAD_DIM = 64
EPS = 1e-05
GROUP = 16
ROWS = 32
LANES = 128
MIB = 1024 * 1024


def params(mib):
    return pltpu.CompilerParams(vmem_limit_bytes=mib * MIB)


def normalize_rows(tokens, gain):
    width = tokens.shape[-1]
    tokens = tokens.astype(jnp.float32)
    center = jnp.sum(tokens, axis=-1, keepdims=True) * (1.0 / width)
    shifted = tokens - center
    spread = jnp.sum(shifted * shifted, axis=-1, keepdims=True) * (1.0 / width)
    return (shifted * lax.rsqrt(spread + EPS) * gain).astype(jnp.bfloat16)


def build_pick(slots_ref, pick_ref):
    stripes, caps = slots_ref.shape
    diagonal = lax.broadcasted_iota(jnp.int32, (caps, caps), 0) == lax.broadcasted_iota(jnp.int32, (caps, caps), 1)
    patch = lax.broadcasted_iota(jnp.int32, (caps, pick_ref.shape[1]), 1)
    for owner in range(stripes):
        row = jnp.broadcast_to(slots_ref[owner : owner + 1, :], (caps, caps))
        column = jnp.sum(jnp.where(diagonal, row, 0), axis=-1, keepdims=True)
        pick = jnp.where(patch == column, 1.0, 0.0)
        pick_ref[owner * caps : (owner + 1) * caps, :] = pick.astype(jnp.bfloat16)


def project_kernel(
    slots_ref,
    tokens_ref,
    gain_ref,
    key_weight_ref,
    value_weight_ref,
    key_ref,
    value_ref,
    even_ref,
    odd_ref,
    pick_ref,
    weight_ref,
):
    step = pl.program_id(0)
    patches = tokens_ref.shape[1]
    local = key_weight_ref.shape[1]

    @pl.when(step == 0)
    def _():
        build_pick(slots_ref, pick_ref)
        weight_ref[:, :local] = key_weight_ref[...]
        weight_ref[:, local:] = value_weight_ref[...]

    def stage(write_ref, read_ref):
        gain = gain_ref[...]
        product = jnp.dot(read_ref[...], weight_ref[...], preferred_element_type=jnp.float32).astype(jnp.bfloat16)
        product = jnp.dot(pick_ref[...], product, preferred_element_type=jnp.float32).astype(jnp.bfloat16)
        key_ref[0] = product[:, :local]
        value_ref[0] = product[:, local:]
        for start in range(0, patches, ROWS):
            part = pl.ds(start, ROWS)
            write_ref[part, :] = normalize_rows(tokens_ref[0, part, :], gain)

    @pl.when(step % 2 == 0)
    def _():
        stage(even_ref, odd_ref)

    @pl.when(step % 2 == 1)
    def _():
        stage(odd_ref, even_ref)


def project(slots, tokens, gain, key_weight, value_weight):
    levels, patches, width = tokens.shape
    local = key_weight.shape[1]
    count = slots.size
    out = jax.ShapeDtypeStruct((levels, count, local), jnp.bfloat16)
    out_spec = pl.BlockSpec((1, count, local), lambda i: (jnp.maximum(i - 1, 0), 0, 0))
    whole = lambda i: (0, 0)
    return pl.pallas_call(
        project_kernel,
        grid=(levels + 1,),
        in_specs=[
            pl.BlockSpec(slots.shape, whole),
            pl.BlockSpec((1, patches, width), lambda i: (jnp.minimum(i, levels - 1), 0, 0)),
            pl.BlockSpec((1, width), whole),
            pl.BlockSpec((width, local), whole),
            pl.BlockSpec((width, local), whole),
        ],
        out_specs=[out_spec, out_spec],
        out_shape=[out, out],
        scratch_shapes=[
            pltpu.VMEM((patches, width), jnp.bfloat16),
            pltpu.VMEM((patches, width), jnp.bfloat16),
            pltpu.VMEM((count, patches), jnp.bfloat16),
            pltpu.VMEM((width, 2 * local), jnp.bfloat16),
        ],
        compiler_params=params(24),
        cost_estimate=pl.CostEstimate(
            flops=4 * levels * patches * (width + count) * local,
            bytes_accessed=2 * levels * patches * (width + 2 * local) + 4 * width * local,
            transcendentals=0,
        ),
        name="norm_project",
    )(slots, tokens, gain.reshape(1, width), key_weight, value_weight)


def attend_kernel(place_ref, query_ref, key_ref, value_ref, *refs):
    out_refs, mixed_ref = refs[:-1], refs[-1]
    levels, slots, local = key_ref.shape
    latents = query_ref.shape[1]
    heads = local // HEAD_DIM
    rows = GROUP * latents
    columns = levels * GROUP
    lane_head = lax.broadcasted_iota(jnp.int32, (rows, local), 1) // HEAD_DIM
    row_slot = (lax.broadcasted_iota(jnp.int32, (heads * rows, columns), 0) // latents) & (GROUP - 1)
    column_slot = lax.broadcasted_iota(jnp.int32, (heads * rows, columns), 1) & (GROUP - 1)
    same = row_slot - column_slot == 0
    ones = jnp.ones((columns, LANES), jnp.bfloat16)

    def by_head(wide):
        mixed = wide[:rows]
        for head in range(1, heads):
            mixed = jnp.where(lane_head == head, wide[head * rows : (head + 1) * rows], mixed)
        return mixed

    starts = range(0, slots, GROUP)
    scores = []
    for start in starts:
        queries = query_ref[pl.ds(start, GROUP)].reshape(rows, local).astype(jnp.float32)
        queries = jnp.concatenate(
            [jnp.where(lane_head == head, queries, 0.0).astype(jnp.bfloat16) for head in range(heads)], axis=0
        )
        keys = key_ref[:, pl.ds(start, GROUP), :].reshape(columns, local)
        product = lax.dot_general(queries, keys, (((1,), (1,)), ((), ())), preferred_element_type=jnp.float32)
        scores.append(jnp.where(same, product, -jnp.inf))
    highest = [jnp.max(product, axis=-1, keepdims=True) for product in scores]
    scale = math.log2(math.e) / math.sqrt(HEAD_DIM)
    expo = [jnp.exp2((product - top) * scale).astype(jnp.bfloat16) for product, top in zip(scores, highest)]
    for start, weights in zip(starts, expo):
        values = value_ref[:, pl.ds(start, GROUP), :].reshape(columns, local)
        wide = jnp.dot(weights, values, preferred_element_type=jnp.float32)
        sums = jnp.dot(weights, ones, preferred_element_type=jnp.float32)
        sums = by_head(jnp.concatenate([sums] * (local // LANES), axis=1))
        mixed = by_head(wide) / sums
        mixed_ref[pl.ds(start * latents, rows), :] = mixed.astype(jnp.bfloat16)
    for step, out_ref in enumerate(out_refs):

        @pl.when(pl.program_id(0) == step)
        def _(out_ref=out_ref):
            out_ref[...] = mixed_ref[...]


def attend(place, queries, keys, values, first, block, steps):
    slots, latents, local = queries.shape
    levels = keys.shape[0]

    def chunk(i, place):
        return jnp.bitwise_xor(place[0], first - i)

    key_spec = pl.BlockSpec((levels, block, local), lambda i, place: (0, chunk(i, place), 0))
    return pl.pallas_call(
        attend_kernel,
        grid_spec=pltpu.PrefetchScalarGridSpec(
            num_scalar_prefetch=1,
            grid=(steps,),
            in_specs=[
                pl.BlockSpec((block, latents, local), lambda i, place: (chunk(i, place), 0, 0)),
                key_spec,
                key_spec,
            ],
            out_specs=[pl.BlockSpec((block * latents, local), lambda i, place: (0, 0))] * steps,
            scratch_shapes=[pltpu.VMEM((block * latents, local), jnp.bfloat16)],
        ),
        out_shape=[jax.ShapeDtypeStruct((block * latents, local), jnp.bfloat16)] * steps,
        compiler_params=params(20),
        cost_estimate=pl.CostEstimate(
            flops=16 * steps * block * latents * levels * GROUP * local,
            bytes_accessed=4 * steps * block * (latents + levels) * local,
            transcendentals=0,
        ),
        name="attend_slots",
    )(place, queries, keys, values)


def combine_kernel(place_ref, *refs):
    out_ref = refs[-1]
    total = None
    for mixed_ref, weight_ref in zip(refs[:4], refs[4:8]):
        term = jnp.dot(mixed_ref[...], weight_ref[...], preferred_element_type=jnp.float32)
        term = term.astype(jnp.bfloat16).astype(jnp.float32)
        total = term if total is None else total + term
    out_ref[...] = total.astype(jnp.bfloat16).reshape(out_ref.shape)


def combine(place, groups, weights, out, shape, first, block, steps):
    slots, latents, local = shape
    spec = pl.BlockSpec((block * latents, local), lambda i, place: (i, 0))
    in_specs = [spec] * 4 + [pl.BlockSpec(weights[0].shape, lambda i, place: (0, 0))] * 4
    operands = [place, *groups, *weights]
    aliases = {}
    if out is not None:
        aliases = {len(operands): 0}
        in_specs.append(pl.BlockSpec(memory_space=pl.ANY))
        operands.append(out)
    return pl.pallas_call(
        combine_kernel,
        grid_spec=pltpu.PrefetchScalarGridSpec(
            num_scalar_prefetch=1,
            grid=(steps,),
            in_specs=in_specs,
            out_specs=pl.BlockSpec(
                (block, latents, local), lambda i, place: (jnp.bitwise_xor(place[0], first - i), 0, 0)
            ),
        ),
        out_shape=jax.ShapeDtypeStruct((slots, latents, local), jnp.bfloat16),
        input_output_aliases=aliases,
        compiler_params=params(20),
        cost_estimate=pl.CostEstimate(
            flops=8 * steps * block * latents * local * local,
            bytes_accessed=10 * steps * block * latents * local,
            transcendentals=0,
        ),
        name="combine_groups",
    )(*operands)


def swap(array, axis_name, distance):
    size = lax.axis_size(axis_name)
    return lax.ppermute(array, axis_name, [(i, i ^ distance) for i in range(size)])


def spread_heads(mixed):
    second = swap(mixed, "head", 2)
    return mixed, swap(mixed, "head", 1), second, swap(second, "head", 1)


def spread_weight(out_weight, head):
    local = out_weight.shape[0]
    parts = []
    for distance in range(lax.axis_size("head")):
        start = jnp.bitwise_xor(head, distance) * local
        part = lax.dynamic_slice_in_dim(out_weight, start, local, 1)
        parts.append(swap(part, "head", distance) if distance else part)
    return parts


def shards(level_tokens, ln_gain, key_weight, value_weight, out_weight, ocean_queries, send_slots):
    stripes = lax.axis_size("lat")
    caps = send_slots.shape[2]
    shape = ocean_queries.shape
    slots, latents, local = shape
    by_stripe = (stripes, caps, latents, local)
    place = lax.axis_index("lat").reshape(1)
    queries = lax.all_to_all(ocean_queries.reshape(by_stripe), "lat", split_axis=0, concat_axis=0, tiled=True)
    queries = queries.reshape(shape)
    weights = spread_weight(out_weight, lax.axis_index("head"))
    tokens = jnp.transpose(level_tokens, (1, 0, 2))
    keys, values = project(send_slots[0], tokens, ln_gain, key_weight, value_weight)
    keys, weights = lax.optimization_barrier((keys, weights))
    if caps % GROUP:
        still = jnp.zeros_like(place)
        steps = slots // 64
        mixed = jnp.concatenate(attend(still + (steps - 1), queries, keys, values, steps - 1, 64, steps))
        mixed = lax.all_to_all(mixed.reshape(stripes, -1, local), "lat", split_axis=0, concat_axis=0, tiled=True)
        groups = spread_heads(mixed.reshape(-1, local))
        return combine(still + (steps - 1), groups, weights, None, shape, steps - 1, 64, steps)
    half = stripes // 2
    arrived = []
    for first in (stripes - 1, half - 1):
        chunks = attend(place, queries, keys, values, first, caps, half)
        chunks = [swap(chunk, "lat", first - i) if first - i else chunk for i, chunk in enumerate(chunks)]
        arrived.append((first, chunks))
    out = None
    for first, chunks in reversed(arrived):
        groups = spread_heads(jnp.concatenate(chunks))
        out = combine(place, groups, weights, out, shape, first, caps, half)
    return out


def solution(mesh):
    return jax.shard_map(
        shards,
        mesh=mesh,
        in_specs=(
            P("lat", None, None),
            P(),
            P(None, "head"),
            P(None, "head"),
            P("head", None),
            P("lat", None, "head"),
            P("lat", None, None),
        ),
        out_specs=P("lat", None, "head"),
        check_vma=False,
    )
```

```python
import functools
import math

import jax
import jax.numpy as jnp
from jax import lax
from jax.experimental import pallas as pl
from jax.experimental.pallas import tpu as pltpu
from jax.sharding import PartitionSpec as P

HEAD_DIM = 64
EPS = 1e-05
GROUP = 16
ROWS = 32
LANES = 128
MIB = 1024 * 1024


def params(mib):
    return pltpu.CompilerParams(vmem_limit_bytes=mib * MIB)


def normalize_rows(tokens, gain):
    width = tokens.shape[-1]
    tokens = tokens.astype(jnp.float32)
    center = jnp.sum(tokens, axis=-1, keepdims=True) * (1.0 / width)
    shifted = tokens - center
    spread = jnp.sum(shifted * shifted, axis=-1, keepdims=True) * (1.0 / width)
    return (shifted * lax.rsqrt(spread + EPS) * gain).astype(jnp.bfloat16)


def build_pick(slots_ref, pick_ref):
    stripes, caps = slots_ref.shape
    diagonal = lax.broadcasted_iota(jnp.int32, (caps, caps), 0) == lax.broadcasted_iota(jnp.int32, (caps, caps), 1)
    patch = lax.broadcasted_iota(jnp.int32, (caps, pick_ref.shape[1]), 1)
    for owner in range(stripes):
        row = jnp.broadcast_to(slots_ref[owner : owner + 1, :], (caps, caps))
        column = jnp.sum(jnp.where(diagonal, row, 0), axis=-1, keepdims=True)
        pick = jnp.where(patch == column, 1.0, 0.0)
        pick_ref[owner * caps : (owner + 1) * caps, :] = pick.astype(jnp.bfloat16)


def project_kernel(
    slots_ref,
    tokens_ref,
    gain_ref,
    key_weight_ref,
    value_weight_ref,
    out_ref,
    even_ref,
    odd_ref,
    pick_ref,
    weight_ref,
):
    step = pl.program_id(0)
    patches = tokens_ref.shape[1]
    local = key_weight_ref.shape[1]

    @pl.when(step == 0)
    def _():
        build_pick(slots_ref, pick_ref)
        weight_ref[:, :local] = key_weight_ref[...]
        weight_ref[:, local:] = value_weight_ref[...]

    def stage(write_ref, read_ref):
        gain = gain_ref[...]
        product = jnp.dot(read_ref[...], weight_ref[...], preferred_element_type=jnp.float32).astype(jnp.bfloat16)
        out_ref[0] = jnp.dot(pick_ref[...], product, preferred_element_type=jnp.float32).astype(jnp.bfloat16)
        for start in range(0, patches, ROWS):
            part = pl.ds(start, ROWS)
            write_ref[part, :] = normalize_rows(tokens_ref[0, part, :], gain)

    @pl.when(step % 2 == 0)
    def _():
        stage(even_ref, odd_ref)

    @pl.when(step % 2 == 1)
    def _():
        stage(odd_ref, even_ref)


def project(slots, tokens, gain, key_weight, value_weight):
    levels, patches, width = tokens.shape
    local = key_weight.shape[1]
    count = slots.size
    whole = lambda i: (0, 0)
    return pl.pallas_call(
        project_kernel,
        grid=(levels + 1,),
        in_specs=[
            pl.BlockSpec(slots.shape, whole),
            pl.BlockSpec((1, patches, width), lambda i: (jnp.minimum(i, levels - 1), 0, 0)),
            pl.BlockSpec((1, width), whole),
            pl.BlockSpec((width, local), whole),
            pl.BlockSpec((width, local), whole),
        ],
        out_specs=pl.BlockSpec((1, count, 2 * local), lambda i: (jnp.maximum(i - 1, 0), 0, 0)),
        out_shape=jax.ShapeDtypeStruct((levels, count, 2 * local), jnp.bfloat16),
        scratch_shapes=[
            pltpu.VMEM((patches, width), jnp.bfloat16),
            pltpu.VMEM((patches, width), jnp.bfloat16),
            pltpu.VMEM((count, patches), jnp.bfloat16),
            pltpu.VMEM((width, 2 * local), jnp.bfloat16),
        ],
        compiler_params=params(58),
        cost_estimate=pl.CostEstimate(
            flops=8 * levels * patches * (width + count) * local,
            bytes_accessed=2 * levels * patches * (width + 2 * local) + 4 * width * local,
            transcendentals=0,
        ),
        name="norm_project",
    )(slots, tokens, gain.reshape(1, width), key_weight, value_weight)


def attend_kernel(steps, place_ref, query_ref, pair_ref, *refs):
    out_refs, mixed_ref = refs[-1 - steps : -1], refs[-1]
    levels, slots, local = pair_ref.shape
    local = local // 2
    latents = query_ref.shape[1]
    heads = local // HEAD_DIM
    rows = GROUP * latents
    columns = levels * GROUP
    lane_head = lax.broadcasted_iota(jnp.int32, (rows, local), 1) // HEAD_DIM
    row_slot = (lax.broadcasted_iota(jnp.int32, (heads * rows, columns), 0) // latents) & (GROUP - 1)
    column_slot = lax.broadcasted_iota(jnp.int32, (heads * rows, columns), 1) & (GROUP - 1)
    same = row_slot - column_slot == 0
    ones = jnp.ones((columns, local), jnp.bfloat16)

    def by_head(wide):
        mixed = wide[:rows]
        for head in range(1, heads):
            mixed = jnp.where(lane_head == head, wide[head * rows : (head + 1) * rows], mixed)
        return mixed

    starts = range(0, slots, GROUP)
    scores = []
    for start in starts:
        queries = query_ref[pl.ds(start, GROUP)].reshape(rows, local).astype(jnp.float32)
        queries = jnp.concatenate(
            [jnp.where(lane_head == head, queries, 0.0).astype(jnp.bfloat16) for head in range(heads)], axis=0
        )
        keys = pair_ref[:, pl.ds(start, GROUP), :local].reshape(columns, local)
        product = lax.dot_general(queries, keys, (((1,), (1,)), ((), ())), preferred_element_type=jnp.float32)
        scores.append(jnp.where(same, product, -jnp.inf))
    highest = [jnp.max(product, axis=-1, keepdims=True) for product in scores]
    scale = math.log2(math.e) / math.sqrt(HEAD_DIM)
    expo = [jnp.exp2((product - top) * scale).astype(jnp.bfloat16) for product, top in zip(scores, highest)]
    for start, weights in zip(starts, expo):
        values = pair_ref[:, pl.ds(start, GROUP), local:].reshape(columns, local)
        values = jnp.concatenate([values, ones], axis=1)
        wide = jnp.dot(weights, values, preferred_element_type=jnp.float32)
        mixed = by_head(wide[:, :local]) / by_head(wide[:, local:])
        mixed_ref[pl.ds(start * latents, rows), :] = mixed.astype(jnp.bfloat16)
    for step, out_ref in enumerate(out_refs):

        @pl.when(pl.program_id(0) == step)
        def _(out_ref=out_ref):
            out_ref[...] = mixed_ref[...]


def attend(place, queries, pairs, first, block, steps, after=()):
    slots, latents, local = queries.shape
    levels = pairs.shape[0]

    def chunk(i, place):
        return jnp.bitwise_xor(place[0], first - i)

    return pl.pallas_call(
        functools.partial(attend_kernel, steps),
        grid_spec=pltpu.PrefetchScalarGridSpec(
            num_scalar_prefetch=1,
            grid=(steps,),
            in_specs=[
                pl.BlockSpec((block, latents, local), lambda i, place: (chunk(i, place), 0, 0)),
                pl.BlockSpec((levels, block, 2 * local), lambda i, place: (0, chunk(i, place), 0)),
            ]
            + [pl.BlockSpec(memory_space=pl.ANY)] * len(after),
            out_specs=[pl.BlockSpec((block * latents, local), lambda i, place: (0, 0))] * steps,
            scratch_shapes=[pltpu.VMEM((block * latents, local), jnp.bfloat16)],
        ),
        out_shape=[jax.ShapeDtypeStruct((block * latents, local), jnp.bfloat16)] * steps,
        compiler_params=params(58),
        cost_estimate=pl.CostEstimate(
            flops=64 * steps * block * latents * levels * GROUP * local,
            bytes_accessed=4 * steps * block * (latents + levels) * local,
            transcendentals=0,
        ),
        name="attend_slots",
    )(place, queries, pairs, *after)


def combine_kernel(first, steps, place_ref, *refs):
    out_ref = refs[-1]
    latents, local = out_ref.shape[1:]
    block = out_ref.shape[0] // steps
    for step in range(steps):
        part = pl.ds(step * block * latents, block * latents)
        total = None
        for mixed_ref, weight_ref in zip(refs[:4], refs[4:8]):
            term = jnp.dot(mixed_ref[part, :], weight_ref[...], preferred_element_type=jnp.float32)
            term = term.astype(jnp.bfloat16).astype(jnp.float32)
            total = term if total is None else total + term
        target = jnp.bitwise_and(jnp.bitwise_xor(place_ref[0], first - step), steps - 1)
        target = pl.ds(pl.multiple_of(target * block, block), block)
        out_ref[target] = total.astype(jnp.bfloat16).reshape(block, latents, local)


def combine(place, groups, weights, out, shape, first, block, steps):
    slots, latents, local = shape
    whole = lambda i, place: (0, 0)
    in_specs = [pl.BlockSpec(array.shape, whole) for array in (*groups, *weights)]
    operands = [place, *groups, *weights]
    aliases = {}
    if out is not None:
        aliases = {len(operands): 0}
        in_specs.append(pl.BlockSpec(memory_space=pl.ANY))
        operands.append(out)
    return pl.pallas_call(
        functools.partial(combine_kernel, first, steps),
        grid_spec=pltpu.PrefetchScalarGridSpec(
            num_scalar_prefetch=1,
            grid=(1,),
            in_specs=in_specs,
            out_specs=pl.BlockSpec(
                (steps * block, latents, local),
                lambda i, place: (jnp.bitwise_xor(place[0], first) // steps, 0, 0),
            ),
        ),
        out_shape=jax.ShapeDtypeStruct((slots, latents, local), jnp.bfloat16),
        input_output_aliases=aliases,
        compiler_params=params(20),
        cost_estimate=pl.CostEstimate(
            flops=24 * steps * block * latents * local * local,
            bytes_accessed=10 * steps * block * latents * local,
            transcendentals=0,
        ),
        name="combine_groups",
    )(*operands)


def swap(array, axis_name, distance):
    size = lax.axis_size(axis_name)
    return lax.ppermute(array, axis_name, [(i, i ^ distance) for i in range(size)])


def spread_heads(mixed):
    second = swap(mixed, "head", 2)
    return mixed, swap(mixed, "head", 1), second, swap(second, "head", 1)


def spread_weight(out_weight, head):
    local = out_weight.shape[0]
    parts = []
    for distance in range(lax.axis_size("head")):
        start = jnp.bitwise_xor(head, distance) * local
        part = lax.dynamic_slice_in_dim(out_weight, start, local, 1)
        parts.append(swap(part, "head", distance) if distance else part)
    return parts


def shards(level_tokens, ln_gain, key_weight, value_weight, out_weight, ocean_queries, send_slots):
    stripes = lax.axis_size("lat")
    caps = send_slots.shape[2]
    shape = ocean_queries.shape
    slots, latents, local = shape
    by_stripe = (stripes, caps, latents, local)
    place = lax.axis_index("lat").reshape(1)
    queries = lax.all_to_all(ocean_queries.reshape(by_stripe), "lat", split_axis=0, concat_axis=0, tiled=True)
    queries = queries.reshape(shape)
    weights = spread_weight(out_weight, lax.axis_index("head"))
    tokens = jnp.transpose(level_tokens, (1, 0, 2))
    pairs = project(send_slots[0], tokens, ln_gain, key_weight, value_weight)
    pairs, weights = lax.optimization_barrier((pairs, weights))
    if caps % GROUP:
        still = jnp.zeros_like(place)
        steps = slots // 64
        mixed = jnp.concatenate(attend(still + (steps - 1), queries, pairs, steps - 1, 64, steps))
        mixed = lax.all_to_all(mixed.reshape(stripes, -1, local), "lat", split_axis=0, concat_axis=0, tiled=True)
        groups = spread_heads(mixed.reshape(-1, local))
        return combine(still + (steps - 1), groups, weights, None, shape, steps - 1, 64, steps)
    batches = [(stripes - 1, stripes // 4), (stripes * 3 // 4 - 1, stripes // 4), (stripes // 2 - 1, stripes // 2)]
    arrived = []
    chunks = ()
    for first, steps in batches:
        chunks = attend(place, queries, pairs, first, caps, steps, after=chunks[:1])
        moved = [swap(chunk, "lat", first - i) if first - i else chunk for i, chunk in enumerate(chunks)]
        arrived.append((first, steps, moved))
    out = None
    for first, steps, moved in arrived:
        groups = spread_heads(jnp.concatenate(moved))
        out = combine(place, groups, weights, out, shape, first, caps, steps)
    return out


def solution(mesh):
    return jax.shard_map(
        shards,
        mesh=mesh,
        in_specs=(
            P("lat", None, None),
            P(),
            P(None, "head"),
            P(None, "head"),
            P("head", None),
            P("lat", None, "head"),
            P("lat", None, None),
        ),
        out_specs=P("lat", None, "head"),
        check_vma=False,
    )
```

```python
import functools
import math

import jax
import jax.numpy as jnp
from jax import lax
from jax.experimental import pallas as pl
from jax.experimental.pallas import tpu as pltpu
from jax.sharding import PartitionSpec as P

HEAD_DIM = 64
EPS = 1e-05
GROUP = 16
ROWS = 32
LANES = 128
MIB = 1024 * 1024


def params(mib):
    return pltpu.CompilerParams(vmem_limit_bytes=mib * MIB)


def normalize_rows(tokens, gain):
    width = tokens.shape[-1]
    tokens = tokens.astype(jnp.float32)
    center = jnp.sum(tokens, axis=-1, keepdims=True) * (1.0 / width)
    shifted = tokens - center
    spread = jnp.sum(shifted * shifted, axis=-1, keepdims=True) * (1.0 / width)
    return (shifted * lax.rsqrt(spread + EPS) * gain).astype(jnp.bfloat16)


def build_pick(slots_ref, pick_ref):
    stripes, caps = slots_ref.shape
    diagonal = lax.broadcasted_iota(jnp.int32, (caps, caps), 0) == lax.broadcasted_iota(jnp.int32, (caps, caps), 1)
    patch = lax.broadcasted_iota(jnp.int32, (caps, pick_ref.shape[1]), 1)
    for owner in range(stripes):
        row = jnp.broadcast_to(slots_ref[owner : owner + 1, :], (caps, caps))
        column = jnp.sum(jnp.where(diagonal, row, 0), axis=-1, keepdims=True)
        pick = jnp.where(patch == column, 1.0, 0.0)
        pick_ref[owner * caps : (owner + 1) * caps, :] = pick.astype(jnp.bfloat16)


def project_kernel(
    slots_ref,
    tokens_ref,
    gain_ref,
    key_weight_ref,
    value_weight_ref,
    out_ref,
    even_ref,
    odd_ref,
    pick_ref,
    weight_ref,
):
    step = pl.program_id(0)
    patches = tokens_ref.shape[1]
    local = key_weight_ref.shape[1]

    @pl.when(step == 0)
    def _():
        build_pick(slots_ref, pick_ref)
        weight_ref[:, :local] = key_weight_ref[...]
        weight_ref[:, local:] = value_weight_ref[...]

    def stage(write_ref, read_ref):
        gain = gain_ref[...]
        product = jnp.dot(read_ref[...], weight_ref[...], preferred_element_type=jnp.float32).astype(jnp.bfloat16)
        out_ref[0] = jnp.dot(pick_ref[...], product, preferred_element_type=jnp.float32).astype(jnp.bfloat16)
        for start in range(0, patches, ROWS):
            part = pl.ds(start, ROWS)
            write_ref[part, :] = normalize_rows(tokens_ref[0, part, :], gain)

    @pl.when(step % 2 == 0)
    def _():
        stage(even_ref, odd_ref)

    @pl.when(step % 2 == 1)
    def _():
        stage(odd_ref, even_ref)


def project(slots, tokens, gain, key_weight, value_weight):
    levels, patches, width = tokens.shape
    local = key_weight.shape[1]
    count = slots.size
    whole = lambda i: (0, 0)
    return pl.pallas_call(
        project_kernel,
        grid=(levels + 1,),
        in_specs=[
            pl.BlockSpec(slots.shape, whole),
            pl.BlockSpec((1, patches, width), lambda i: (jnp.minimum(i, levels - 1), 0, 0)),
            pl.BlockSpec((1, width), whole),
            pl.BlockSpec((width, local), whole),
            pl.BlockSpec((width, local), whole),
        ],
        out_specs=pl.BlockSpec((1, count, 2 * local), lambda i: (jnp.maximum(i - 1, 0), 0, 0)),
        out_shape=jax.ShapeDtypeStruct((levels, count, 2 * local), jnp.bfloat16),
        scratch_shapes=[
            pltpu.VMEM((patches, width), jnp.bfloat16),
            pltpu.VMEM((patches, width), jnp.bfloat16),
            pltpu.VMEM((count, patches), jnp.bfloat16),
            pltpu.VMEM((width, 2 * local), jnp.bfloat16),
        ],
        compiler_params=params(58),
        cost_estimate=pl.CostEstimate(
            flops=8 * levels * patches * (width + count) * local,
            bytes_accessed=2 * levels * patches * (width + 2 * local) + 4 * width * local,
            transcendentals=0,
        ),
        name="norm_project",
    )(slots, tokens, gain.reshape(1, width), key_weight, value_weight)


def attend_kernel(sizes, place_ref, query_ref, pair_ref, *refs):
    out_refs, mixed_ref, bias_ref = refs[: len(sizes)], refs[-2], refs[-1]
    levels, slots, local = pair_ref.shape
    local = local // 2
    latents = query_ref.shape[1]
    rows = GROUP * latents
    columns = levels * GROUP
    heads = LANES // HEAD_DIM
    step = pl.program_id(0)

    @pl.when(step == 0)
    def _():
        row_slot = lax.broadcasted_iota(jnp.int32, bias_ref.shape, 0) // latents
        column_slot = lax.broadcasted_iota(jnp.int32, bias_ref.shape, 1) & (GROUP - 1)
        bias_ref[...] = jnp.where(row_slot - column_slot == 0, 0.0, -jnp.inf)

    lane_head = lax.broadcasted_iota(jnp.int32, (rows, LANES), 1) // HEAD_DIM
    ones = jnp.ones((columns, LANES), jnp.bfloat16)
    scale = math.log2(math.e) / math.sqrt(HEAD_DIM)

    def by_head(wide):
        mixed = wide[:rows]
        for head in range(1, heads):
            mixed = jnp.where(lane_head == head, wide[head * rows : (head + 1) * rows], mixed)
        return mixed

    tasks = [(start, lane) for start in range(0, slots, GROUP) for lane in range(0, local, LANES)]
    scores = []
    for start, lane in tasks:
        queries = query_ref[pl.ds(start, GROUP), :, pl.ds(lane, LANES)].reshape(rows, LANES).astype(jnp.float32)
        queries = jnp.concatenate(
            [jnp.where(lane_head == head, queries, 0.0).astype(jnp.bfloat16) for head in range(heads)], axis=0
        )
        keys = pair_ref[:, pl.ds(start, GROUP), pl.ds(lane, LANES)].reshape(columns, LANES)
        product = lax.dot_general(queries, keys, (((1,), (1,)), ((), ())), preferred_element_type=jnp.float32)
        scores.append(product + jnp.concatenate([bias_ref[...]] * heads, axis=0))
    highest = [jnp.max(product, axis=-1, keepdims=True) for product in scores]
    expo = [jnp.exp2((product - top) * scale).astype(jnp.bfloat16) for product, top in zip(scores, highest)]
    for (start, lane), weights in zip(tasks, expo):
        values = pair_ref[:, pl.ds(start, GROUP), pl.ds(local + lane, LANES)].reshape(columns, LANES)
        wide = jnp.dot(weights, jnp.concatenate([values, ones], axis=1), preferred_element_type=jnp.float32)
        mixed = by_head(wide[:, :LANES]) / by_head(wide[:, LANES:])
        mixed_ref[pl.ds(start * latents, rows), pl.ds(lane, LANES)] = mixed.astype(jnp.bfloat16)
    begin = 0
    for size, out_ref in zip(sizes, out_refs):

        @pl.when((step >= begin) & (step < begin + size))
        def _(out_ref=out_ref):
            out_ref[...] = mixed_ref[...]

        begin += size


def attend(place, queries, pairs, block, sizes):
    slots, latents, local = queries.shape
    levels = pairs.shape[0]
    rows = block * latents
    steps = sum(sizes)
    begins = [sum(sizes[:index]) for index in range(len(sizes))]

    def chunk(i, place):
        return jnp.bitwise_xor(place[0], steps - 1 - i)

    def out_spec(begin, size):
        return pl.BlockSpec((rows, local), lambda i, place: (jnp.clip(i - begin, 0, size - 1), 0))

    return pl.pallas_call(
        functools.partial(attend_kernel, sizes),
        grid_spec=pltpu.PrefetchScalarGridSpec(
            num_scalar_prefetch=1,
            grid=(steps,),
            in_specs=[
                pl.BlockSpec((block, latents, local), lambda i, place: (chunk(i, place), 0, 0)),
                pl.BlockSpec((levels, block, 2 * local), lambda i, place: (0, chunk(i, place), 0)),
            ],
            out_specs=[out_spec(begin, size) for begin, size in zip(begins, sizes)],
            scratch_shapes=[
                pltpu.VMEM((rows, local), jnp.bfloat16),
                pltpu.VMEM((GROUP * latents, levels * GROUP), jnp.float32),
            ],
        ),
        out_shape=[jax.ShapeDtypeStruct((size * rows, local), jnp.bfloat16) for size in sizes],
        compiler_params=params(58),
        cost_estimate=pl.CostEstimate(
            flops=64 * slots * latents * levels * GROUP * local,
            bytes_accessed=4 * slots * (latents + levels) * local,
            transcendentals=0,
        ),
        name="attend_slots",
    )(place, queries, pairs)


def combine_rows(part, mixed_refs, weight_refs):
    total = None
    for mixed_ref, weight_ref in zip(mixed_refs, weight_refs):
        term = jnp.dot(mixed_ref[part, :], weight_ref[...], preferred_element_type=jnp.float32)
        term = term.astype(jnp.bfloat16).astype(jnp.float32)
        total = term if total is None else total + term
    return total.astype(jnp.bfloat16)


def combine_kernel(first, steps, place_ref, *refs):
    out_refs = refs[8:] if first is None else refs[-1:]
    latents, local = out_refs[0].shape[1:]
    block = refs[0].shape[0] // steps // latents
    for step in range(steps):
        part = pl.ds(step * block * latents, block * latents)
        rows = combine_rows(part, refs[:4], refs[4:8]).reshape(block, latents, local)
        if first is None:
            out_refs[step][...] = rows
        else:
            target = jnp.bitwise_and(jnp.bitwise_xor(place_ref[0], first - step), steps - 1)
            out_refs[0][pl.ds(pl.multiple_of(target * block, block), block)] = rows


def combine(place, groups, weights, shape, block, steps, first=None, out=None):
    slots, latents, local = shape
    whole = lambda i, place: (0, 0)
    operands = [place, *groups, *weights]
    in_specs = [pl.BlockSpec(array.shape, whole) for array in operands[1:]]
    aliases = {}
    if out is not None:
        aliases = {len(operands): 0}
        operands.append(out)
        in_specs.append(pl.BlockSpec(memory_space=pl.ANY))
    if first is None:
        out_specs = [pl.BlockSpec((block, latents, local), lambda i, place: (0, 0, 0))] * steps
        out_shape = [jax.ShapeDtypeStruct((block, latents, local), jnp.bfloat16)] * steps
    else:
        out_specs = pl.BlockSpec(
            (steps * block, latents, local), lambda i, place: (jnp.bitwise_xor(place[0], first) // steps, 0, 0)
        )
        out_shape = jax.ShapeDtypeStruct(shape, jnp.bfloat16)
    return pl.pallas_call(
        functools.partial(combine_kernel, first, steps),
        grid_spec=pltpu.PrefetchScalarGridSpec(
            num_scalar_prefetch=1,
            grid=(1,),
            in_specs=in_specs,
            out_specs=out_specs,
        ),
        out_shape=out_shape,
        input_output_aliases=aliases,
        compiler_params=params(20),
        cost_estimate=pl.CostEstimate(
            flops=24 * steps * block * latents * local * local,
            bytes_accessed=10 * steps * block * latents * local,
            transcendentals=0,
        ),
        name="combine_groups",
    )(*operands)


def settle_kernel(distances, place_ref, *refs):
    count = len(distances)
    out_ref, done = refs[count], refs[count + 1]
    copies = []
    for index, distance in enumerate(distances):
        block = refs[index].shape[0]
        target = pl.multiple_of(jnp.bitwise_xor(place_ref[0], distance) * block, block)
        copies.append(pltpu.make_async_copy(refs[index], out_ref.at[pl.ds(target, block)], done.at[index]))
    for copy in copies:
        copy.start()
    for copy in copies:
        copy.wait()


def settle(place, chunks, shape):
    anywhere = pl.BlockSpec(memory_space=pl.ANY)
    distances = tuple(chunks)
    return pl.pallas_call(
        functools.partial(settle_kernel, distances),
        grid_spec=pltpu.PrefetchScalarGridSpec(
            num_scalar_prefetch=1,
            grid=(1,),
            in_specs=[anywhere] * len(distances),
            out_specs=anywhere,
            scratch_shapes=[pltpu.SemaphoreType.DMA((len(distances),))],
        ),
        out_shape=jax.ShapeDtypeStruct(shape, jnp.bfloat16),
        compiler_params=params(20),
        cost_estimate=pl.CostEstimate(flops=0, bytes_accessed=4 * math.prod(shape), transcendentals=0),
        name="settle_chunks",
    )(place, *chunks.values())


def swap(array, axis_name, distance):
    size = lax.axis_size(axis_name)
    return lax.ppermute(array, axis_name, [(i, i ^ distance) for i in range(size)])


def follow(array, others):
    return lax.optimization_barrier((array, *others))[0]


def spread_heads(mixed):
    second = swap(mixed, "head", 2)
    return mixed, swap(mixed, "head", 1), second, swap(second, "head", 1)


def spread_weight(out_weight, head):
    local = out_weight.shape[0]
    parts = []
    for distance in range(lax.axis_size("head")):
        start = jnp.bitwise_xor(head, distance) * local
        part = lax.dynamic_slice_in_dim(out_weight, start, local, 1)
        parts.append(swap(part, "head", distance) if distance else part)
    return parts


def shards(level_tokens, ln_gain, key_weight, value_weight, out_weight, ocean_queries, send_slots):
    stripes = lax.axis_size("lat")
    caps = send_slots.shape[2]
    shape = ocean_queries.shape
    slots, latents, local = shape
    by_stripe = (stripes, caps, latents, local)
    place = lax.axis_index("lat").reshape(1)
    queries = lax.all_to_all(ocean_queries.reshape(by_stripe), "lat", split_axis=0, concat_axis=0, tiled=True)
    queries = queries.reshape(shape)
    weights = spread_weight(out_weight, lax.axis_index("head"))
    tokens = jnp.transpose(level_tokens, (1, 0, 2))
    pairs = project(send_slots[0], tokens, ln_gain, key_weight, value_weight)
    pairs, weights = lax.optimization_barrier((pairs, weights))
    if caps % GROUP:
        still = jnp.zeros_like(place)
        steps = slots // 64
        (mixed,) = attend(still + (steps - 1), queries, pairs, 64, (steps,))
        mixed = lax.all_to_all(mixed.reshape(stripes, -1, local), "lat", split_axis=0, concat_axis=0, tiled=True)
        groups = spread_heads(mixed.reshape(-1, local))
        return combine(still + (steps - 1), groups, weights, shape, 64, steps, steps - 1)
    pair = stripes // 4
    *far, near = attend(place, queries, pairs, caps, (1,) * (2 * pair) + (2 * pair,))
    far = [swap(chunk, "lat", stripes - 1 - i) for i, chunk in enumerate(far)]
    far, middle = jnp.concatenate(far[:pair]), jnp.concatenate(far[pair:])
    near = combine(place, spread_heads(near), weights, shape, caps, 2 * pair)
    far = combine(place, spread_heads(far), weights, shape, caps, pair)
    second = swap(middle, "head", 2)
    chunks = {stripes - 1 - i: chunk for i, chunk in enumerate(far)}
    for i, chunk in enumerate(near):
        distance = 2 * pair - 1 - i
        chunks[distance] = swap(chunk, "lat", distance) if distance else chunk
    out = settle(place, chunks, shape)
    middle = (middle, swap(middle, "head", 1), second, swap(follow(second, (out,)), "head", 1))
    return combine(place, middle, weights, shape, caps, pair, 3 * pair - 1, out)


def solution(mesh):
    return jax.shard_map(
        shards,
        mesh=mesh,
        in_specs=(
            P("lat", None, None),
            P(),
            P(None, "head"),
            P(None, "head"),
            P("head", None),
            P("lat", None, "head"),
            P("lat", None, None),
        ),
        out_specs=P("lat", None, "head"),
        check_vma=False,
    )
```

```python
import functools
import math

import jax
import jax.numpy as jnp
from jax import lax
from jax.experimental import pallas as pl
from jax.experimental.pallas import tpu as pltpu
from jax.sharding import PartitionSpec as P

HEAD_DIM = 64
EPS = 1e-05
GROUP = 16
ROWS = 32
LANES = 128
MIB = 1024 * 1024


def params(mib):
    return pltpu.CompilerParams(vmem_limit_bytes=mib * MIB)


def normalize_rows(tokens, gain):
    width = tokens.shape[-1]
    tokens = tokens.astype(jnp.float32)
    center = jnp.sum(tokens, axis=-1, keepdims=True) * (1.0 / width)
    shifted = tokens - center
    spread = jnp.sum(shifted * shifted, axis=-1, keepdims=True) * (1.0 / width)
    return (shifted * lax.rsqrt(spread + EPS) * gain).astype(jnp.bfloat16)


def build_pick(slots_ref, pick_ref):
    stripes, caps = slots_ref.shape
    diagonal = lax.broadcasted_iota(jnp.int32, (caps, caps), 0) == lax.broadcasted_iota(jnp.int32, (caps, caps), 1)
    patch = lax.broadcasted_iota(jnp.int32, (caps, pick_ref.shape[1]), 1)
    for owner in range(stripes):
        row = jnp.broadcast_to(slots_ref[owner : owner + 1, :], (caps, caps))
        column = jnp.sum(jnp.where(diagonal, row, 0), axis=-1, keepdims=True)
        pick = jnp.where(patch == column, 1.0, 0.0)
        pick_ref[owner * caps : (owner + 1) * caps, :] = pick.astype(jnp.bfloat16)


def project_kernel(
    slots_ref,
    tokens_ref,
    gain_ref,
    key_weight_ref,
    value_weight_ref,
    out_ref,
    even_ref,
    odd_ref,
    pick_ref,
    weight_ref,
):
    step = pl.program_id(0)
    patches = tokens_ref.shape[1]
    local = key_weight_ref.shape[1]

    @pl.when(step == 0)
    def _():
        build_pick(slots_ref, pick_ref)
        weight_ref[:, :local] = key_weight_ref[...]
        weight_ref[:, local:] = value_weight_ref[...]

    def stage(write_ref, read_ref):
        gain = gain_ref[...]
        half, quarter = patches // 2, patches // 4

        def normalize(index):
            for start in range(index * quarter, (index + 1) * quarter, ROWS):
                part = pl.ds(start, ROWS)
                write_ref[part, :] = normalize_rows(tokens_ref[0, part, :], gain)

        products = []
        for index in range(2):
            part = pl.ds(index * half, half)
            product = jnp.dot(read_ref[part, :], weight_ref[...], preferred_element_type=jnp.float32)
            products.append(product.astype(jnp.bfloat16))
            normalize(index)
        product = jnp.concatenate(products, axis=0)
        half = out_ref.shape[1] // 2
        for index in range(2):
            part = pl.ds(index * half, half)
            picked = jnp.dot(pick_ref[part, :], product, preferred_element_type=jnp.float32)
            out_ref[0, part, :] = picked.astype(jnp.bfloat16)
            normalize(2 + index)

    @pl.when(step % 2 == 0)
    def _():
        stage(even_ref, odd_ref)

    @pl.when(step % 2 == 1)
    def _():
        stage(odd_ref, even_ref)


def project(slots, tokens, gain, key_weight, value_weight):
    levels, patches, width = tokens.shape
    local = key_weight.shape[1]
    count = slots.size
    whole = lambda i: (0, 0)
    return pl.pallas_call(
        project_kernel,
        grid=(levels + 1,),
        in_specs=[
            pl.BlockSpec(slots.shape, whole),
            pl.BlockSpec((1, patches, width), lambda i: (jnp.minimum(i, levels - 1), 0, 0)),
            pl.BlockSpec((1, width), whole),
            pl.BlockSpec((width, local), whole),
            pl.BlockSpec((width, local), whole),
        ],
        out_specs=pl.BlockSpec((1, count, 2 * local), lambda i: (jnp.maximum(i - 1, 0), 0, 0)),
        out_shape=jax.ShapeDtypeStruct((levels, count, 2 * local), jnp.bfloat16),
        scratch_shapes=[
            pltpu.VMEM((patches, width), jnp.bfloat16),
            pltpu.VMEM((patches, width), jnp.bfloat16),
            pltpu.VMEM((count, patches), jnp.bfloat16),
            pltpu.VMEM((width, 2 * local), jnp.bfloat16),
        ],
        compiler_params=params(58),
        cost_estimate=pl.CostEstimate(
            flops=8 * levels * patches * (width + count) * local,
            bytes_accessed=2 * levels * patches * (width + 2 * local) + 4 * width * local,
            transcendentals=0,
        ),
        name="norm_project",
    )(slots, tokens, gain.reshape(1, width), key_weight, value_weight)


def attend_kernel(sizes, place_ref, query_ref, pair_ref, *refs):
    out_refs, mixed_ref = refs[: len(sizes)], refs[-1]
    levels, slots, local = pair_ref.shape
    local = local // 2
    latents = query_ref.shape[1]
    rows = GROUP * latents
    columns = levels * GROUP
    heads = LANES // HEAD_DIM
    step = pl.program_id(0)
    lane_head = lax.broadcasted_iota(jnp.int32, (rows, LANES), 1) // HEAD_DIM
    row_slot = lax.broadcasted_iota(jnp.int32, (GROUP, heads * rows), 0)
    column_slot = (lax.broadcasted_iota(jnp.int32, (GROUP, heads * rows), 1) // latents) & (GROUP - 1)
    same = row_slot - column_slot == 0
    scale = math.log2(math.e) / math.sqrt(HEAD_DIM)
    queries = query_ref[...].reshape(slots * latents, local).astype(jnp.float32)

    tasks = [(start, lane) for start in range(0, slots, GROUP) for lane in range(0, local, LANES)]
    scores = []
    for start, lane in tasks:
        part = queries[start * latents : start * latents + rows, lane : lane + LANES]
        part = jnp.concatenate(
            [jnp.where(lane_head == head, part, 0.0).astype(jnp.bfloat16) for head in range(heads)], axis=0
        )
        keys = pair_ref[:, pl.ds(start, GROUP), pl.ds(lane, LANES)].reshape(columns, LANES)
        product = lax.dot_general(keys, part, (((1,), (1,)), ((), ())), preferred_element_type=jnp.float32)
        scores.append(product.reshape(levels, GROUP, heads * rows))
    softs = []
    for product in scores:
        expo = jnp.exp2((product - jnp.max(product, axis=0, keepdims=True)) * scale)
        inverse = jnp.where(same, 1.0 / jnp.sum(expo, axis=0), 0.0)
        softs.append((expo * inverse[None]).reshape(columns, heads * rows).astype(jnp.bfloat16))
    for (start, lane), soft in zip(tasks, softs):
        values = pair_ref[:, pl.ds(start, GROUP), pl.ds(local + lane, LANES)].reshape(columns, LANES)
        wide = lax.dot_general(soft, values, (((0,), (0,)), ((), ())), preferred_element_type=jnp.float32)
        mixed = wide[:rows]
        for head in range(1, heads):
            mixed = jnp.where(lane_head == head, wide[head * rows : (head + 1) * rows], mixed)
        mixed_ref[pl.ds(start * latents, rows), pl.ds(lane, LANES)] = mixed.astype(jnp.bfloat16)
    begin = 0
    for size, out_ref in zip(sizes, out_refs):

        @pl.when((step >= begin) & (step < begin + size))
        def _(out_ref=out_ref):
            out_ref[...] = mixed_ref[...]

        begin += size


def attend(place, queries, pairs, block, sizes):
    slots, latents, local = queries.shape
    levels = pairs.shape[0]
    rows = block * latents
    steps = sum(sizes)
    begins = [sum(sizes[:index]) for index in range(len(sizes))]

    def chunk(i, place):
        return jnp.bitwise_xor(place[0], steps - 1 - i)

    def out_spec(begin, size):
        return pl.BlockSpec((rows, local), lambda i, place: (jnp.clip(i - begin, 0, size - 1), 0))

    return pl.pallas_call(
        functools.partial(attend_kernel, sizes),
        grid_spec=pltpu.PrefetchScalarGridSpec(
            num_scalar_prefetch=1,
            grid=(steps,),
            in_specs=[
                pl.BlockSpec((block, latents, local), lambda i, place: (chunk(i, place), 0, 0)),
                pl.BlockSpec((levels, block, 2 * local), lambda i, place: (0, chunk(i, place), 0)),
            ],
            out_specs=[out_spec(begin, size) for begin, size in zip(begins, sizes)],
            scratch_shapes=[pltpu.VMEM((rows, local), jnp.bfloat16)],
        ),
        out_shape=[jax.ShapeDtypeStruct((size * rows, local), jnp.bfloat16) for size in sizes],
        compiler_params=params(58),
        cost_estimate=pl.CostEstimate(
            flops=64 * slots * latents * levels * GROUP * local,
            bytes_accessed=4 * slots * (latents + levels) * local,
            transcendentals=0,
        ),
        name="attend_slots",
    )(place, queries, pairs)


def combine_rows(part, mixed_refs, weight_refs):
    total = None
    for mixed_ref, weight_ref in zip(mixed_refs, weight_refs):
        term = jnp.dot(mixed_ref[part, :], weight_ref[...], preferred_element_type=jnp.float32)
        term = term.astype(jnp.bfloat16).astype(jnp.float32)
        total = term if total is None else total + term
    return total.astype(jnp.bfloat16)


def combine_kernel(first, steps, place_ref, *refs):
    out_refs = refs[8:] if first is None else refs[-1:]
    latents, local = out_refs[0].shape[1:]
    block = refs[0].shape[0] // steps // latents
    for step in range(steps):
        part = pl.ds(step * block * latents, block * latents)
        rows = combine_rows(part, refs[:4], refs[4:8]).reshape(block, latents, local)
        if first is None:
            out_refs[step][...] = rows
        else:
            target = jnp.bitwise_and(jnp.bitwise_xor(place_ref[0], first - step), steps - 1)
            out_refs[0][pl.ds(pl.multiple_of(target * block, block), block)] = rows


def combine(place, groups, weights, shape, block, steps, first=None, out=None):
    slots, latents, local = shape
    whole = lambda i, place: (0, 0)
    operands = [place, *groups, *weights]
    in_specs = [pl.BlockSpec(array.shape, whole) for array in operands[1:]]
    aliases = {}
    if out is not None:
        aliases = {len(operands): 0}
        operands.append(out)
        in_specs.append(pl.BlockSpec(memory_space=pl.ANY))
    if first is None:
        out_specs = [pl.BlockSpec((block, latents, local), lambda i, place: (0, 0, 0))] * steps
        out_shape = [jax.ShapeDtypeStruct((block, latents, local), jnp.bfloat16)] * steps
    else:
        out_specs = pl.BlockSpec(
            (steps * block, latents, local), lambda i, place: (jnp.bitwise_xor(place[0], first) // steps, 0, 0)
        )
        out_shape = jax.ShapeDtypeStruct(shape, jnp.bfloat16)
    return pl.pallas_call(
        functools.partial(combine_kernel, first, steps),
        grid_spec=pltpu.PrefetchScalarGridSpec(
            num_scalar_prefetch=1,
            grid=(1,),
            in_specs=in_specs,
            out_specs=out_specs,
        ),
        out_shape=out_shape,
        input_output_aliases=aliases,
        compiler_params=params(20),
        cost_estimate=pl.CostEstimate(
            flops=24 * steps * block * latents * local * local,
            bytes_accessed=10 * steps * block * latents * local,
            transcendentals=0,
        ),
        name="combine_groups",
    )(*operands)


def settle_kernel(distances, place_ref, *refs):
    count = len(distances)
    out_ref, done = refs[count], refs[count + 1]
    copies = []
    for index, distance in enumerate(distances):
        block = refs[index].shape[0]
        target = pl.multiple_of(jnp.bitwise_xor(place_ref[0], distance) * block, block)
        copies.append(pltpu.make_async_copy(refs[index], out_ref.at[pl.ds(target, block)], done.at[index]))
    for copy in copies:
        copy.start()
    for copy in copies:
        copy.wait()


def settle(place, chunks, shape):
    anywhere = pl.BlockSpec(memory_space=pl.ANY)
    distances = tuple(chunks)
    return pl.pallas_call(
        functools.partial(settle_kernel, distances),
        grid_spec=pltpu.PrefetchScalarGridSpec(
            num_scalar_prefetch=1,
            grid=(1,),
            in_specs=[anywhere] * len(distances),
            out_specs=anywhere,
            scratch_shapes=[pltpu.SemaphoreType.DMA((len(distances),))],
        ),
        out_shape=jax.ShapeDtypeStruct(shape, jnp.bfloat16),
        compiler_params=params(20),
        cost_estimate=pl.CostEstimate(flops=0, bytes_accessed=4 * math.prod(shape), transcendentals=0),
        name="settle_chunks",
    )(place, *chunks.values())


def swap(array, axis_name, distance):
    size = lax.axis_size(axis_name)
    return lax.ppermute(array, axis_name, [(i, i ^ distance) for i in range(size)])


def follow(array, others):
    return lax.optimization_barrier((array, *others))[0]


def spread_heads(mixed, others=()):
    second = swap(mixed, "head", 2)
    late = follow(second, others) if others else second
    return mixed, swap(follow(mixed, (late,)), "head", 1), second, swap(late, "head", 1)


def spread_weight(out_weight, head):
    local = out_weight.shape[0]
    parts = []
    for distance in range(lax.axis_size("head")):
        start = jnp.bitwise_xor(head, distance) * local
        part = lax.dynamic_slice_in_dim(out_weight, start, local, 1)
        parts.append(swap(part, "head", distance) if distance else part)
    return parts


def shards(level_tokens, ln_gain, key_weight, value_weight, out_weight, ocean_queries, send_slots):
    stripes = lax.axis_size("lat")
    caps = send_slots.shape[2]
    shape = ocean_queries.shape
    slots, latents, local = shape
    by_stripe = (stripes, caps, latents, local)
    place = lax.axis_index("lat").reshape(1)
    queries = lax.all_to_all(ocean_queries.reshape(by_stripe), "lat", split_axis=0, concat_axis=0, tiled=True)
    queries = queries.reshape(shape)
    weights = spread_weight(out_weight, lax.axis_index("head"))
    tokens = jnp.transpose(level_tokens, (1, 0, 2))
    pairs = project(send_slots[0], tokens, ln_gain, key_weight, value_weight)
    pairs, weights = lax.optimization_barrier((pairs, weights))
    if caps % GROUP:
        still = jnp.zeros_like(place)
        steps = slots // 64
        (mixed,) = attend(still + (steps - 1), queries, pairs, 64, (steps,))
        mixed = lax.all_to_all(mixed.reshape(stripes, -1, local), "lat", split_axis=0, concat_axis=0, tiled=True)
        groups = spread_heads(mixed.reshape(-1, local))
        return combine(still + (steps - 1), groups, weights, shape, 64, steps, steps - 1)
    pair = stripes // 4
    *far, near = attend(place, queries, pairs, caps, (1,) * (2 * pair) + (2 * pair,))
    far = [swap(chunk, "lat", stripes - 1 - i) for i, chunk in enumerate(far)]
    near = combine(place, spread_heads(near, far[pair : pair + 1]), weights, shape, caps, 2 * pair)
    far, middle = jnp.concatenate(far[:pair]), jnp.concatenate(far[pair:])
    far = combine(place, spread_heads(far), weights, shape, caps, pair)
    chunks = {stripes - 1 - i: chunk for i, chunk in enumerate(far)}
    for i, chunk in enumerate(near):
        distance = 2 * pair - 1 - i
        chunks[distance] = swap(chunk, "lat", distance) if distance else chunk
    out = settle(place, chunks, shape)
    middle = spread_heads(middle, (out,))
    return combine(place, middle, weights, shape, caps, pair, 3 * pair - 1, out)


def solution(mesh):
    return jax.shard_map(
        shards,
        mesh=mesh,
        in_specs=(
            P("lat", None, None),
            P(),
            P(None, "head"),
            P(None, "head"),
            P("head", None),
            P("lat", None, "head"),
            P("lat", None, None),
        ),
        out_specs=P("lat", None, "head"),
        check_vma=False,
    )
```

```python
import math

import jax
import jax.numpy as jnp
from jax import lax
from jax.experimental import pallas as pl
from jax.experimental.pallas import tpu as pltpu
from jax.sharding import PartitionSpec as P

HEAD_DIM = 64
EPS = 1e-05
GROUP = 16
BLOCK = 64
ROWS = 32
LANES = 128
MIB = 1024 * 1024


def params(mib):
    return pltpu.CompilerParams(vmem_limit_bytes=mib * MIB)


def normalize_rows(tokens, gain):
    width = tokens.shape[-1]
    tokens = tokens.astype(jnp.float32)
    center = jnp.sum(tokens, axis=-1, keepdims=True) * (1.0 / width)
    shifted = tokens - center
    spread = jnp.sum(shifted * shifted, axis=-1, keepdims=True) * (1.0 / width)
    return (shifted * lax.rsqrt(spread + EPS) * gain).astype(jnp.bfloat16)


def build_pick(slots_ref, pick_ref):
    stripes, caps = slots_ref.shape
    diagonal = lax.broadcasted_iota(jnp.int32, (caps, caps), 0) == lax.broadcasted_iota(jnp.int32, (caps, caps), 1)
    patch = lax.broadcasted_iota(jnp.int32, (caps, pick_ref.shape[1]), 1)
    for owner in range(stripes):
        row = jnp.broadcast_to(slots_ref[owner : owner + 1, :], (caps, caps))
        column = jnp.sum(jnp.where(diagonal, row, 0), axis=-1, keepdims=True)
        pick = jnp.where(patch == column, 1.0, 0.0)
        pick_ref[owner * caps : (owner + 1) * caps, :] = pick.astype(jnp.bfloat16)


def project_kernel(
    slots_ref,
    tokens_ref,
    gain_ref,
    key_weight_ref,
    value_weight_ref,
    out_ref,
    even_ref,
    odd_ref,
    pick_ref,
    weight_ref,
):
    step = pl.program_id(0)
    patches = tokens_ref.shape[1]
    local = key_weight_ref.shape[1]

    @pl.when(step == 0)
    def _():
        build_pick(slots_ref, pick_ref)
        weight_ref[:, :local] = key_weight_ref[...]
        weight_ref[:, local:] = value_weight_ref[...]

    def stage(write_ref, read_ref):
        gain = gain_ref[...]
        half, quarter = patches // 2, patches // 4

        def normalize(index):
            for start in range(index * quarter, (index + 1) * quarter, ROWS):
                part = pl.ds(start, ROWS)
                write_ref[part, :] = normalize_rows(tokens_ref[0, part, :], gain)

        products = []
        for index in range(2):
            part = pl.ds(index * half, half)
            product = jnp.dot(read_ref[part, :], weight_ref[...], preferred_element_type=jnp.float32)
            products.append(product.astype(jnp.bfloat16))
            normalize(index)
        product = jnp.concatenate(products, axis=0)
        half, blocks = pick_ref.shape[0] // 2, out_ref.shape[0] // 2
        for index in range(2):
            part = pl.ds(index * half, half)
            picked = jnp.dot(pick_ref[part, :], product, preferred_element_type=jnp.float32)
            out_ref[index * blocks : (index + 1) * blocks, 0] = (
                picked.astype(jnp.bfloat16).reshape(blocks, BLOCK, out_ref.shape[-1])
            )
            normalize(2 + index)

    @pl.when(step % 2 == 0)
    def _():
        stage(even_ref, odd_ref)

    @pl.when(step % 2 == 1)
    def _():
        stage(odd_ref, even_ref)


def project(slots, tokens, gain, key_weight, value_weight):
    levels, patches, width = tokens.shape
    local = key_weight.shape[1]
    count = slots.size
    whole = lambda i: (0, 0)
    return pl.pallas_call(
        project_kernel,
        grid=(levels + 1,),
        in_specs=[
            pl.BlockSpec(slots.shape, whole),
            pl.BlockSpec((1, patches, width), lambda i: (jnp.minimum(i, levels - 1), 0, 0)),
            pl.BlockSpec((1, width), whole),
            pl.BlockSpec((width, local), whole),
            pl.BlockSpec((width, local), whole),
        ],
        out_specs=pl.BlockSpec((count // BLOCK, 1, BLOCK, 2 * local), lambda i: (0, jnp.maximum(i - 1, 0), 0, 0)),
        out_shape=jax.ShapeDtypeStruct((count // BLOCK, levels, BLOCK, 2 * local), jnp.bfloat16),
        scratch_shapes=[
            pltpu.VMEM((patches, width), jnp.bfloat16),
            pltpu.VMEM((patches, width), jnp.bfloat16),
            pltpu.VMEM((count, patches), jnp.bfloat16),
            pltpu.VMEM((width, 2 * local), jnp.bfloat16),
        ],
        compiler_params=params(58),
        cost_estimate=pl.CostEstimate(
            flops=8 * levels * patches * (width + count) * local,
            bytes_accessed=2 * levels * patches * (width + 2 * local) + 4 * width * local,
            transcendentals=0,
        ),
        name="norm_project",
    )(slots, tokens, gain.reshape(1, width), key_weight, value_weight)


def attend_kernel(query_ref, pair_ref, *out_refs):
    levels, slots, local = pair_ref.shape[1:]
    local = local // 2
    latents = query_ref.shape[1]
    rows = GROUP * latents
    columns = levels * GROUP
    heads = LANES // HEAD_DIM
    half = slots // len(out_refs)
    lane_head = lax.broadcasted_iota(jnp.int32, (rows, LANES), 1) // HEAD_DIM
    row_slot = lax.broadcasted_iota(jnp.int32, (GROUP, heads * rows), 0)
    column_slot = (lax.broadcasted_iota(jnp.int32, (GROUP, heads * rows), 1) // latents) & (GROUP - 1)
    same = row_slot - column_slot == 0
    scale = math.log2(math.e) / math.sqrt(HEAD_DIM)
    queries = query_ref[...].reshape(slots * latents, local).astype(jnp.float32)

    tasks = [(start, lane) for start in range(0, slots, GROUP) for lane in range(0, local, LANES)]
    scores = []
    for start, lane in tasks:
        part = queries[start * latents : start * latents + rows, lane : lane + LANES]
        part = jnp.concatenate(
            [jnp.where(lane_head == head, part, 0.0).astype(jnp.bfloat16) for head in range(heads)], axis=0
        )
        keys = pair_ref[0, :, pl.ds(start, GROUP), pl.ds(lane, LANES)].reshape(columns, LANES)
        product = lax.dot_general(keys, part, (((1,), (1,)), ((), ())), preferred_element_type=jnp.float32)
        scores.append(product.reshape(levels, GROUP, heads * rows))
    softs = []
    for product in scores:
        expo = jnp.exp2((product - jnp.max(product, axis=0, keepdims=True)) * scale)
        inverse = jnp.where(same, 1.0 / jnp.sum(expo, axis=0), 0.0)
        softs.append((expo * inverse[None]).reshape(columns, heads * rows).astype(jnp.bfloat16))
    for (start, lane), soft in zip(tasks, softs):
        values = pair_ref[0, :, pl.ds(start, GROUP), pl.ds(local + lane, LANES)].reshape(columns, LANES)
        wide = lax.dot_general(soft, values, (((0,), (0,)), ((), ())), preferred_element_type=jnp.float32)
        mixed = wide[:rows]
        for head in range(1, heads):
            mixed = jnp.where(lane_head == head, wide[head * rows : (head + 1) * rows], mixed)
        part = pl.ds(start % half * latents, rows)
        out_refs[start // half][part, pl.ds(lane, LANES)] = mixed.astype(jnp.bfloat16)


def attend(queries, pairs, halves):
    slots, latents, local = queries.shape
    levels = pairs.shape[1]
    rows = BLOCK * latents // halves
    steps = slots // BLOCK
    return pl.pallas_call(
        attend_kernel,
        grid=(steps,),
        in_specs=[
            pl.BlockSpec((BLOCK, latents, local), lambda i: (i, 0, 0)),
            pl.BlockSpec((1, levels, BLOCK, 2 * local), lambda i: (i, 0, 0, 0)),
        ],
        out_specs=[pl.BlockSpec((rows, local), lambda i: (i, 0))] * halves,
        out_shape=[jax.ShapeDtypeStruct((steps * rows, local), jnp.bfloat16)] * halves,
        compiler_params=params(58),
        cost_estimate=pl.CostEstimate(
            flops=64 * slots * latents * levels * GROUP * local,
            bytes_accessed=4 * slots * (latents + levels) * local,
            transcendentals=0,
        ),
        name="attend_slots",
    )(queries, pairs)


def combine_rows(mixed_refs, weight_refs, part):
    total = None
    for mixed_ref, weight_ref in zip(mixed_refs, weight_refs):
        term = jnp.dot(mixed_ref[part, :], weight_ref[...], preferred_element_type=jnp.float32)
        term = term.astype(jnp.bfloat16).astype(jnp.float32)
        total = term if total is None else total + term
    return total.astype(jnp.bfloat16)


def combine_kernel(*refs):
    out_ref = refs[-1]
    stripes, caps, latents, local = out_ref.shape
    rest = refs[8:-1]
    half = caps - sum(ref.shape[1] for ref in rest)
    for stripe in range(stripes):
        part = pl.ds(stripe * half * latents, half * latents)
        rows = combine_rows(refs[:4], refs[4:8], part)
        out_ref[stripe, :half] = rows.reshape(half, latents, local)
        for ref in rest:
            out_ref[stripe, half:] = ref[stripe]


def combine(groups, weights, shape, rest=()):
    operands = (*groups, *weights, *rest)
    rows, local = groups[0].shape
    vmem = pl.BlockSpec(memory_space=pltpu.VMEM)
    return pl.pallas_call(
        combine_kernel,
        in_specs=[vmem] * len(operands),
        out_specs=vmem,
        out_shape=jax.ShapeDtypeStruct(shape, jnp.bfloat16),
        compiler_params=params(20),
        cost_estimate=pl.CostEstimate(
            flops=24 * rows * local * local, bytes_accessed=10 * rows * local, transcendentals=0
        ),
        name="combine_groups",
    )(*operands)


def swap(array, axis_name, distance):
    size = lax.axis_size(axis_name)
    return lax.ppermute(array, axis_name, [(i, i ^ distance) for i in range(size)])


def spread_heads(mixed):
    second = swap(mixed, "head", 2)
    return mixed, swap(mixed, "head", 1), second, swap(second, "head", 1)


def exchange(array, stripes):
    array = array.reshape(stripes, -1, *array.shape[1:])
    return lax.all_to_all(array, "lat", split_axis=0, concat_axis=0, tiled=True)


def spread_weight(out_weight, head):
    local = out_weight.shape[0]
    parts = []
    for distance in range(lax.axis_size("head")):
        start = jnp.bitwise_xor(head, distance) * local
        part = lax.dynamic_slice_in_dim(out_weight, start, local, 1)
        parts.append(swap(part, "head", distance) if distance else part)
    return parts


def shards(level_tokens, ln_gain, key_weight, value_weight, out_weight, ocean_queries, send_slots):
    stripes = lax.axis_size("lat")
    caps = send_slots.shape[2]
    shape = ocean_queries.shape
    slots, latents, local = shape
    queries = exchange(ocean_queries, stripes).reshape(shape)
    weights = spread_weight(out_weight, lax.axis_index("head"))
    tokens = jnp.transpose(level_tokens, (1, 0, 2))
    pairs = project(send_slots[0], tokens, ln_gain, key_weight, value_weight)
    pairs, weights = lax.optimization_barrier((pairs, weights))
    if caps != BLOCK:
        (mixed,) = attend(queries, pairs, 1)
        mixed = exchange(mixed, stripes).reshape(-1, local)
        return combine(spread_heads(mixed), weights, (stripes, caps, latents, local)).reshape(shape)
    early, late = attend(queries, pairs, 2)
    late = combine(spread_heads(late), weights, (stripes, caps // 2, latents, local))
    late = exchange(late.reshape(-1, latents, local), stripes)
    early = exchange(early, stripes).reshape(-1, local)
    return combine(spread_heads(early), weights, (stripes, caps, latents, local), (late,)).reshape(shape)


def solution(mesh):
    return jax.shard_map(
        shards,
        mesh=mesh,
        in_specs=(
            P("lat", None, None),
            P(),
            P(None, "head"),
            P(None, "head"),
            P("head", None),
            P("lat", None, "head"),
            P("lat", None, None),
        ),
        out_specs=P("lat", None, "head"),
        check_vma=False,
    )
```

```python
import functools
import math

import jax
import jax.numpy as jnp
from jax import lax
from jax.experimental import pallas as pl
from jax.experimental.pallas import tpu as pltpu
from jax.sharding import PartitionSpec as P

HEAD_DIM = 64
EPS = 1e-05
GROUP = 16
BLOCK = 64
ROWS = 32
LANES = 128
MIB = 1024 * 1024


def params(mib):
    return pltpu.CompilerParams(vmem_limit_bytes=mib * MIB)


def normalize_rows(tokens, gain):
    width = tokens.shape[-1]
    tokens = tokens.astype(jnp.float32)
    center = jnp.sum(tokens, axis=-1, keepdims=True) * (1.0 / width)
    shifted = tokens - center
    spread = jnp.sum(shifted * shifted, axis=-1, keepdims=True) * (1.0 / width)
    return (shifted * lax.rsqrt(spread + EPS) * gain).astype(jnp.bfloat16)


def build_pick(slots_ref, pick_ref, halves):
    stripes, caps = slots_ref.shape
    half = caps // halves
    diagonal = lax.broadcasted_iota(jnp.int32, (caps, caps), 0) == lax.broadcasted_iota(jnp.int32, (caps, caps), 1)
    patch = lax.broadcasted_iota(jnp.int32, (caps, pick_ref.shape[1]), 1)
    for owner in range(stripes):
        row = jnp.broadcast_to(slots_ref[owner : owner + 1, :], (caps, caps))
        column = jnp.sum(jnp.where(diagonal, row, 0), axis=-1, keepdims=True)
        pick = jnp.where(patch == column, 1.0, 0.0).astype(jnp.bfloat16)
        for index in range(halves):
            start = (index * stripes + owner) * half
            pick_ref[start : start + half, :] = pick[index * half : (index + 1) * half]


def project_kernel(
    halves,
    slots_ref,
    tokens_ref,
    gain_ref,
    key_weight_ref,
    value_weight_ref,
    out_ref,
    even_ref,
    odd_ref,
    pick_ref,
    weight_ref,
):
    step = pl.program_id(0)
    patches = tokens_ref.shape[1]
    local = key_weight_ref.shape[1]

    @pl.when(step == 0)
    def _():
        build_pick(slots_ref, pick_ref, halves)
        weight_ref[:, :local] = key_weight_ref[...]
        weight_ref[:, local:] = value_weight_ref[...]

    def stage(write_ref, read_ref):
        gain = gain_ref[...]
        product = jnp.dot(read_ref[...], weight_ref[...], preferred_element_type=jnp.float32).astype(jnp.bfloat16)
        picked = jnp.dot(pick_ref[...], product, preferred_element_type=jnp.float32).astype(jnp.bfloat16)
        out_ref[:, 0] = picked.reshape(out_ref.shape[0], BLOCK, out_ref.shape[-1])
        for start in range(0, patches, ROWS):
            part = pl.ds(start, ROWS)
            write_ref[part, :] = normalize_rows(tokens_ref[0, part, :], gain)

    @pl.when(step % 2 == 0)
    def _():
        stage(even_ref, odd_ref)

    @pl.when(step % 2 == 1)
    def _():
        stage(odd_ref, even_ref)


def project(slots, tokens, gain, key_weight, value_weight, halves):
    levels, patches, width = tokens.shape
    local = key_weight.shape[1]
    count = slots.size
    whole = lambda i: (0, 0)
    return pl.pallas_call(
        functools.partial(project_kernel, halves),
        grid=(levels + 1,),
        in_specs=[
            pl.BlockSpec(slots.shape, whole),
            pl.BlockSpec((1, patches, width), lambda i: (jnp.minimum(i, levels - 1), 0, 0)),
            pl.BlockSpec((1, width), whole),
            pl.BlockSpec((width, local), whole),
            pl.BlockSpec((width, local), whole),
        ],
        out_specs=pl.BlockSpec((count // BLOCK, 1, BLOCK, 2 * local), lambda i: (0, jnp.maximum(i - 1, 0), 0, 0)),
        out_shape=jax.ShapeDtypeStruct((count // BLOCK, levels, BLOCK, 2 * local), jnp.bfloat16),
        scratch_shapes=[
            pltpu.VMEM((patches, width), jnp.bfloat16),
            pltpu.VMEM((patches, width), jnp.bfloat16),
            pltpu.VMEM((count, patches), jnp.bfloat16),
            pltpu.VMEM((width, 2 * local), jnp.bfloat16),
        ],
        compiler_params=params(58),
        cost_estimate=pl.CostEstimate(
            flops=8 * levels * patches * (width + count) * local,
            bytes_accessed=2 * levels * patches * (width + 2 * local) + 4 * width * local,
            transcendentals=0,
        ),
        name="norm_project",
    )(slots, tokens, gain.reshape(1, width), key_weight, value_weight)


def attend_kernel(query_ref, pair_ref, *refs):
    out_ref = refs[-1]
    levels, slots, local = pair_ref.shape[1:]
    local = local // 2
    latents = out_ref.shape[0] // slots
    rows = GROUP * latents
    columns = levels * GROUP
    heads = LANES // HEAD_DIM
    lane_head = lax.broadcasted_iota(jnp.int32, (rows, LANES), 1) // HEAD_DIM
    row_slot = lax.broadcasted_iota(jnp.int32, (GROUP, heads * rows), 0)
    column_slot = (lax.broadcasted_iota(jnp.int32, (GROUP, heads * rows), 1) // latents) & (GROUP - 1)
    same = row_slot - column_slot == 0
    scale = math.log2(math.e) / math.sqrt(HEAD_DIM)
    queries = query_ref[...].reshape(slots * latents, local).astype(jnp.float32)

    tasks = [(start, lane) for start in range(0, slots, GROUP) for lane in range(0, local, LANES)]
    scores = []
    for start, lane in tasks:
        part = queries[start * latents : start * latents + rows, lane : lane + LANES]
        part = jnp.concatenate(
            [jnp.where(lane_head == head, part, 0.0).astype(jnp.bfloat16) for head in range(heads)], axis=0
        )
        keys = pair_ref[0, :, pl.ds(start, GROUP), pl.ds(lane, LANES)].reshape(columns, LANES)
        product = lax.dot_general(keys, part, (((1,), (1,)), ((), ())), preferred_element_type=jnp.float32)
        scores.append(product.reshape(levels, GROUP, heads * rows))
    softs = []
    for product in scores:
        expo = jnp.exp2((product - jnp.max(product, axis=0, keepdims=True)) * scale)
        inverse = jnp.where(same, 1.0 / jnp.sum(expo, axis=0), 0.0)
        softs.append((expo * inverse[None]).reshape(columns, heads * rows).astype(jnp.bfloat16))
    for (start, lane), soft in zip(tasks, softs):
        values = pair_ref[0, :, pl.ds(start, GROUP), pl.ds(local + lane, LANES)].reshape(columns, LANES)
        wide = lax.dot_general(soft, values, (((0,), (0,)), ((), ())), preferred_element_type=jnp.float32)
        mixed = wide[:rows]
        for head in range(1, heads):
            mixed = jnp.where(lane_head == head, wide[head * rows : (head + 1) * rows], mixed)
        out_ref[pl.ds(start * latents, rows), pl.ds(lane, LANES)] = mixed.astype(jnp.bfloat16)


def attend(queries, pairs, index, after=()):
    stripes, halves, rows, local = queries.shape
    levels = pairs.shape[1]
    steps = pairs.shape[0] // halves
    block = stripes * rows // steps
    return pl.pallas_call(
        attend_kernel,
        grid=(steps,),
        in_specs=[
            pl.BlockSpec((stripes // steps, 1, rows, local), lambda i: (i, index, 0, 0)),
            pl.BlockSpec((1, levels, BLOCK, 2 * local), lambda i: (index * steps + i, 0, 0, 0)),
        ]
        + [pl.BlockSpec(memory_space=pl.ANY)] * len(after),
        out_specs=pl.BlockSpec((block, local), lambda i: (i, 0)),
        out_shape=jax.ShapeDtypeStruct((steps * block, local), jnp.bfloat16),
        compiler_params=params(55),
        cost_estimate=pl.CostEstimate(
            flops=64 * steps * block * levels * GROUP * local,
            bytes_accessed=4 * steps * (block + levels * BLOCK) * local,
            transcendentals=0,
        ),
        name="attend_slots",
    )(queries, pairs, *after)


def combine_rows(mixed_refs, weight_refs, part):
    total = None
    for mixed_ref, weight_ref in zip(mixed_refs, weight_refs):
        term = jnp.dot(mixed_ref[part, :], weight_ref[...], preferred_element_type=jnp.float32)
        term = term.astype(jnp.bfloat16).astype(jnp.float32)
        total = term if total is None else total + term
    return total.astype(jnp.bfloat16)


def combine_kernel(*refs):
    out_ref = refs[-1]
    stripes, caps, latents, local = out_ref.shape
    rest = refs[8:-1]
    half = caps - sum(ref.shape[1] for ref in rest)
    for stripe in range(stripes):
        part = pl.ds(stripe * half * latents, half * latents)
        rows = combine_rows(refs[:4], refs[4:8], part)
        out_ref[stripe, :half] = rows.reshape(half, latents, local)
        for ref in rest:
            out_ref[stripe, half:] = ref[stripe]


def combine(groups, weights, shape, rest=()):
    operands = (*groups, *weights, *rest)
    rows, local = groups[0].shape
    vmem = pl.BlockSpec(memory_space=pltpu.VMEM)
    return pl.pallas_call(
        combine_kernel,
        in_specs=[vmem] * len(operands),
        out_specs=vmem,
        out_shape=jax.ShapeDtypeStruct(shape, jnp.bfloat16),
        compiler_params=params(20),
        cost_estimate=pl.CostEstimate(
            flops=24 * rows * local * local, bytes_accessed=10 * rows * local, transcendentals=0
        ),
        name="combine_groups",
    )(*operands)


def swap(array, axis_name, distance):
    size = lax.axis_size(axis_name)
    return lax.ppermute(array, axis_name, [(i, i ^ distance) for i in range(size)])


def follow(array, *others):
    return lax.optimization_barrier((array, *others))[0]


def spread_heads(mixed):
    second = swap(mixed, "head", 2)
    return mixed, swap(mixed, "head", 1), second, swap(second, "head", 1)


def exchange(array, stripes):
    array = array.reshape(stripes, -1, *array.shape[1:])
    return lax.all_to_all(array, "lat", split_axis=0, concat_axis=0, tiled=True)


def spread_weight(out_weight, head):
    local = out_weight.shape[0]
    parts = []
    for distance in range(lax.axis_size("head")):
        start = jnp.bitwise_xor(head, distance) * local
        part = lax.dynamic_slice_in_dim(out_weight, start, local, 1)
        parts.append(swap(part, "head", distance) if distance else part)
    return parts


def shards(level_tokens, ln_gain, key_weight, value_weight, out_weight, ocean_queries, send_slots):
    stripes = lax.axis_size("lat")
    caps = send_slots.shape[2]
    shape = ocean_queries.shape
    slots, latents, local = shape
    halves = 2 if caps == BLOCK else 1
    queries = exchange(ocean_queries, stripes).reshape(stripes, halves, -1, local)
    weights = spread_weight(out_weight, lax.axis_index("head"))
    tokens = jnp.transpose(level_tokens, (1, 0, 2))
    pairs = project(send_slots[0], tokens, ln_gain, key_weight, value_weight, halves)
    pairs, weights = lax.optimization_barrier((pairs, weights))
    if halves == 1:
        mixed = exchange(attend(queries, pairs, 0), stripes).reshape(-1, local)
        return combine(spread_heads(mixed), weights, (stripes, caps, latents, local)).reshape(shape)
    late = attend(queries, pairs, 1)
    early = attend(queries, pairs, 0, (late,))
    late = combine(spread_heads(late), weights, (stripes, caps // 2, latents, local))
    early = follow(exchange(early, stripes), late).reshape(-1, local)
    late = exchange(late.reshape(-1, latents, local), stripes)
    return combine(spread_heads(early), weights, (stripes, caps, latents, local), (late,)).reshape(shape)


def solution(mesh):
    return jax.shard_map(
        shards,
        mesh=mesh,
        in_specs=(
            P("lat", None, None),
            P(),
            P(None, "head"),
            P(None, "head"),
            P("head", None),
            P("lat", None, "head"),
            P("lat", None, None),
        ),
        out_specs=P("lat", None, "head"),
        check_vma=False,
    )
```

```python
import functools
import math

import jax
import jax.numpy as jnp
from jax import lax
from jax.experimental import pallas as pl
from jax.experimental.pallas import tpu as pltpu
from jax.sharding import PartitionSpec as P

HEAD_DIM = 64
EPS = 1e-05
GROUP = 16
BLOCK = 64
ROWS = 32
LANES = 128
MIB = 1024 * 1024


def params(mib):
    return pltpu.CompilerParams(vmem_limit_bytes=mib * MIB)


def normalize_rows(tokens, gain):
    width = tokens.shape[-1]
    tokens = tokens.astype(jnp.float32)
    center = jnp.sum(tokens, axis=-1, keepdims=True) * (1.0 / width)
    shifted = tokens - center
    spread = jnp.sum(shifted * shifted, axis=-1, keepdims=True) * (1.0 / width)
    return (shifted * lax.rsqrt(spread + EPS) * gain).astype(jnp.bfloat16)


def build_pick(slots_ref, pick_ref, halves):
    stripes, caps = slots_ref.shape
    half = caps // halves
    diagonal = lax.broadcasted_iota(jnp.int32, (caps, caps), 0) == lax.broadcasted_iota(jnp.int32, (caps, caps), 1)
    patch = lax.broadcasted_iota(jnp.int32, (caps, pick_ref.shape[1]), 1)
    for owner in range(stripes):
        row = jnp.broadcast_to(slots_ref[owner : owner + 1, :], (caps, caps))
        column = jnp.sum(jnp.where(diagonal, row, 0), axis=-1, keepdims=True)
        pick = jnp.where(patch == column, 1.0, 0.0).astype(jnp.bfloat16)
        for index in range(halves):
            start = (index * stripes + owner) * half
            pick_ref[start : start + half, :] = pick[index * half : (index + 1) * half]


def project_kernel(
    halves,
    slots_ref,
    tokens_ref,
    gain_ref,
    key_weight_ref,
    value_weight_ref,
    out_ref,
    even_ref,
    odd_ref,
    pick_ref,
    weight_ref,
):
    step = pl.program_id(0)
    patches = tokens_ref.shape[1]
    local = key_weight_ref.shape[1]

    @pl.when(step == 0)
    def _():
        build_pick(slots_ref, pick_ref, halves)
        weight_ref[:, :local] = key_weight_ref[...]
        weight_ref[:, local:] = value_weight_ref[...]

    def stage(write_ref, read_ref):
        gain = gain_ref[...]
        product = jnp.dot(read_ref[...], weight_ref[...], preferred_element_type=jnp.float32).astype(jnp.bfloat16)
        picked = jnp.dot(pick_ref[...], product, preferred_element_type=jnp.float32).astype(jnp.bfloat16)
        out_ref[:, 0] = picked.reshape(out_ref.shape[0], BLOCK, out_ref.shape[-1])
        for start in range(0, patches, ROWS):
            part = pl.ds(start, ROWS)
            write_ref[part, :] = normalize_rows(tokens_ref[0, part, :], gain)

    @pl.when(step % 2 == 0)
    def _():
        stage(even_ref, odd_ref)

    @pl.when(step % 2 == 1)
    def _():
        stage(odd_ref, even_ref)


def project(slots, tokens, gain, key_weight, value_weight, halves):
    levels, patches, width = tokens.shape
    local = key_weight.shape[1]
    count = slots.size
    whole = lambda i: (0, 0)
    return pl.pallas_call(
        functools.partial(project_kernel, halves),
        grid=(levels + 1,),
        in_specs=[
            pl.BlockSpec(slots.shape, whole),
            pl.BlockSpec((1, patches, width), lambda i: (jnp.minimum(i, levels - 1), 0, 0)),
            pl.BlockSpec((1, width), whole),
            pl.BlockSpec((width, local), whole),
            pl.BlockSpec((width, local), whole),
        ],
        out_specs=pl.BlockSpec((count // BLOCK, 1, BLOCK, 2 * local), lambda i: (0, jnp.maximum(i - 1, 0), 0, 0)),
        out_shape=jax.ShapeDtypeStruct((count // BLOCK, levels, BLOCK, 2 * local), jnp.bfloat16),
        scratch_shapes=[
            pltpu.VMEM((patches, width), jnp.bfloat16),
            pltpu.VMEM((patches, width), jnp.bfloat16),
            pltpu.VMEM((count, patches), jnp.bfloat16),
            pltpu.VMEM((width, 2 * local), jnp.bfloat16),
        ],
        compiler_params=params(58),
        cost_estimate=pl.CostEstimate(
            flops=8 * levels * patches * (width + count) * local,
            bytes_accessed=2 * levels * patches * (width + 2 * local) + 4 * width * local,
            transcendentals=0,
        ),
        name="norm_project",
    )(slots, tokens, gain.reshape(1, width), key_weight, value_weight)


def attend_kernel(query_ref, pair_ref, *refs):
    out_ref = refs[-1]
    levels, slots, local = pair_ref.shape[1:]
    local = local // 2
    latents = out_ref.shape[0] // slots
    rows = GROUP * latents
    columns = levels * GROUP
    heads = local // HEAD_DIM
    lane_head = lax.broadcasted_iota(jnp.int32, (rows, local), 1) // HEAD_DIM
    row_slot = lax.broadcasted_iota(jnp.int32, (GROUP, heads * rows), 0)
    column_slot = (lax.broadcasted_iota(jnp.int32, (GROUP, heads * rows), 1) // latents) & (GROUP - 1)
    same = row_slot - column_slot == 0
    scale = math.log2(math.e) / math.sqrt(HEAD_DIM)
    queries = query_ref[...].reshape(slots * latents, local).astype(jnp.float32)

    def score(start):
        part = queries[start * latents : start * latents + rows]
        part = jnp.concatenate(
            [jnp.where(lane_head == head, part, 0.0).astype(jnp.bfloat16) for head in range(heads)], axis=0
        )
        keys = pair_ref[0, :, pl.ds(start, GROUP), :local].reshape(columns, local)
        product = lax.dot_general(keys, part, (((1,), (1,)), ((), ())), preferred_element_type=jnp.float32)
        return product.reshape(levels, GROUP, heads * rows)

    def soften(product):
        expo = jnp.exp2((product - jnp.max(product, axis=0, keepdims=True)) * scale)
        inverse = jnp.where(same, 1.0 / jnp.sum(expo, axis=0), 0.0)
        return (expo * inverse[None]).reshape(columns, heads * rows).astype(jnp.bfloat16)

    def mix(start, soft):
        values = pair_ref[0, :, pl.ds(start, GROUP), local:].reshape(columns, local)
        wide = lax.dot_general(soft, values, (((0,), (0,)), ((), ())), preferred_element_type=jnp.float32)
        mixed = wide[:rows]
        for head in range(1, heads):
            mixed = jnp.where(lane_head == head, wide[head * rows : (head + 1) * rows], mixed)
        out_ref[pl.ds(start * latents, rows), :] = mixed.astype(jnp.bfloat16)

    starts = range(0, slots, GROUP)
    scores, softs = {}, {}
    for index in range(len(starts) + 2):
        if index < len(starts):
            scores[index] = score(starts[index])
        if 0 <= index - 1 < len(starts):
            softs[index - 1] = soften(scores.pop(index - 1))
        if 0 <= index - 2:
            mix(starts[index - 2], softs.pop(index - 2))


def attend(queries, pairs, index, after=()):
    stripes, halves, half, latents, local = queries.shape
    levels = pairs.shape[1]
    steps = pairs.shape[0] // halves
    block = stripes * half * latents // steps
    return pl.pallas_call(
        attend_kernel,
        grid=(steps,),
        in_specs=[
            pl.BlockSpec((stripes // steps, 1, half, latents, local), lambda i: (i, index, 0, 0, 0)),
            pl.BlockSpec((1, levels, BLOCK, 2 * local), lambda i: (index * steps + i, 0, 0, 0)),
        ]
        + [pl.BlockSpec(memory_space=pl.ANY)] * len(after),
        out_specs=pl.BlockSpec((block, local), lambda i: (i, 0)),
        out_shape=jax.ShapeDtypeStruct((steps * block, local), jnp.bfloat16),
        compiler_params=params(55),
        cost_estimate=pl.CostEstimate(
            flops=64 * steps * block * levels * GROUP * local,
            bytes_accessed=4 * steps * (block + levels * BLOCK) * local,
            transcendentals=0,
        ),
        name="attend_slots",
    )(queries, pairs, *after)


def combine_rows(mixed_refs, weight_refs, part):
    total = None
    for mixed_ref, weight_ref in zip(mixed_refs, weight_refs):
        term = jnp.dot(mixed_ref[part, :], weight_ref[...], preferred_element_type=jnp.float32)
        term = term.astype(jnp.bfloat16).astype(jnp.float32)
        total = term if total is None else total + term
    return total.astype(jnp.bfloat16)


def combine_kernel(*refs):
    out_ref = refs[-1]
    stripes, caps, latents, local = out_ref.shape
    rest = refs[8:-1]
    half = caps - sum(ref.shape[1] for ref in rest)
    for stripe in range(stripes):
        part = pl.ds(stripe * half * latents, half * latents)
        rows = combine_rows(refs[:4], refs[4:8], part)
        out_ref[stripe, :half] = rows.reshape(half, latents, local)
        for ref in rest:
            out_ref[stripe, half:] = ref[stripe]


def combine(groups, weights, shape, rest=()):
    operands = (*groups, *weights, *rest)
    rows, local = groups[0].shape
    vmem = pl.BlockSpec(memory_space=pltpu.VMEM)
    return pl.pallas_call(
        combine_kernel,
        in_specs=[vmem] * len(operands),
        out_specs=vmem,
        out_shape=jax.ShapeDtypeStruct(shape, jnp.bfloat16),
        compiler_params=params(20),
        cost_estimate=pl.CostEstimate(
            flops=24 * rows * local * local, bytes_accessed=10 * rows * local, transcendentals=0
        ),
        name="combine_groups",
    )(*operands)


def swap(array, axis_name, distance):
    size = lax.axis_size(axis_name)
    return lax.ppermute(array, axis_name, [(i, i ^ distance) for i in range(size)])


def follow(array, *others):
    return lax.optimization_barrier((array, *others))[0]


def spread_heads(mixed):
    second = swap(mixed, "head", 2)
    return mixed, swap(mixed, "head", 1), second, swap(second, "head", 1)


def exchange(array, stripes):
    array = array.reshape(stripes, -1, *array.shape[1:])
    return lax.all_to_all(array, "lat", split_axis=0, concat_axis=0, tiled=True)


def spread_weight(out_weight, head):
    local = out_weight.shape[0]
    parts = []
    for distance in range(lax.axis_size("head")):
        start = jnp.bitwise_xor(head, distance) * local
        part = lax.dynamic_slice_in_dim(out_weight, start, local, 1)
        parts.append(swap(part, "head", distance) if distance else part)
    return parts


def shards(level_tokens, ln_gain, key_weight, value_weight, out_weight, ocean_queries, send_slots):
    stripes = lax.axis_size("lat")
    caps = send_slots.shape[2]
    shape = ocean_queries.shape
    slots, latents, local = shape
    halves = 2 if caps == BLOCK else 1
    queries = exchange(ocean_queries, stripes).reshape(stripes, halves, -1, latents, local)
    weights = spread_weight(out_weight, lax.axis_index("head"))
    tokens = jnp.transpose(level_tokens, (1, 0, 2))
    pairs = project(send_slots[0], tokens, ln_gain, key_weight, value_weight, halves)
    pairs, weights = lax.optimization_barrier((pairs, weights))
    if halves == 1:
        mixed = exchange(attend(queries, pairs, 0), stripes).reshape(-1, local)
        return combine(spread_heads(mixed), weights, (stripes, caps, latents, local)).reshape(shape)
    late = attend(queries, pairs, 1)
    early = attend(queries, pairs, 0, (late,))
    late = combine(spread_heads(late), weights, (stripes, caps // 2, latents, local))
    early = follow(exchange(early, stripes), late).reshape(-1, local)
    late = exchange(late.reshape(-1, latents, local), stripes)
    return combine(spread_heads(early), weights, (stripes, caps, latents, local), (late,)).reshape(shape)


def solution(mesh):
    return jax.shard_map(
        shards,
        mesh=mesh,
        in_specs=(
            P("lat", None, None),
            P(),
            P(None, "head"),
            P(None, "head"),
            P("head", None),
            P("lat", None, "head"),
            P("lat", None, None),
        ),
        out_specs=P("lat", None, "head"),
        check_vma=False,
    )
```

```python
import functools
import math

import jax
import jax.numpy as jnp
from jax import lax
from jax.experimental import pallas as pl
from jax.experimental.pallas import tpu as pltpu
from jax.sharding import PartitionSpec as P

HEAD_DIM = 64
EPS = 1e-05
GROUP = 16
BLOCK = 64
ROWS = 32
COPIES = 4
LANES = 128
MIB = 1024 * 1024


def params(mib):
    return pltpu.CompilerParams(vmem_limit_bytes=mib * MIB)


def normalize_rows(tokens, gain):
    width = tokens.shape[-1]
    tokens = tokens.astype(jnp.float32)
    center = jnp.sum(tokens, axis=-1, keepdims=True) * (1.0 / width)
    shifted = tokens - center
    spread = jnp.sum(shifted * shifted, axis=-1, keepdims=True) * (1.0 / width)
    return (shifted * lax.rsqrt(spread + EPS) * gain).astype(jnp.bfloat16)


def build_pick(slots_ref, pick_ref, halves):
    stripes, caps = slots_ref.shape
    half = caps // halves
    diagonal = lax.broadcasted_iota(jnp.int32, (caps, caps), 0) == lax.broadcasted_iota(jnp.int32, (caps, caps), 1)
    patch = lax.broadcasted_iota(jnp.int32, (caps, pick_ref.shape[1]), 1)
    for owner in range(stripes):
        row = jnp.broadcast_to(slots_ref[owner : owner + 1, :], (caps, caps))
        column = jnp.sum(jnp.where(diagonal, row, 0), axis=-1, keepdims=True)
        pick = jnp.where(patch == column, 1.0, 0.0).astype(jnp.bfloat16)
        for index in range(halves):
            start = (index * stripes + owner) * half
            pick_ref[start : start + half, :] = pick[index * half : (index + 1) * half]


def project_kernel(
    halves,
    slots_ref,
    gain_ref,
    key_weight_ref,
    value_weight_ref,
    *refs,
):
    tokens_refs, out_refs = refs[:COPIES], refs[COPIES : COPIES + halves]
    even_ref, odd_ref, pick_ref, weight_ref = refs[COPIES + halves :]
    step = pl.program_id(0)
    local = key_weight_ref.shape[1]

    @pl.when(step == 0)
    def _():
        build_pick(slots_ref, pick_ref, halves)
        weight_ref[:, :local] = key_weight_ref[...]
        weight_ref[:, local:] = value_weight_ref[...]

    def stage(write_ref, read_ref):
        gain = gain_ref[...]
        product = jnp.dot(read_ref[...], weight_ref[...], preferred_element_type=jnp.float32).astype(jnp.bfloat16)
        picked = jnp.dot(pick_ref[...], product, preferred_element_type=jnp.float32).astype(jnp.bfloat16)
        half = picked.shape[0] // halves
        for index, out_ref in enumerate(out_refs):
            out_ref[:, 0] = picked[index * half : (index + 1) * half].reshape(half // BLOCK, BLOCK, 2 * local)
        for index, tokens_ref in enumerate(tokens_refs):
            size = tokens_ref.shape[1]
            for start in range(0, size, ROWS):
                normed = normalize_rows(tokens_ref[0, pl.ds(start, ROWS), :], gain)
                write_ref[pl.ds(index * size + start, ROWS), :] = normed

    @pl.when(step % 2 == 0)
    def _():
        stage(even_ref, odd_ref)

    @pl.when(step % 2 == 1)
    def _():
        stage(odd_ref, even_ref)


def project(slots, tokens, gain, key_weight, value_weight, halves):
    levels, patches, width = tokens.shape
    local = key_weight.shape[1]
    count = slots.size
    whole = lambda i: (0, 0)
    blocks = count // BLOCK // halves

    def tokens_spec(index):
        return pl.BlockSpec((1, patches // COPIES, width), lambda i: (jnp.minimum(i, levels - 1), index, 0))

    return pl.pallas_call(
        functools.partial(project_kernel, halves),
        grid=(levels + 1,),
        in_specs=[
            pl.BlockSpec(slots.shape, whole),
            pl.BlockSpec((1, width), whole),
            pl.BlockSpec((width, local), whole),
            pl.BlockSpec((width, local), whole),
        ]
        + [tokens_spec(index) for index in range(COPIES)],
        out_specs=[pl.BlockSpec((blocks, 1, BLOCK, 2 * local), lambda i: (0, jnp.maximum(i - 1, 0), 0, 0))] * halves,
        out_shape=[jax.ShapeDtypeStruct((blocks, levels, BLOCK, 2 * local), jnp.bfloat16)] * halves,
        scratch_shapes=[
            pltpu.VMEM((patches, width), jnp.bfloat16),
            pltpu.VMEM((patches, width), jnp.bfloat16),
            pltpu.VMEM((count, patches), jnp.bfloat16),
            pltpu.VMEM((width, 2 * local), jnp.bfloat16),
        ],
        compiler_params=params(58),
        cost_estimate=pl.CostEstimate(
            flops=8 * levels * patches * (width + count) * local,
            bytes_accessed=2 * levels * patches * (width + 2 * local) + 4 * width * local,
            transcendentals=0,
        ),
        name="norm_project",
    )(slots, gain.reshape(1, width), key_weight, value_weight, *[tokens] * COPIES)


def attend_kernel(query_ref, *refs):
    pair_refs, out_ref = refs[: BLOCK // GROUP], refs[-1]
    levels, _, local = pair_refs[0].shape[1:]
    slots, local = BLOCK, local // 2
    latents = out_ref.shape[0] // slots
    rows = GROUP * latents
    columns = levels * GROUP
    heads = local // HEAD_DIM
    lane_head = lax.broadcasted_iota(jnp.int32, (rows, local), 1) // HEAD_DIM
    row_slot = lax.broadcasted_iota(jnp.int32, (GROUP, heads * rows), 0)
    column_slot = (lax.broadcasted_iota(jnp.int32, (GROUP, heads * rows), 1) // latents) & (GROUP - 1)
    same = row_slot - column_slot == 0
    scale = math.log2(math.e) / math.sqrt(HEAD_DIM)
    queries = query_ref[...].reshape(slots * latents, local).astype(jnp.float32)

    def score(start):
        part = queries[start * latents : start * latents + rows]
        part = jnp.concatenate(
            [jnp.where(lane_head == head, part, 0.0).astype(jnp.bfloat16) for head in range(heads)], axis=0
        )
        keys = pair_refs[start // GROUP][0, :, :, :local].reshape(columns, local)
        product = lax.dot_general(keys, part, (((1,), (1,)), ((), ())), preferred_element_type=jnp.float32)
        return product.reshape(levels, GROUP, heads * rows)

    def soften(product):
        expo = jnp.exp2((product - jnp.max(product, axis=0, keepdims=True)) * scale)
        inverse = jnp.where(same, 1.0 / jnp.sum(expo, axis=0), 0.0)
        return (expo * inverse[None]).reshape(columns, heads * rows).astype(jnp.bfloat16)

    def mix(start, soft):
        values = pair_refs[start // GROUP][0, :, :, local:].reshape(columns, local)
        wide = lax.dot_general(soft, values, (((0,), (0,)), ((), ())), preferred_element_type=jnp.float32)
        mixed = wide[:rows]
        for head in range(1, heads):
            mixed = jnp.where(lane_head == head, wide[head * rows : (head + 1) * rows], mixed)
        out_ref[pl.ds(start * latents, rows), :] = mixed.astype(jnp.bfloat16)

    starts = range(0, slots, GROUP)
    scores, softs = {}, {}
    for index in range(len(starts) + 2):
        if index < len(starts):
            scores[index] = score(starts[index])
        if 0 <= index - 1 < len(starts):
            softs[index - 1] = soften(scores.pop(index - 1))
        if 0 <= index - 2:
            mix(starts[index - 2], softs.pop(index - 2))


def attend(queries, pairs, index, after=()):
    stripes, halves, half, latents, local = queries.shape
    levels = pairs.shape[1]
    steps = pairs.shape[0]
    block = stripes * half * latents // steps

    def pair_spec(group):
        return pl.BlockSpec((1, levels, GROUP, 2 * local), lambda i: (i, 0, group, 0))

    return pl.pallas_call(
        attend_kernel,
        grid=(steps,),
        in_specs=[
            pl.BlockSpec((stripes // steps, 1, half, latents, local), lambda i: (i, index, 0, 0, 0)),
        ]
        + [pair_spec(group) for group in range(BLOCK // GROUP)]
        + [pl.BlockSpec(memory_space=pl.ANY)] * len(after),
        out_specs=pl.BlockSpec((block, local), lambda i: (i, 0)),
        out_shape=jax.ShapeDtypeStruct((steps * block, local), jnp.bfloat16),
        compiler_params=params(55),
        cost_estimate=pl.CostEstimate(
            flops=64 * steps * block * levels * GROUP * local,
            bytes_accessed=4 * steps * (block + levels * BLOCK) * local,
            transcendentals=0,
        ),
        name="attend_slots",
    )(queries, *[pairs] * (BLOCK // GROUP), *after)


def combine_rows(mixed_refs, weight_refs, part):
    total = None
    for mixed_ref, weight_ref in zip(mixed_refs, weight_refs):
        term = jnp.dot(mixed_ref[part, :], weight_ref[...], preferred_element_type=jnp.float32)
        term = term.astype(jnp.bfloat16).astype(jnp.float32)
        total = term if total is None else total + term
    return total.astype(jnp.bfloat16)


def combine_kernel(*refs):
    out_ref = refs[-1]
    stripes, caps, latents, local = out_ref.shape
    rest = refs[8:-1]
    half = caps - sum(ref.shape[1] for ref in rest)
    for stripe in range(stripes):
        part = pl.ds(stripe * half * latents, half * latents)
        rows = combine_rows(refs[:4], refs[4:8], part)
        out_ref[stripe, :half] = rows.reshape(half, latents, local)
        for ref in rest:
            out_ref[stripe, half:] = ref[stripe]


def combine(groups, weights, shape, rest=()):
    operands = (*groups, *weights, *rest)
    rows, local = groups[0].shape
    vmem = pl.BlockSpec(memory_space=pltpu.VMEM)
    return pl.pallas_call(
        combine_kernel,
        in_specs=[vmem] * len(operands),
        out_specs=vmem,
        out_shape=jax.ShapeDtypeStruct(shape, jnp.bfloat16),
        compiler_params=params(20),
        cost_estimate=pl.CostEstimate(
            flops=24 * rows * local * local, bytes_accessed=10 * rows * local, transcendentals=0
        ),
        name="combine_groups",
    )(*operands)


def swap(array, axis_name, distance):
    size = lax.axis_size(axis_name)
    return lax.ppermute(array, axis_name, [(i, i ^ distance) for i in range(size)])


def follow(array, *others):
    return lax.optimization_barrier((array, *others))[0]


def spread_heads(mixed):
    second = swap(mixed, "head", 2)
    return mixed, swap(mixed, "head", 1), second, swap(second, "head", 1)


def exchange(array, stripes):
    array = array.reshape(stripes, -1, *array.shape[1:])
    return lax.all_to_all(array, "lat", split_axis=0, concat_axis=0, tiled=True)


def spread_weight(out_weight, head):
    local = out_weight.shape[0]
    parts = []
    for distance in range(lax.axis_size("head")):
        start = jnp.bitwise_xor(head, distance) * local
        part = lax.dynamic_slice_in_dim(out_weight, start, local, 1)
        parts.append(swap(part, "head", distance) if distance else part)
    return parts


def shards(level_tokens, ln_gain, key_weight, value_weight, out_weight, ocean_queries, send_slots):
    stripes = lax.axis_size("lat")
    caps = send_slots.shape[2]
    shape = ocean_queries.shape
    slots, latents, local = shape
    halves = 2 if caps == BLOCK else 1
    queries = exchange(ocean_queries, stripes).reshape(stripes, halves, -1, latents, local)
    weights = spread_weight(out_weight, lax.axis_index("head"))
    tokens = jnp.transpose(level_tokens, (1, 0, 2))
    pairs = project(send_slots[0], tokens, ln_gain, key_weight, value_weight, halves)
    pairs, weights = lax.optimization_barrier((pairs, weights))
    if halves == 1:
        mixed = exchange(attend(queries, pairs[0], 0), stripes).reshape(-1, local)
        return combine(spread_heads(mixed), weights, (stripes, caps, latents, local)).reshape(shape)
    late = attend(queries, pairs[1], 1)
    early = attend(queries, pairs[0], 0, (late,))
    late = combine(spread_heads(late), weights, (stripes, caps // 2, latents, local))
    early = follow(exchange(early, stripes), late).reshape(-1, local)
    late = exchange(late.reshape(-1, latents, local), stripes)
    return combine(spread_heads(early), weights, (stripes, caps, latents, local), (late,)).reshape(shape)


def solution(mesh):
    return jax.shard_map(
        shards,
        mesh=mesh,
        in_specs=(
            P("lat", None, None),
            P(),
            P(None, "head"),
            P(None, "head"),
            P("head", None),
            P("lat", None, "head"),
            P("lat", None, None),
        ),
        out_specs=P("lat", None, "head"),
        check_vma=False,
    )
```

```python
import functools
import math

import jax
import jax.numpy as jnp
from jax import lax
from jax.experimental import pallas as pl
from jax.experimental.pallas import tpu as pltpu
from jax.sharding import PartitionSpec as P

HEAD_DIM = 64
EPS = 1e-05
GROUP = 16
BLOCK = 64
ROWS = 32
LANES = 128
MIB = 1024 * 1024


def params(mib):
    return pltpu.CompilerParams(vmem_limit_bytes=mib * MIB)


def normalize_rows(tokens, gain):
    width = tokens.shape[-1]
    tokens = tokens.astype(jnp.float32)
    center = jnp.sum(tokens, axis=-1, keepdims=True) * (1.0 / width)
    shifted = tokens - center
    spread = jnp.sum(shifted * shifted, axis=-1, keepdims=True) * (1.0 / width)
    return (shifted * lax.rsqrt(spread + EPS) * gain).astype(jnp.bfloat16)


def build_pick(slots_ref, pick_ref, halves):
    stripes, caps = slots_ref.shape
    half = caps // halves
    diagonal = lax.broadcasted_iota(jnp.int32, (caps, caps), 0) == lax.broadcasted_iota(jnp.int32, (caps, caps), 1)
    patch = lax.broadcasted_iota(jnp.int32, (caps, pick_ref.shape[1]), 1)
    for owner in range(stripes):
        row = jnp.broadcast_to(slots_ref[owner : owner + 1, :], (caps, caps))
        column = jnp.sum(jnp.where(diagonal, row, 0), axis=-1, keepdims=True)
        pick = jnp.where(patch == column, 1.0, 0.0).astype(jnp.bfloat16)
        for index in range(halves):
            start = (index * stripes + owner) * half
            pick_ref[start : start + half, :] = pick[index * half : (index + 1) * half]


def project_kernel(
    halves,
    slots_ref,
    tokens_ref,
    gain_ref,
    key_weight_ref,
    value_weight_ref,
    out_ref,
    even_ref,
    odd_ref,
    pick_ref,
    weight_ref,
):
    step = pl.program_id(0)
    patches = tokens_ref.shape[1]
    local = key_weight_ref.shape[1]

    @pl.when(step == 0)
    def _():
        build_pick(slots_ref, pick_ref, halves)
        weight_ref[:, :local] = key_weight_ref[...]
        weight_ref[:, local:] = value_weight_ref[...]

    def stage(write_ref, read_ref):
        gain = gain_ref[...]
        product = jnp.dot(read_ref[...], weight_ref[...], preferred_element_type=jnp.float32).astype(jnp.bfloat16)
        picked = jnp.dot(pick_ref[...], product, preferred_element_type=jnp.float32).astype(jnp.bfloat16)
        out_ref[:, 0] = picked.reshape(out_ref.shape[0], BLOCK, out_ref.shape[-1])
        for start in range(0, patches, ROWS):
            part = pl.ds(start, ROWS)
            write_ref[part, :] = normalize_rows(tokens_ref[0, part, :], gain)

    @pl.when(step % 2 == 0)
    def _():
        stage(even_ref, odd_ref)

    @pl.when(step % 2 == 1)
    def _():
        stage(odd_ref, even_ref)


def project(slots, tokens, gain, key_weight, value_weight, halves):
    levels, patches, width = tokens.shape
    local = key_weight.shape[1]
    count = slots.size
    whole = lambda i: (0, 0)
    return pl.pallas_call(
        functools.partial(project_kernel, halves),
        grid=(levels + 1,),
        in_specs=[
            pl.BlockSpec(slots.shape, whole),
            pl.BlockSpec((1, patches, width), lambda i: (jnp.minimum(i, levels - 1), 0, 0)),
            pl.BlockSpec((1, width), whole),
            pl.BlockSpec((width, local), whole),
            pl.BlockSpec((width, local), whole),
        ],
        out_specs=pl.BlockSpec((count // BLOCK, 1, BLOCK, 2 * local), lambda i: (0, jnp.maximum(i - 1, 0), 0, 0)),
        out_shape=jax.ShapeDtypeStruct((count // BLOCK, levels, BLOCK, 2 * local), jnp.bfloat16),
        scratch_shapes=[
            pltpu.VMEM((patches, width), jnp.bfloat16),
            pltpu.VMEM((patches, width), jnp.bfloat16),
            pltpu.VMEM((count, patches), jnp.bfloat16),
            pltpu.VMEM((width, 2 * local), jnp.bfloat16),
        ],
        compiler_params=params(58),
        cost_estimate=pl.CostEstimate(
            flops=8 * levels * patches * (width + count) * local,
            bytes_accessed=2 * levels * patches * (width + 2 * local) + 4 * width * local,
            transcendentals=0,
        ),
        name="norm_project",
    )(slots, tokens, gain.reshape(1, width), key_weight, value_weight)


def attend_kernel(query_ref, pair_ref, *refs):
    out_ref = refs[-1]
    levels, slots, local = pair_ref.shape[1:]
    local = local // 2
    latents = out_ref.shape[0] // slots
    rows = GROUP * latents
    columns = levels * GROUP
    heads = LANES // HEAD_DIM
    lane_head = lax.broadcasted_iota(jnp.int32, (rows, LANES), 1) // HEAD_DIM
    row_slot = lax.broadcasted_iota(jnp.int32, (GROUP, heads * rows), 0)
    column_slot = (lax.broadcasted_iota(jnp.int32, (GROUP, heads * rows), 1) // latents) & (GROUP - 1)
    same = row_slot - column_slot == 0
    scale = math.log2(math.e) / math.sqrt(HEAD_DIM)
    queries = query_ref[...].reshape(slots * latents, local).astype(jnp.float32)

    tasks = [(start, lane) for start in range(0, slots, GROUP) for lane in range(0, local, LANES)]
    scores = []
    for start, lane in tasks:
        part = queries[start * latents : start * latents + rows, lane : lane + LANES]
        part = jnp.concatenate(
            [jnp.where(lane_head == head, part, 0.0).astype(jnp.bfloat16) for head in range(heads)], axis=0
        )
        keys = pair_ref[0, :, pl.ds(start, GROUP), pl.ds(lane, LANES)].reshape(columns, LANES)
        product = lax.dot_general(keys, part, (((1,), (1,)), ((), ())), preferred_element_type=jnp.float32)
        scores.append(product.reshape(levels, GROUP, heads * rows))
    softs = []
    for product in scores:
        expo = jnp.exp2((product - jnp.max(product, axis=0, keepdims=True)) * scale)
        inverse = jnp.where(same, 1.0 / jnp.sum(expo, axis=0), 0.0)
        softs.append((expo * inverse[None]).reshape(columns, heads * rows).astype(jnp.bfloat16))
    for (start, lane), soft in zip(tasks, softs):
        values = pair_ref[0, :, pl.ds(start, GROUP), pl.ds(local + lane, LANES)].reshape(columns, LANES)
        wide = lax.dot_general(soft, values, (((0,), (0,)), ((), ())), preferred_element_type=jnp.float32)
        mixed = wide[:rows]
        for head in range(1, heads):
            mixed = jnp.where(lane_head == head, wide[head * rows : (head + 1) * rows], mixed)
        out_ref[pl.ds(start * latents, rows), pl.ds(lane, LANES)] = mixed.astype(jnp.bfloat16)


def attend(queries, pairs, index, after=()):
    stripes, halves, rows, local = queries.shape
    levels = pairs.shape[1]
    steps = pairs.shape[0] // halves
    block = stripes * rows // steps
    return pl.pallas_call(
        attend_kernel,
        grid=(steps,),
        in_specs=[
            pl.BlockSpec((stripes // steps, 1, rows, local), lambda i: (i, index, 0, 0)),
            pl.BlockSpec((1, levels, BLOCK, 2 * local), lambda i: (index * steps + i, 0, 0, 0)),
        ]
        + [pl.BlockSpec(memory_space=pl.ANY)] * len(after),
        out_specs=pl.BlockSpec((block, local), lambda i: (i, 0)),
        out_shape=jax.ShapeDtypeStruct((steps * block, local), jnp.bfloat16),
        compiler_params=params(55),
        cost_estimate=pl.CostEstimate(
            flops=64 * steps * block * levels * GROUP * local,
            bytes_accessed=4 * steps * (block + levels * BLOCK) * local,
            transcendentals=0,
        ),
        name="attend_slots",
    )(queries, pairs, *after)


def combine_rows(mixed_refs, weight_refs, part):
    total = None
    for mixed_ref, weight_ref in zip(mixed_refs, weight_refs):
        term = jnp.dot(mixed_ref[part, :], weight_ref[...], preferred_element_type=jnp.float32)
        term = term.astype(jnp.bfloat16).astype(jnp.float32)
        total = term if total is None else total + term
    return total.astype(jnp.bfloat16)


def combine_home_kernel(place_ref, *refs):
    for distance, out_ref in enumerate(refs[8:]):
        rows = out_ref.shape[0] * out_ref.shape[1]
        start = jnp.bitwise_xor(place_ref[0], distance) * rows
        part = pl.ds(pl.multiple_of(start, rows), rows)
        out_ref[...] = combine_rows(refs[:4], refs[4:8], part).reshape(out_ref.shape)


def combine_kernel(place_ref, *refs):
    out_ref = refs[-1]
    stripes, caps, latents, local = out_ref.shape
    rest = refs[8:-1]
    half = caps - sum(ref.shape[0] for ref in rest[:1])
    for distance, ref in enumerate(rest):
        out_ref[jnp.bitwise_xor(place_ref[0], distance), half:] = ref[...]
    for stripe in range(stripes):
        part = pl.ds(stripe * half * latents, half * latents)
        rows = combine_rows(refs[:4], refs[4:8], part)
        out_ref[stripe, :half] = rows.reshape(half, latents, local)


def combine(kernel, place, groups, weights, out_shape, rest=()):
    operands = (*groups, *weights, *rest)
    rows, local = groups[0].shape
    vmem = pl.BlockSpec(memory_space=pltpu.VMEM)
    return pl.pallas_call(
        kernel,
        in_specs=[pl.BlockSpec(memory_space=pltpu.SMEM)] + [vmem] * len(operands),
        out_specs=jax.tree.map(lambda _: vmem, out_shape),
        out_shape=out_shape,
        compiler_params=params(20),
        cost_estimate=pl.CostEstimate(
            flops=24 * rows * local * local, bytes_accessed=10 * rows * local, transcendentals=0
        ),
        name="combine_groups",
    )(place, *operands)


def swap(array, axis_name, distance):
    size = lax.axis_size(axis_name)
    return lax.ppermute(array, axis_name, [(i, i ^ distance) for i in range(size)])


def follow(array, *others):
    return lax.optimization_barrier((array, *others))[0]


def spread_heads(mixed, others=()):
    second = swap(mixed, "head", 2)
    return mixed, swap(mixed, "head", 1), second, swap(follow(second, *others), "head", 1)


def exchange(array, stripes):
    array = array.reshape(stripes, -1, *array.shape[1:])
    return lax.all_to_all(array, "lat", split_axis=0, concat_axis=0, tiled=True)


def spread_weight(out_weight, head):
    local = out_weight.shape[0]
    parts = []
    for distance in range(lax.axis_size("head")):
        start = jnp.bitwise_xor(head, distance) * local
        part = lax.dynamic_slice_in_dim(out_weight, start, local, 1)
        parts.append(swap(part, "head", distance) if distance else part)
    return parts


def shards(level_tokens, ln_gain, key_weight, value_weight, out_weight, ocean_queries, send_slots):
    stripes = lax.axis_size("lat")
    caps = send_slots.shape[2]
    shape = ocean_queries.shape
    slots, latents, local = shape
    place = lax.axis_index("lat").reshape(1)
    halves = 2 if caps == BLOCK else 1
    queries = exchange(ocean_queries, stripes).reshape(stripes, halves, -1, local)
    weights = spread_weight(out_weight, lax.axis_index("head"))
    tokens = jnp.transpose(level_tokens, (1, 0, 2))
    pairs = project(send_slots[0], tokens, ln_gain, key_weight, value_weight, halves)
    pairs, weights = lax.optimization_barrier((pairs, weights))
    whole = jax.ShapeDtypeStruct((stripes, caps, latents, local), jnp.bfloat16)
    if halves == 1:
        mixed = exchange(attend(queries, pairs, 0), stripes).reshape(-1, local)
        return combine(combine_kernel, place, spread_heads(mixed), weights, whole).reshape(shape)
    late = attend(queries, pairs, 1)
    early = attend(queries, pairs, 0, (late,))
    chunks = [jax.ShapeDtypeStruct((caps // 2, latents, local), jnp.bfloat16)] * stripes
    chunks = combine(combine_home_kernel, place, spread_heads(late, (early,)), weights, chunks)
    chunks = [swap(chunk, "lat", distance) if distance else chunk for distance, chunk in enumerate(chunks)]
    near, far = chunks[: stripes // 2], chunks[stripes // 2 :]
    early = follow(exchange(early, stripes), *near).reshape(-1, local)
    return combine(combine_kernel, place, spread_heads(early, far), weights, whole, chunks).reshape(shape)


def solution(mesh):
    return jax.shard_map(
        shards,
        mesh=mesh,
        in_specs=(
            P("lat", None, None),
            P(),
            P(None, "head"),
            P(None, "head"),
            P("head", None),
            P("lat", None, "head"),
            P("lat", None, None),
        ),
        out_specs=P("lat", None, "head"),
        check_vma=False,
    )
```

```python
import functools
import math

import jax
import jax.numpy as jnp
from jax import lax
from jax.experimental import pallas as pl
from jax.experimental.pallas import tpu as pltpu
from jax.sharding import PartitionSpec as P

HEAD_DIM = 64
EPS = 1e-05
GROUP = 16
BLOCK = 64
ROWS = 32
LANES = 128
MIB = 1024 * 1024


def params(mib):
    return pltpu.CompilerParams(vmem_limit_bytes=mib * MIB)


def normalize_rows(tokens, gain):
    width = tokens.shape[-1]
    tokens = tokens.astype(jnp.float32)
    center = jnp.sum(tokens, axis=-1, keepdims=True) * (1.0 / width)
    shifted = tokens - center
    spread = jnp.sum(shifted * shifted, axis=-1, keepdims=True) * (1.0 / width)
    return (shifted * lax.rsqrt(spread + EPS) * gain).astype(jnp.bfloat16)


def build_pick(slots_ref, pick_ref, halves):
    stripes, caps = slots_ref.shape
    half = caps // halves
    diagonal = lax.broadcasted_iota(jnp.int32, (caps, caps), 0) == lax.broadcasted_iota(jnp.int32, (caps, caps), 1)
    patch = lax.broadcasted_iota(jnp.int32, (caps, pick_ref.shape[1]), 1)
    for owner in range(stripes):
        row = jnp.broadcast_to(slots_ref[owner : owner + 1, :], (caps, caps))
        column = jnp.sum(jnp.where(diagonal, row, 0), axis=-1, keepdims=True)
        pick = jnp.where(patch == column, 1.0, 0.0).astype(jnp.bfloat16)
        for index in range(halves):
            start = (index * stripes + owner) * half
            pick_ref[start : start + half, :] = pick[index * half : (index + 1) * half]


def project_kernel(
    halves,
    slots_ref,
    tokens_ref,
    gain_ref,
    key_weight_ref,
    value_weight_ref,
    out_ref,
    even_ref,
    odd_ref,
    pick_ref,
    weight_ref,
):
    step = pl.program_id(0)
    patches = tokens_ref.shape[1]
    local = key_weight_ref.shape[1]

    @pl.when(step == 0)
    def _():
        build_pick(slots_ref, pick_ref, halves)
        weight_ref[:, :local] = key_weight_ref[...]
        weight_ref[:, local:] = value_weight_ref[...]

    def stage(write_ref, read_ref):
        gain = gain_ref[...]
        product = jnp.dot(read_ref[...], weight_ref[...], preferred_element_type=jnp.float32).astype(jnp.bfloat16)
        picked = jnp.dot(pick_ref[...], product, preferred_element_type=jnp.float32).astype(jnp.bfloat16)
        out_ref[:, 0] = picked.reshape(out_ref.shape[0], BLOCK, out_ref.shape[-1])
        for start in range(0, patches, ROWS):
            part = pl.ds(start, ROWS)
            write_ref[part, :] = normalize_rows(tokens_ref[0, part, :], gain)

    @pl.when(step % 2 == 0)
    def _():
        stage(even_ref, odd_ref)

    @pl.when(step % 2 == 1)
    def _():
        stage(odd_ref, even_ref)


def project(slots, tokens, gain, key_weight, value_weight, halves):
    levels, patches, width = tokens.shape
    local = key_weight.shape[1]
    count = slots.size
    whole = lambda i: (0, 0)
    return pl.pallas_call(
        functools.partial(project_kernel, halves),
        grid=(levels + 1,),
        in_specs=[
            pl.BlockSpec(slots.shape, whole),
            pl.BlockSpec((1, patches, width), lambda i: (jnp.minimum(i, levels - 1), 0, 0)),
            pl.BlockSpec((1, width), whole),
            pl.BlockSpec((width, local), whole),
            pl.BlockSpec((width, local), whole),
        ],
        out_specs=pl.BlockSpec((count // BLOCK, 1, BLOCK, 2 * local), lambda i: (0, jnp.maximum(i - 1, 0), 0, 0)),
        out_shape=jax.ShapeDtypeStruct((count // BLOCK, levels, BLOCK, 2 * local), jnp.bfloat16),
        scratch_shapes=[
            pltpu.VMEM((patches, width), jnp.bfloat16),
            pltpu.VMEM((patches, width), jnp.bfloat16),
            pltpu.VMEM((count, patches), jnp.bfloat16),
            pltpu.VMEM((width, 2 * local), jnp.bfloat16),
        ],
        compiler_params=params(58),
        cost_estimate=pl.CostEstimate(
            flops=8 * levels * patches * (width + count) * local,
            bytes_accessed=2 * levels * patches * (width + 2 * local) + 4 * width * local,
            transcendentals=0,
        ),
        name="norm_project",
    )(slots, tokens, gain.reshape(1, width), key_weight, value_weight)


def attend_kernel(query_ref, pair_ref, *refs):
    out_ref = refs[-1]
    levels, slots, local = pair_ref.shape[1:]
    local = local // 2
    latents = out_ref.shape[0] // slots
    rows = GROUP * latents
    columns = levels * GROUP
    heads = LANES // HEAD_DIM
    lane_head = lax.broadcasted_iota(jnp.int32, (rows, LANES), 1) // HEAD_DIM
    row_slot = lax.broadcasted_iota(jnp.int32, (GROUP, heads * rows), 0)
    column_slot = (lax.broadcasted_iota(jnp.int32, (GROUP, heads * rows), 1) // latents) & (GROUP - 1)
    same = row_slot - column_slot == 0
    scale = math.log2(math.e) / math.sqrt(HEAD_DIM)
    queries = query_ref[...].reshape(slots * latents, local).astype(jnp.float32)

    tasks = [(start, lane) for start in range(0, slots, GROUP) for lane in range(0, local, LANES)]
    scores = []
    for start, lane in tasks:
        part = queries[start * latents : start * latents + rows, lane : lane + LANES]
        part = jnp.concatenate(
            [jnp.where(lane_head == head, part, 0.0).astype(jnp.bfloat16) for head in range(heads)], axis=0
        )
        keys = pair_ref[0, :, pl.ds(start, GROUP), pl.ds(lane, LANES)].reshape(columns, LANES)
        product = lax.dot_general(keys, part, (((1,), (1,)), ((), ())), preferred_element_type=jnp.float32)
        scores.append(product.reshape(levels, GROUP, heads * rows))
    softs = []
    for product in scores:
        expo = jnp.exp2((product - jnp.max(product, axis=0, keepdims=True)) * scale)
        inverse = jnp.where(same, 1.0 / jnp.sum(expo, axis=0), 0.0)
        softs.append((expo * inverse[None]).reshape(columns, heads * rows).astype(jnp.bfloat16))
    for (start, lane), soft in zip(tasks, softs):
        values = pair_ref[0, :, pl.ds(start, GROUP), pl.ds(local + lane, LANES)].reshape(columns, LANES)
        wide = lax.dot_general(soft, values, (((0,), (0,)), ((), ())), preferred_element_type=jnp.float32)
        mixed = wide[:rows]
        for head in range(1, heads):
            mixed = jnp.where(lane_head == head, wide[head * rows : (head + 1) * rows], mixed)
        out_ref[pl.ds(start * latents, rows), pl.ds(lane, LANES)] = mixed.astype(jnp.bfloat16)


def attend(queries, pairs, index, after=()):
    stripes, halves, rows, local = queries.shape
    levels = pairs.shape[1]
    steps = pairs.shape[0] // halves
    block = stripes * rows // steps
    return pl.pallas_call(
        attend_kernel,
        grid=(steps,),
        in_specs=[
            pl.BlockSpec((stripes // steps, 1, rows, local), lambda i: (i, index, 0, 0)),
            pl.BlockSpec((1, levels, BLOCK, 2 * local), lambda i: (index * steps + i, 0, 0, 0)),
        ]
        + [pl.BlockSpec(memory_space=pl.ANY)] * len(after),
        out_specs=pl.BlockSpec((block, local), lambda i: (i, 0)),
        out_shape=jax.ShapeDtypeStruct((steps * block, local), jnp.bfloat16),
        compiler_params=params(55),
        cost_estimate=pl.CostEstimate(
            flops=64 * steps * block * levels * GROUP * local,
            bytes_accessed=4 * steps * (block + levels * BLOCK) * local,
            transcendentals=0,
        ),
        name="attend_slots",
    )(queries, pairs, *after)


def combine_rows(mixed_refs, weight_refs, part):
    total = None
    for mixed_ref, weight_ref in zip(mixed_refs, weight_refs):
        term = jnp.dot(mixed_ref[part, :], weight_ref[...], preferred_element_type=jnp.float32)
        term = term.astype(jnp.bfloat16).astype(jnp.float32)
        total = term if total is None else total + term
    return total.astype(jnp.bfloat16)


def combine_home_kernel(place_ref, *refs):
    for distance, out_ref in enumerate(refs[8:]):
        rows = out_ref.shape[0] * out_ref.shape[1]
        start = jnp.bitwise_xor(place_ref[0], distance) * rows
        part = pl.ds(pl.multiple_of(start, rows), rows)
        out_ref[...] = combine_rows(refs[:4], refs[4:8], part).reshape(out_ref.shape)


def combine_kernel(place_ref, *refs):
    out_ref = refs[-1]
    stripes, caps, latents, local = out_ref.shape
    rest = refs[8:-1]
    half = caps - sum(ref.shape[0] for ref in rest[:1])
    for distance, ref in enumerate(rest):
        out_ref[jnp.bitwise_xor(place_ref[0], distance), half:] = ref[...]
    for stripe in range(stripes):
        part = pl.ds(stripe * half * latents, half * latents)
        rows = combine_rows(refs[:4], refs[4:8], part)
        out_ref[stripe, :half] = rows.reshape(half, latents, local)


def combine(kernel, place, groups, weights, out_shape, rest=()):
    operands = (*groups, *weights, *rest)
    rows, local = groups[0].shape
    vmem = pl.BlockSpec(memory_space=pltpu.VMEM)
    return pl.pallas_call(
        kernel,
        in_specs=[pl.BlockSpec(memory_space=pltpu.SMEM)] + [vmem] * len(operands),
        out_specs=jax.tree.map(lambda _: vmem, out_shape),
        out_shape=out_shape,
        compiler_params=params(20),
        cost_estimate=pl.CostEstimate(
            flops=24 * rows * local * local, bytes_accessed=10 * rows * local, transcendentals=0
        ),
        name="combine_groups",
    )(place, *operands)


def swap(array, axis_name, distance):
    size = lax.axis_size(axis_name)
    return lax.ppermute(array, axis_name, [(i, i ^ distance) for i in range(size)])


def follow(array, *others):
    return lax.optimization_barrier((array, *others))[0]


def spread_heads(mixed, others=()):
    second = swap(mixed, "head", 2)
    return mixed, swap(mixed, "head", 1), second, swap(follow(second, *others), "head", 1)


def exchange(array, stripes):
    array = array.reshape(stripes, -1, *array.shape[1:])
    return lax.all_to_all(array, "lat", split_axis=0, concat_axis=0, tiled=True)


def spread_weight(out_weight, head):
    local = out_weight.shape[0]
    parts = []
    for distance in range(lax.axis_size("head")):
        start = jnp.bitwise_xor(head, distance) * local
        part = lax.dynamic_slice_in_dim(out_weight, start, local, 1)
        parts.append(swap(part, "head", distance) if distance else part)
    return parts


def shards(level_tokens, ln_gain, key_weight, value_weight, out_weight, ocean_queries, send_slots):
    stripes = lax.axis_size("lat")
    caps = send_slots.shape[2]
    shape = ocean_queries.shape
    slots, latents, local = shape
    place = lax.axis_index("lat").reshape(1)
    halves = 2 if caps == BLOCK else 1
    queries = exchange(ocean_queries, stripes).reshape(stripes, halves, -1, local)
    weights = spread_weight(out_weight, lax.axis_index("head"))
    tokens = jnp.transpose(level_tokens, (1, 0, 2))
    pairs = project(send_slots[0], tokens, ln_gain, key_weight, value_weight, halves)
    pairs, weights = lax.optimization_barrier((pairs, weights))
    whole = jax.ShapeDtypeStruct((stripes, caps, latents, local), jnp.bfloat16)
    if halves == 1:
        mixed = exchange(attend(queries, pairs, 0), stripes).reshape(-1, local)
        return combine(combine_kernel, place, spread_heads(mixed), weights, whole).reshape(shape)
    late = attend(queries, pairs, 1)
    early = attend(queries, pairs, 0, (late,))
    chunks = [jax.ShapeDtypeStruct((caps // 2, latents, local), jnp.bfloat16)] * stripes
    chunks = combine(combine_home_kernel, place, spread_heads(late, (early,)), weights, chunks)
    moved = [swap(chunks[distance], "lat", distance) for distance in range(stripes - 1, 0, -1)]
    pair = stripes // 4
    early = follow(exchange(early, stripes), *moved[:pair]).reshape(-1, local)
    chunks = [chunks[0], *reversed(moved)]
    return combine(combine_kernel, place, spread_heads(early, moved[pair:]), weights, whole, chunks).reshape(shape)


def solution(mesh):
    return jax.shard_map(
        shards,
        mesh=mesh,
        in_specs=(
            P("lat", None, None),
            P(),
            P(None, "head"),
            P(None, "head"),
            P("head", None),
            P("lat", None, "head"),
            P("lat", None, None),
        ),
        out_specs=P("lat", None, "head"),
        check_vma=False,
    )
```

```python
import functools
import math

import jax
import jax.numpy as jnp
from jax import lax
from jax.experimental import pallas as pl
from jax.experimental.pallas import tpu as pltpu
from jax.sharding import PartitionSpec as P

HEAD_DIM = 64
EPS = 1e-05
GROUP = 16
BLOCK = 64
ROWS = 32
LANES = 128
MIB = 1024 * 1024


def params(mib):
    return pltpu.CompilerParams(vmem_limit_bytes=mib * MIB)


def normalize_rows(tokens, gain):
    width = tokens.shape[-1]
    tokens = tokens.astype(jnp.float32)
    center = jnp.sum(tokens, axis=-1, keepdims=True) * (1.0 / width)
    shifted = tokens - center
    spread = jnp.sum(shifted * shifted, axis=-1, keepdims=True) * (1.0 / width)
    return (shifted * lax.rsqrt(spread + EPS) * gain).astype(jnp.bfloat16)


def build_pick(slots_ref, pick_ref, halves):
    stripes, caps = slots_ref.shape
    half = caps // halves
    diagonal = lax.broadcasted_iota(jnp.int32, (caps, caps), 0) == lax.broadcasted_iota(jnp.int32, (caps, caps), 1)
    patch = lax.broadcasted_iota(jnp.int32, (caps, pick_ref.shape[1]), 1)
    for owner in range(stripes):
        row = jnp.broadcast_to(slots_ref[owner : owner + 1, :], (caps, caps))
        column = jnp.sum(jnp.where(diagonal, row, 0), axis=-1, keepdims=True)
        pick = jnp.where(patch == column, 1.0, 0.0).astype(jnp.bfloat16)
        for index in range(halves):
            start = (index * stripes + owner) * half
            pick_ref[start : start + half, :] = pick[index * half : (index + 1) * half]


def project_kernel(
    halves,
    slots_ref,
    tokens_ref,
    gain_ref,
    key_weight_ref,
    value_weight_ref,
    out_ref,
    even_ref,
    odd_ref,
    pick_ref,
    weight_ref,
):
    step = pl.program_id(0)
    patches = tokens_ref.shape[1]
    local = key_weight_ref.shape[1]

    @pl.when(step == 0)
    def _():
        build_pick(slots_ref, pick_ref, halves)
        weight_ref[:, :local] = key_weight_ref[...]
        weight_ref[:, local:] = value_weight_ref[...]

    def stage(write_ref, read_ref):
        gain = gain_ref[...]
        product = jnp.dot(read_ref[...], weight_ref[...], preferred_element_type=jnp.float32).astype(jnp.bfloat16)
        picked = jnp.dot(pick_ref[...], product, preferred_element_type=jnp.float32).astype(jnp.bfloat16)
        out_ref[:, 0] = picked.reshape(out_ref.shape[0], BLOCK, out_ref.shape[-1])
        for start in range(0, patches, ROWS):
            part = pl.ds(start, ROWS)
            write_ref[part, :] = normalize_rows(tokens_ref[0, part, :], gain)

    @pl.when(step % 2 == 0)
    def _():
        stage(even_ref, odd_ref)

    @pl.when(step % 2 == 1)
    def _():
        stage(odd_ref, even_ref)


def project(slots, tokens, gain, key_weight, value_weight, halves):
    levels, patches, width = tokens.shape
    local = key_weight.shape[1]
    count = slots.size
    whole = lambda i: (0, 0)
    return pl.pallas_call(
        functools.partial(project_kernel, halves),
        grid=(levels + 1,),
        in_specs=[
            pl.BlockSpec(slots.shape, whole),
            pl.BlockSpec((1, patches, width), lambda i: (jnp.minimum(i, levels - 1), 0, 0)),
            pl.BlockSpec((1, width), whole),
            pl.BlockSpec((width, local), whole),
            pl.BlockSpec((width, local), whole),
        ],
        out_specs=pl.BlockSpec((count // BLOCK, 1, BLOCK, 2 * local), lambda i: (0, jnp.maximum(i - 1, 0), 0, 0)),
        out_shape=jax.ShapeDtypeStruct((count // BLOCK, levels, BLOCK, 2 * local), jnp.bfloat16),
        scratch_shapes=[
            pltpu.VMEM((patches, width), jnp.bfloat16),
            pltpu.VMEM((patches, width), jnp.bfloat16),
            pltpu.VMEM((count, patches), jnp.bfloat16),
            pltpu.VMEM((width, 2 * local), jnp.bfloat16),
        ],
        compiler_params=params(58),
        cost_estimate=pl.CostEstimate(
            flops=8 * levels * patches * (width + count) * local,
            bytes_accessed=2 * levels * patches * (width + 2 * local) + 4 * width * local,
            transcendentals=0,
        ),
        name="norm_project",
    )(slots, tokens, gain.reshape(1, width), key_weight, value_weight)


def attend_kernel(query_ref, pair_ref, *refs):
    out_ref = refs[-1]
    levels, slots, local = pair_ref.shape[1:]
    local = local // 2
    latents = out_ref.shape[0] // slots
    rows = GROUP * latents
    columns = levels * GROUP
    heads = LANES // HEAD_DIM
    lane_head = lax.broadcasted_iota(jnp.int32, (rows, LANES), 1) // HEAD_DIM
    row_slot = lax.broadcasted_iota(jnp.int32, (GROUP, heads * rows), 0)
    column_slot = (lax.broadcasted_iota(jnp.int32, (GROUP, heads * rows), 1) // latents) & (GROUP - 1)
    same = row_slot - column_slot == 0
    scale = math.log2(math.e) / math.sqrt(HEAD_DIM)
    queries = query_ref[...].reshape(slots * latents, local).astype(jnp.float32)

    tasks = [(start, lane) for start in range(0, slots, GROUP) for lane in range(0, local, LANES)]
    scores = []
    for start, lane in tasks:
        part = queries[start * latents : start * latents + rows, lane : lane + LANES]
        part = jnp.concatenate(
            [jnp.where(lane_head == head, part, 0.0).astype(jnp.bfloat16) for head in range(heads)], axis=0
        )
        keys = pair_ref[0, :, pl.ds(start, GROUP), pl.ds(lane, LANES)].reshape(columns, LANES)
        product = lax.dot_general(keys, part, (((1,), (1,)), ((), ())), preferred_element_type=jnp.float32)
        scores.append(product.reshape(levels, GROUP, heads * rows))
    softs = []
    for product in scores:
        expo = jnp.exp2((product - jnp.max(product, axis=0, keepdims=True)) * scale)
        inverse = jnp.where(same, 1.0 / jnp.sum(expo, axis=0), 0.0)
        softs.append((expo * inverse[None]).reshape(columns, heads * rows).astype(jnp.bfloat16))
    for (start, lane), soft in zip(tasks, softs):
        values = pair_ref[0, :, pl.ds(start, GROUP), pl.ds(local + lane, LANES)].reshape(columns, LANES)
        wide = lax.dot_general(soft, values, (((0,), (0,)), ((), ())), preferred_element_type=jnp.float32)
        mixed = wide[:rows]
        for head in range(1, heads):
            mixed = jnp.where(lane_head == head, wide[head * rows : (head + 1) * rows], mixed)
        out_ref[pl.ds(start * latents, rows), pl.ds(lane, LANES)] = mixed.astype(jnp.bfloat16)


def attend(queries, pairs, index, after=()):
    stripes, halves, rows, local = queries.shape
    levels = pairs.shape[1]
    steps = pairs.shape[0] // halves
    block = stripes * rows // steps
    return pl.pallas_call(
        attend_kernel,
        grid=(steps,),
        in_specs=[
            pl.BlockSpec((stripes // steps, 1, rows, local), lambda i: (i, index, 0, 0)),
            pl.BlockSpec((1, levels, BLOCK, 2 * local), lambda i: (index * steps + i, 0, 0, 0)),
        ]
        + [pl.BlockSpec(memory_space=pl.ANY)] * len(after),
        out_specs=pl.BlockSpec((block, local), lambda i: (i, 0)),
        out_shape=jax.ShapeDtypeStruct((steps * block, local), jnp.bfloat16),
        compiler_params=params(55),
        cost_estimate=pl.CostEstimate(
            flops=64 * steps * block * levels * GROUP * local,
            bytes_accessed=4 * steps * (block + levels * BLOCK) * local,
            transcendentals=0,
        ),
        name="attend_slots",
    )(queries, pairs, *after)


def combine_rows(mixed_refs, weight_refs, part):
    total = None
    for mixed_ref, weight_ref in zip(mixed_refs, weight_refs):
        term = jnp.dot(mixed_ref[part, :], weight_ref[...], preferred_element_type=jnp.float32)
        term = term.astype(jnp.bfloat16).astype(jnp.float32)
        total = term if total is None else total + term
    return total.astype(jnp.bfloat16)


def combine_home_kernel(place_ref, *refs):
    for distance, out_ref in enumerate(refs[8:]):
        rows = out_ref.shape[0] * out_ref.shape[1]
        start = jnp.bitwise_xor(place_ref[0], distance) * rows
        part = pl.ds(pl.multiple_of(start, rows), rows)
        out_ref[...] = combine_rows(refs[:4], refs[4:8], part).reshape(out_ref.shape)


def combine_kernel(place_ref, *refs):
    out_ref = refs[-1]
    stripes, caps, latents, local = out_ref.shape
    rest = refs[8:-1]
    half = caps - sum(ref.shape[0] for ref in rest[:1])
    for distance, ref in enumerate(rest):
        out_ref[jnp.bitwise_xor(place_ref[0], distance), half:] = ref[...]
    for stripe in range(stripes):
        part = pl.ds(stripe * half * latents, half * latents)
        rows = combine_rows(refs[:4], refs[4:8], part)
        out_ref[stripe, :half] = rows.reshape(half, latents, local)


def combine(kernel, place, groups, weights, out_shape, rest=()):
    operands = (*groups, *weights, *rest)
    rows, local = groups[0].shape
    vmem = pl.BlockSpec(memory_space=pltpu.VMEM)
    return pl.pallas_call(
        kernel,
        in_specs=[pl.BlockSpec(memory_space=pltpu.SMEM)] + [vmem] * len(operands),
        out_specs=jax.tree.map(lambda _: vmem, out_shape),
        out_shape=out_shape,
        compiler_params=params(20),
        cost_estimate=pl.CostEstimate(
            flops=24 * rows * local * local, bytes_accessed=10 * rows * local, transcendentals=0
        ),
        name="combine_groups",
    )(place, *operands)


def swap(array, axis_name, distance):
    size = lax.axis_size(axis_name)
    return lax.ppermute(array, axis_name, [(i, i ^ distance) for i in range(size)])


def follow(array, *others):
    return lax.optimization_barrier((array, *others))[0]


def spread_heads(mixed, others=()):
    second = swap(mixed, "head", 2)
    return mixed, swap(mixed, "head", 1), second, swap(follow(second, *others), "head", 1)


def exchange(array, stripes):
    array = array.reshape(stripes, -1, *array.shape[1:])
    return lax.all_to_all(array, "lat", split_axis=0, concat_axis=0, tiled=True)


def spread_weight(out_weight, head):
    local = out_weight.shape[0]
    parts = []
    for distance in range(lax.axis_size("head")):
        start = jnp.bitwise_xor(head, distance) * local
        part = lax.dynamic_slice_in_dim(out_weight, start, local, 1)
        parts.append(swap(part, "head", distance) if distance else part)
    return parts


def shards(level_tokens, ln_gain, key_weight, value_weight, out_weight, ocean_queries, send_slots):
    stripes = lax.axis_size("lat")
    caps = send_slots.shape[2]
    shape = ocean_queries.shape
    slots, latents, local = shape
    place = lax.axis_index("lat").reshape(1)
    halves = 2 if caps == BLOCK else 1
    queries = exchange(ocean_queries, stripes).reshape(stripes, halves, -1, local)
    weights = spread_weight(out_weight, lax.axis_index("head"))
    tokens = jnp.transpose(level_tokens, (1, 0, 2))
    pairs = project(send_slots[0], tokens, ln_gain, key_weight, value_weight, halves)
    pairs, weights = lax.optimization_barrier((pairs, weights))
    whole = jax.ShapeDtypeStruct((stripes, caps, latents, local), jnp.bfloat16)
    if halves == 1:
        mixed = exchange(attend(queries, pairs, 0), stripes).reshape(-1, local)
        return combine(combine_kernel, place, spread_heads(mixed), weights, whole).reshape(shape)
    early = attend(queries, pairs, 0)
    late = attend(queries, pairs, 1, (early,))
    early = exchange(early, stripes)
    late = spread_heads(late, (early,))
    chunks = [jax.ShapeDtypeStruct((caps // 2, latents, local), jnp.bfloat16)] * stripes
    chunks = combine(combine_home_kernel, place, late, weights, chunks)
    moved = [swap(chunks[distance], "lat", distance) for distance in range(stripes - 1, 0, -1)]
    early = follow(early, late[2]).reshape(-1, local)
    chunks = [chunks[0], *reversed(moved)]
    return combine(combine_kernel, place, spread_heads(early, moved), weights, whole, chunks).reshape(shape)


def solution(mesh):
    return jax.shard_map(
        shards,
        mesh=mesh,
        in_specs=(
            P("lat", None, None),
            P(),
            P(None, "head"),
            P(None, "head"),
            P("head", None),
            P("lat", None, "head"),
            P("lat", None, None),
        ),
        out_specs=P("lat", None, "head"),
        check_vma=False,
    )
```

```python
import math

import jax
import jax.numpy as jnp
from jax import lax
from jax.experimental import pallas as pl
from jax.experimental.pallas import tpu as pltpu
from jax.sharding import PartitionSpec as P

HEAD_DIM = 64
EPS = 1e-05
GROUP = 16
BLOCK = 64
ROWS = 32
LANES = 128
MIB = 1024 * 1024


def params(mib):
    return pltpu.CompilerParams(vmem_limit_bytes=mib * MIB)


def normalize_rows(tokens, gain):
    width = tokens.shape[-1]
    tokens = tokens.astype(jnp.float32)
    center = jnp.sum(tokens, axis=-1, keepdims=True) * (1.0 / width)
    shifted = tokens - center
    spread = jnp.sum(shifted * shifted, axis=-1, keepdims=True) * (1.0 / width)
    return (shifted * lax.rsqrt(spread + EPS) * gain).astype(jnp.bfloat16)


def build_pick(slots_ref, pick_ref):
    stripes, caps = slots_ref.shape
    diagonal = lax.broadcasted_iota(jnp.int32, (caps, caps), 0) == lax.broadcasted_iota(jnp.int32, (caps, caps), 1)
    patch = lax.broadcasted_iota(jnp.int32, (caps, pick_ref.shape[1]), 1)
    for owner in range(stripes):
        row = jnp.broadcast_to(slots_ref[owner : owner + 1, :], (caps, caps))
        column = jnp.sum(jnp.where(diagonal, row, 0), axis=-1, keepdims=True)
        pick = jnp.where(patch == column, 1.0, 0.0).astype(jnp.bfloat16)
        pick_ref[owner * caps : (owner + 1) * caps, :] = pick


def project_kernel(
    slots_ref,
    tokens_ref,
    gain_ref,
    key_weight_ref,
    value_weight_ref,
    out_ref,
    even_ref,
    odd_ref,
    pick_ref,
    weight_ref,
):
    step = pl.program_id(0)
    patches = tokens_ref.shape[1]
    local = key_weight_ref.shape[1]

    @pl.when(step == 0)
    def _():
        build_pick(slots_ref, pick_ref)
        weight_ref[:, :local] = key_weight_ref[...]
        weight_ref[:, local:] = value_weight_ref[...]

    def stage(write_ref, read_ref):
        gain = gain_ref[...]
        product = jnp.dot(read_ref[...], weight_ref[...], preferred_element_type=jnp.float32).astype(jnp.bfloat16)
        picked = jnp.dot(pick_ref[...], product, preferred_element_type=jnp.float32).astype(jnp.bfloat16)
        out_ref[:, 0] = picked.reshape(out_ref.shape[0], BLOCK, out_ref.shape[-1])
        for start in range(0, patches, ROWS):
            part = pl.ds(start, ROWS)
            write_ref[part, :] = normalize_rows(tokens_ref[0, part, :], gain)

    @pl.when(step % 2 == 0)
    def _():
        stage(even_ref, odd_ref)

    @pl.when(step % 2 == 1)
    def _():
        stage(odd_ref, even_ref)


def project(slots, tokens, gain, key_weight, value_weight):
    levels, patches, width = tokens.shape
    local = key_weight.shape[1]
    count = slots.size
    whole = lambda i: (0, 0)
    return pl.pallas_call(
        project_kernel,
        grid=(levels + 1,),
        in_specs=[
            pl.BlockSpec(slots.shape, whole),
            pl.BlockSpec((1, patches, width), lambda i: (jnp.minimum(i, levels - 1), 0, 0)),
            pl.BlockSpec((1, width), whole),
            pl.BlockSpec((width, local), whole),
            pl.BlockSpec((width, local), whole),
        ],
        out_specs=pl.BlockSpec((count // BLOCK, 1, BLOCK, 2 * local), lambda i: (0, jnp.maximum(i - 1, 0), 0, 0)),
        out_shape=jax.ShapeDtypeStruct((count // BLOCK, levels, BLOCK, 2 * local), jnp.bfloat16),
        scratch_shapes=[
            pltpu.VMEM((patches, width), jnp.bfloat16),
            pltpu.VMEM((patches, width), jnp.bfloat16),
            pltpu.VMEM((count, patches), jnp.bfloat16),
            pltpu.VMEM((width, 2 * local), jnp.bfloat16),
        ],
        compiler_params=params(58),
        cost_estimate=pl.CostEstimate(
            flops=8 * levels * patches * (width + count) * local,
            bytes_accessed=2 * levels * patches * (width + 2 * local) + 4 * width * local,
            transcendentals=0,
        ),
        name="norm_project",
    )(slots, tokens, gain.reshape(1, width), key_weight, value_weight)


def attend_kernel(query_ref, pair_ref, *out_refs):
    levels, slots, local = pair_ref.shape[1:]
    local = local // 2
    latents = query_ref.shape[0] // slots
    half = slots // len(out_refs)
    rows = GROUP * latents
    columns = levels * GROUP
    heads = LANES // HEAD_DIM
    lane_head = lax.broadcasted_iota(jnp.int32, (rows, LANES), 1) // HEAD_DIM
    row_slot = lax.broadcasted_iota(jnp.int32, (GROUP, heads * rows), 0)
    column_slot = (lax.broadcasted_iota(jnp.int32, (GROUP, heads * rows), 1) // latents) & (GROUP - 1)
    same = row_slot - column_slot == 0
    scale = math.log2(math.e) / math.sqrt(HEAD_DIM)
    queries = query_ref[...].astype(jnp.float32)

    tasks = [(start, lane) for start in range(0, slots, GROUP) for lane in range(0, local, LANES)]
    scores = []
    for start, lane in tasks:
        part = queries[start * latents : start * latents + rows, lane : lane + LANES]
        part = jnp.concatenate(
            [jnp.where(lane_head == head, part, 0.0).astype(jnp.bfloat16) for head in range(heads)], axis=0
        )
        keys = pair_ref[0, :, pl.ds(start, GROUP), pl.ds(lane, LANES)].reshape(columns, LANES)
        product = lax.dot_general(keys, part, (((1,), (1,)), ((), ())), preferred_element_type=jnp.float32)
        scores.append(product.reshape(levels, GROUP, heads * rows))
    softs = []
    for product in scores:
        expo = jnp.exp2((product - jnp.max(product, axis=0, keepdims=True)) * scale)
        inverse = jnp.where(same, 1.0 / jnp.sum(expo, axis=0), 0.0)
        softs.append((expo * inverse[None]).reshape(columns, heads * rows).astype(jnp.bfloat16))
    for (start, lane), soft in zip(tasks, softs):
        values = pair_ref[0, :, pl.ds(start, GROUP), pl.ds(local + lane, LANES)].reshape(columns, LANES)
        wide = lax.dot_general(soft, values, (((0,), (0,)), ((), ())), preferred_element_type=jnp.float32)
        mixed = wide[:rows]
        for head in range(1, heads):
            mixed = jnp.where(lane_head == head, wide[head * rows : (head + 1) * rows], mixed)
        part = pl.ds(start % half * latents, rows)
        out_refs[start // half][part, pl.ds(lane, LANES)] = mixed.astype(jnp.bfloat16)


def attend(queries, pairs, halves):
    total, local = queries.shape
    steps, levels = pairs.shape[:2]
    rows = total // steps
    return pl.pallas_call(
        attend_kernel,
        grid=(steps,),
        in_specs=[
            pl.BlockSpec((rows, local), lambda i: (i, 0)),
            pl.BlockSpec((1, levels, BLOCK, 2 * local), lambda i: (i, 0, 0, 0)),
        ],
        out_specs=[pl.BlockSpec((rows // halves, local), lambda i: (i, 0))] * halves,
        out_shape=[jax.ShapeDtypeStruct((total // halves, local), jnp.bfloat16)] * halves,
        compiler_params=params(55),
        cost_estimate=pl.CostEstimate(
            flops=64 * total * levels * GROUP * local,
            bytes_accessed=4 * steps * (rows + levels * BLOCK) * local,
            transcendentals=0,
        ),
        name="attend_slots",
    )(queries, pairs)


def combine_rows(mixed_refs, weight_refs, part):
    total = None
    for mixed_ref, weight_ref in zip(mixed_refs, weight_refs):
        term = jnp.dot(mixed_ref[part, :], weight_ref[...], preferred_element_type=jnp.float32)
        term = term.astype(jnp.bfloat16).astype(jnp.float32)
        total = term if total is None else total + term
    return total.astype(jnp.bfloat16)


def combine_home_kernel(place_ref, *refs):
    out_refs = refs[8:]
    steps, half, latents, local = out_refs[0].shape
    rows = half * latents
    for step in range(steps):
        for across, out_ref in enumerate(out_refs):
            owner = jnp.bitwise_xor(place_ref[0], 2 * step + across)
            part = pl.ds(pl.multiple_of(owner * rows, rows), rows)
            out_ref[step] = combine_rows(refs[:4], refs[4:8], part).reshape(half, latents, local)


def combine_kernel(place_ref, *refs):
    out_ref = refs[-1]
    stripes, caps, latents, local = out_ref.shape
    rest = refs[8:-1]
    half = caps if not rest else caps - rest[0].shape[1]
    for step, ref in enumerate(rest):
        for across in range(2):
            out_ref[jnp.bitwise_xor(place_ref[0], 2 * step + across), half:] = ref[across]
    for stripe in range(stripes):
        part = pl.ds(stripe * half * latents, half * latents)
        rows = combine_rows(refs[:4], refs[4:8], part)
        out_ref[stripe, :half] = rows.reshape(half, latents, local)


def combine(kernel, place, groups, weights, out_shape, rest=()):
    operands = (*groups, *weights, *rest)
    rows, local = groups[0].shape
    vmem = pl.BlockSpec(memory_space=pltpu.VMEM)
    return pl.pallas_call(
        kernel,
        in_specs=[pl.BlockSpec(memory_space=pltpu.SMEM)] + [vmem] * len(operands),
        out_specs=jax.tree.map(lambda _: vmem, out_shape),
        out_shape=out_shape,
        compiler_params=params(20),
        cost_estimate=pl.CostEstimate(
            flops=24 * rows * local * local, bytes_accessed=10 * rows * local, transcendentals=0
        ),
        name="combine_groups",
    )(place, *operands)


def swap(array, axis_name, distance):
    size = lax.axis_size(axis_name)
    return lax.ppermute(array, axis_name, [(i, i ^ distance) for i in range(size)])


def follow(array, *others):
    return lax.optimization_barrier((array, *others))[0]


def spread_heads(mixed, others=()):
    second = swap(mixed, "head", 2)
    return mixed, swap(mixed, "head", 1), second, swap(follow(second, *others), "head", 1)


def exchange(array, stripes):
    array = array.reshape(stripes, -1, *array.shape[1:])
    return lax.all_to_all(array, "lat", split_axis=0, concat_axis=0, tiled=True)


def spread_weight(out_weight, head):
    local = out_weight.shape[0]
    parts = []
    for distance in range(lax.axis_size("head")):
        start = jnp.bitwise_xor(head, distance) * local
        part = lax.dynamic_slice_in_dim(out_weight, start, local, 1)
        parts.append(swap(part, "head", distance) if distance else part)
    return parts


def shards(level_tokens, ln_gain, key_weight, value_weight, out_weight, ocean_queries, send_slots):
    stripes = lax.axis_size("lat")
    caps = send_slots.shape[2]
    shape = ocean_queries.shape
    slots, latents, local = shape
    place = lax.axis_index("lat").reshape(1)
    queries = exchange(ocean_queries, stripes).reshape(-1, local)
    weights = spread_weight(out_weight, lax.axis_index("head"))
    tokens = jnp.transpose(level_tokens, (1, 0, 2))
    pairs = project(send_slots[0], tokens, ln_gain, key_weight, value_weight)
    pairs, weights = lax.optimization_barrier((pairs, weights))
    whole = jax.ShapeDtypeStruct((stripes, caps, latents, local), jnp.bfloat16)
    if caps != BLOCK:
        (mixed,) = attend(queries, pairs, 1)
        mixed = exchange(mixed, stripes).reshape(-1, local)
        return combine(combine_kernel, place, spread_heads(mixed), weights, whole).reshape(shape)
    early, late = attend(queries, pairs, 2)
    chunks = [jax.ShapeDtypeStruct((stripes // 2, caps // 2, latents, local), jnp.bfloat16)] * 2
    same, other = combine(combine_home_kernel, place, spread_heads(late), weights, chunks)
    other = swap(other, "lat", 1)
    early = follow(exchange(early, stripes), other).reshape(-1, local)
    both = jnp.stack([same, other], axis=1)
    moved = [swap(both[step], "lat", 2 * step) for step in range(stripes // 2 - 1, 0, -1)]
    chunks = [both[0], *reversed(moved)]
    return combine(combine_kernel, place, spread_heads(early, moved), weights, whole, chunks).reshape(shape)


def solution(mesh):
    return jax.shard_map(
        shards,
        mesh=mesh,
        in_specs=(
            P("lat", None, None),
            P(),
            P(None, "head"),
            P(None, "head"),
            P("head", None),
            P("lat", None, "head"),
            P("lat", None, None),
        ),
        out_specs=P("lat", None, "head"),
        check_vma=False,
    )
```

```python
import functools
import math

import jax
import jax.numpy as jnp
from jax import lax
from jax.experimental import pallas as pl
from jax.experimental.pallas import tpu as pltpu
from jax.sharding import PartitionSpec as P

HEAD_DIM = 64
EPS = 1e-05
GROUP = 16
BLOCK = 64
STEP_BLOCKS = 2
ROWS = 32
LANES = 128
MIB = 1024 * 1024


def params(mib):
    return pltpu.CompilerParams(vmem_limit_bytes=mib * MIB)


def normalize_rows(tokens, gain):
    width = tokens.shape[-1]
    tokens = tokens.astype(jnp.float32)
    center = jnp.sum(tokens, axis=-1, keepdims=True) * (1.0 / width)
    shifted = tokens - center
    spread = jnp.sum(shifted * shifted, axis=-1, keepdims=True) * (1.0 / width)
    return (shifted * lax.rsqrt(spread + EPS) * gain).astype(jnp.bfloat16)


def build_pick(slots_ref, pick_ref, halves):
    stripes, caps = slots_ref.shape
    half = caps // halves
    diagonal = lax.broadcasted_iota(jnp.int32, (caps, caps), 0) == lax.broadcasted_iota(jnp.int32, (caps, caps), 1)
    patch = lax.broadcasted_iota(jnp.int32, (caps, pick_ref.shape[1]), 1)
    for owner in range(stripes):
        row = jnp.broadcast_to(slots_ref[owner : owner + 1, :], (caps, caps))
        column = jnp.sum(jnp.where(diagonal, row, 0), axis=-1, keepdims=True)
        pick = jnp.where(patch == column, 1.0, 0.0).astype(jnp.bfloat16)
        for index in range(halves):
            start = (index * stripes + owner) * half
            pick_ref[start : start + half, :] = pick[index * half : (index + 1) * half]


def project_kernel(
    halves,
    slots_ref,
    tokens_ref,
    gain_ref,
    key_weight_ref,
    value_weight_ref,
    out_ref,
    even_ref,
    odd_ref,
    pick_ref,
    weight_ref,
):
    step = pl.program_id(0)
    patches = tokens_ref.shape[1]
    local = key_weight_ref.shape[1]

    @pl.when(step == 0)
    def _():
        build_pick(slots_ref, pick_ref, halves)
        weight_ref[:, :local] = key_weight_ref[...]
        weight_ref[:, local:] = value_weight_ref[...]

    def stage(write_ref, read_ref):
        gain = gain_ref[...]
        product = jnp.dot(read_ref[...], weight_ref[...], preferred_element_type=jnp.float32).astype(jnp.bfloat16)
        picked = jnp.dot(pick_ref[...], product, preferred_element_type=jnp.float32).astype(jnp.bfloat16)
        out_ref[:, 0] = picked.reshape(out_ref.shape[0], BLOCK, out_ref.shape[-1])
        for start in range(0, patches, ROWS):
            part = pl.ds(start, ROWS)
            write_ref[part, :] = normalize_rows(tokens_ref[0, part, :], gain)

    @pl.when(step % 2 == 0)
    def _():
        stage(even_ref, odd_ref)

    @pl.when(step % 2 == 1)
    def _():
        stage(odd_ref, even_ref)


def project(slots, tokens, gain, key_weight, value_weight, halves):
    levels, patches, width = tokens.shape
    local = key_weight.shape[1]
    count = slots.size
    whole = lambda i: (0, 0)
    return pl.pallas_call(
        functools.partial(project_kernel, halves),
        grid=(levels + 1,),
        in_specs=[
            pl.BlockSpec(slots.shape, whole),
            pl.BlockSpec((1, patches, width), lambda i: (jnp.minimum(i, levels - 1), 0, 0)),
            pl.BlockSpec((1, width), whole),
            pl.BlockSpec((width, local), whole),
            pl.BlockSpec((width, local), whole),
        ],
        out_specs=pl.BlockSpec((count // BLOCK, 1, BLOCK, 2 * local), lambda i: (0, jnp.maximum(i - 1, 0), 0, 0)),
        out_shape=jax.ShapeDtypeStruct((count // BLOCK, levels, BLOCK, 2 * local), jnp.bfloat16),
        scratch_shapes=[
            pltpu.VMEM((patches, width), jnp.bfloat16),
            pltpu.VMEM((patches, width), jnp.bfloat16),
            pltpu.VMEM((count, patches), jnp.bfloat16),
            pltpu.VMEM((width, 2 * local), jnp.bfloat16),
        ],
        compiler_params=params(58),
        cost_estimate=pl.CostEstimate(
            flops=8 * levels * patches * (width + count) * local,
            bytes_accessed=2 * levels * patches * (width + 2 * local) + 4 * width * local,
            transcendentals=0,
        ),
        name="norm_project",
    )(slots, tokens, gain.reshape(1, width), key_weight, value_weight)


def attend_kernel(query_ref, pair_ref, *refs):
    out_ref = refs[-1]
    blocks, levels, block, local = pair_ref.shape
    slots, local = blocks * block, local // 2
    latents = out_ref.shape[0] // slots
    rows = GROUP * latents
    columns = levels * GROUP
    heads = LANES // HEAD_DIM
    lane_head = lax.broadcasted_iota(jnp.int32, (rows, LANES), 1) // HEAD_DIM
    row_slot = lax.broadcasted_iota(jnp.int32, (GROUP, heads * rows), 0)
    column_slot = (lax.broadcasted_iota(jnp.int32, (GROUP, heads * rows), 1) // latents) & (GROUP - 1)
    same = row_slot - column_slot == 0
    scale = math.log2(math.e) / math.sqrt(HEAD_DIM)
    queries = query_ref[...].reshape(slots * latents, local).astype(jnp.float32)

    for first in range(0, slots, block):
        tasks = [(start, lane) for start in range(first, first + block, GROUP) for lane in range(0, local, LANES)]
        scores = []
        for start, lane in tasks:
            part = queries[start * latents : start * latents + rows, lane : lane + LANES]
            part = jnp.concatenate(
                [jnp.where(lane_head == head, part, 0.0).astype(jnp.bfloat16) for head in range(heads)], axis=0
            )
            part_of = pl.ds(start % block, GROUP)
            keys = pair_ref[start // block, :, part_of, pl.ds(lane, LANES)].reshape(columns, LANES)
            product = lax.dot_general(keys, part, (((1,), (1,)), ((), ())), preferred_element_type=jnp.float32)
            scores.append(product.reshape(levels, GROUP, heads * rows))
        softs = []
        for product in scores:
            expo = jnp.exp2((product - jnp.max(product, axis=0, keepdims=True)) * scale)
            inverse = jnp.where(same, 1.0 / jnp.sum(expo, axis=0), 0.0)
            softs.append((expo * inverse[None]).reshape(columns, heads * rows).astype(jnp.bfloat16))
        for (start, lane), soft in zip(tasks, softs):
            part_of = pl.ds(start % block, GROUP)
            values = pair_ref[start // block, :, part_of, pl.ds(local + lane, LANES)].reshape(columns, LANES)
            wide = lax.dot_general(soft, values, (((0,), (0,)), ((), ())), preferred_element_type=jnp.float32)
            mixed = wide[:rows]
            for head in range(1, heads):
                mixed = jnp.where(lane_head == head, wide[head * rows : (head + 1) * rows], mixed)
            out_ref[pl.ds(start * latents, rows), pl.ds(lane, LANES)] = mixed.astype(jnp.bfloat16)


def attend(queries, pairs, index, after=()):
    stripes, halves, rows, local = queries.shape
    levels = pairs.shape[1]
    steps = pairs.shape[0] // halves // STEP_BLOCKS
    block = stripes * rows // steps
    return pl.pallas_call(
        attend_kernel,
        grid=(steps,),
        in_specs=[
            pl.BlockSpec((stripes // steps, 1, rows, local), lambda i: (i, index, 0, 0)),
            pl.BlockSpec((STEP_BLOCKS, levels, BLOCK, 2 * local), lambda i: (index * steps + i, 0, 0, 0)),
        ]
        + [pl.BlockSpec(memory_space=pl.ANY)] * len(after),
        out_specs=pl.BlockSpec((block, local), lambda i: (i, 0)),
        out_shape=jax.ShapeDtypeStruct((steps * block, local), jnp.bfloat16),
        compiler_params=params(55),
        cost_estimate=pl.CostEstimate(
            flops=64 * steps * block * levels * GROUP * local,
            bytes_accessed=4 * steps * (block + levels * STEP_BLOCKS * BLOCK) * local,
            transcendentals=0,
        ),
        name="attend_slots",
    )(queries, pairs, *after)


def combine_rows(mixed_refs, weight_refs, part):
    total = None
    for mixed_ref, weight_ref in zip(mixed_refs, weight_refs):
        term = jnp.dot(mixed_ref[part, :], weight_ref[...], preferred_element_type=jnp.float32)
        term = term.astype(jnp.bfloat16).astype(jnp.float32)
        total = term if total is None else total + term
    return total.astype(jnp.bfloat16)


def combine_home_kernel(place_ref, *refs):
    for distance, out_ref in enumerate(refs[8:]):
        rows = out_ref.shape[0] * out_ref.shape[1]
        start = jnp.bitwise_xor(place_ref[0], distance) * rows
        part = pl.ds(pl.multiple_of(start, rows), rows)
        out_ref[...] = combine_rows(refs[:4], refs[4:8], part).reshape(out_ref.shape)


def combine_kernel(place_ref, *refs):
    out_ref = refs[-1]
    stripes, caps, latents, local = out_ref.shape
    rest = refs[8:-1]
    half = caps - sum(ref.shape[0] for ref in rest[:1])
    for distance, ref in enumerate(rest):
        out_ref[jnp.bitwise_xor(place_ref[0], distance), half:] = ref[...]
    for stripe in range(stripes):
        part = pl.ds(stripe * half * latents, half * latents)
        rows = combine_rows(refs[:4], refs[4:8], part)
        out_ref[stripe, :half] = rows.reshape(half, latents, local)


def combine(kernel, place, groups, weights, out_shape, rest=()):
    operands = (*groups, *weights, *rest)
    rows, local = groups[0].shape
    vmem = pl.BlockSpec(memory_space=pltpu.VMEM)
    return pl.pallas_call(
        kernel,
        in_specs=[pl.BlockSpec(memory_space=pltpu.SMEM)] + [vmem] * len(operands),
        out_specs=jax.tree.map(lambda _: vmem, out_shape),
        out_shape=out_shape,
        compiler_params=params(20),
        cost_estimate=pl.CostEstimate(
            flops=24 * rows * local * local, bytes_accessed=10 * rows * local, transcendentals=0
        ),
        name="combine_groups",
    )(place, *operands)


def swap(array, axis_name, distance):
    size = lax.axis_size(axis_name)
    return lax.ppermute(array, axis_name, [(i, i ^ distance) for i in range(size)])


def follow(array, *others):
    return lax.optimization_barrier((array, *others))[0]


def spread_heads(mixed, others=()):
    second = swap(mixed, "head", 2)
    return mixed, swap(mixed, "head", 1), second, swap(follow(second, *others), "head", 1)


def exchange(array, stripes):
    array = array.reshape(stripes, -1, *array.shape[1:])
    return lax.all_to_all(array, "lat", split_axis=0, concat_axis=0, tiled=True)


def spread_weight(out_weight, head):
    local = out_weight.shape[0]
    parts = []
    for distance in range(lax.axis_size("head")):
        start = jnp.bitwise_xor(head, distance) * local
        part = lax.dynamic_slice_in_dim(out_weight, start, local, 1)
        parts.append(swap(part, "head", distance) if distance else part)
    return parts


def shards(level_tokens, ln_gain, key_weight, value_weight, out_weight, ocean_queries, send_slots):
    stripes = lax.axis_size("lat")
    caps = send_slots.shape[2]
    shape = ocean_queries.shape
    slots, latents, local = shape
    place = lax.axis_index("lat").reshape(1)
    halves = 2 if caps == BLOCK else 1
    queries = exchange(ocean_queries, stripes).reshape(stripes, halves, -1, local)
    weights = spread_weight(out_weight, lax.axis_index("head"))
    tokens = jnp.transpose(level_tokens, (1, 0, 2))
    pairs = project(send_slots[0], tokens, ln_gain, key_weight, value_weight, halves)
    pairs, weights = lax.optimization_barrier((pairs, weights))
    whole = jax.ShapeDtypeStruct((stripes, caps, latents, local), jnp.bfloat16)
    if halves == 1:
        mixed = exchange(attend(queries, pairs, 0), stripes).reshape(-1, local)
        return combine(combine_kernel, place, spread_heads(mixed), weights, whole).reshape(shape)
    late = attend(queries, pairs, 1)
    early = attend(queries, pairs, 0, (late,))
    chunks = [jax.ShapeDtypeStruct((caps // 2, latents, local), jnp.bfloat16)] * stripes
    chunks = combine(combine_home_kernel, place, spread_heads(late, (early,)), weights, chunks)
    chunks = [swap(chunk, "lat", distance) if distance else chunk for distance, chunk in enumerate(chunks)]
    near, far = chunks[: stripes // 2], chunks[stripes // 2 :]
    early = follow(exchange(early, stripes), *near).reshape(-1, local)
    return combine(combine_kernel, place, spread_heads(early, far), weights, whole, chunks).reshape(shape)


def solution(mesh):
    return jax.shard_map(
        shards,
        mesh=mesh,
        in_specs=(
            P("lat", None, None),
            P(),
            P(None, "head"),
            P(None, "head"),
            P("head", None),
            P("lat", None, "head"),
            P("lat", None, None),
        ),
        out_specs=P("lat", None, "head"),
        check_vma=False,
    )
```

```python
import functools
import math

import jax
import jax.numpy as jnp
from jax import lax
from jax.experimental import pallas as pl
from jax.experimental.pallas import tpu as pltpu
from jax.sharding import PartitionSpec as P

HEAD_DIM = 64
EPS = 1e-05
GROUP = 16
BLOCK = 64
STEP_BLOCKS = 2
ROWS = 32
LANES = 128
MIB = 1024 * 1024


def params(mib):
    return pltpu.CompilerParams(vmem_limit_bytes=mib * MIB)


def normalize_rows(tokens, gain):
    width = tokens.shape[-1]
    tokens = tokens.astype(jnp.float32)
    center = jnp.sum(tokens, axis=-1, keepdims=True) * (1.0 / width)
    shifted = tokens - center
    spread = jnp.sum(shifted * shifted, axis=-1, keepdims=True) * (1.0 / width)
    return (shifted * lax.rsqrt(spread + EPS) * gain).astype(jnp.bfloat16)


def build_pick(slots_ref, pick_ref, halves):
    stripes, caps = slots_ref.shape
    half = caps // halves
    diagonal = lax.broadcasted_iota(jnp.int32, (caps, caps), 0) == lax.broadcasted_iota(jnp.int32, (caps, caps), 1)
    patch = lax.broadcasted_iota(jnp.int32, (caps, pick_ref.shape[1]), 1)
    for owner in range(stripes):
        row = jnp.broadcast_to(slots_ref[owner : owner + 1, :], (caps, caps))
        column = jnp.sum(jnp.where(diagonal, row, 0), axis=-1, keepdims=True)
        pick = jnp.where(patch == column, 1.0, 0.0).astype(jnp.bfloat16)
        for index in range(halves):
            start = (index * stripes + owner) * half
            pick_ref[start : start + half, :] = pick[index * half : (index + 1) * half]


def project_kernel(
    halves,
    slots_ref,
    gain_ref,
    key_weight_ref,
    value_weight_ref,
    even_ref,
    odd_ref,
    even_out_ref,
    odd_out_ref,
    normed_ref,
    pick_ref,
    weight_ref,
):
    patches = even_ref.shape[1]
    local = key_weight_ref.shape[1]

    @pl.when(pl.program_id(0) == 0)
    def _():
        build_pick(slots_ref, pick_ref, halves)
        weight_ref[:, :local] = key_weight_ref[...]
        weight_ref[:, local:] = value_weight_ref[...]

    gain = gain_ref[...]
    for index, tokens_ref in enumerate((even_ref, odd_ref)):
        for start in range(0, patches, ROWS):
            normed = normalize_rows(tokens_ref[0, pl.ds(start, ROWS), :], gain)
            normed_ref[pl.ds(index * patches + start, ROWS), :] = normed
    product = jnp.dot(normed_ref[...], weight_ref[...], preferred_element_type=jnp.float32).astype(jnp.bfloat16)
    product = jnp.concatenate([product[:patches], product[patches:]], axis=1)
    picked = jnp.dot(pick_ref[...], product, preferred_element_type=jnp.float32).astype(jnp.bfloat16)
    for index, out_ref in enumerate((even_out_ref, odd_out_ref)):
        part = picked[:, index * 2 * local : (index + 1) * 2 * local]
        out_ref[:, 0] = part.reshape(out_ref.shape[0], BLOCK, 2 * local)


def project(slots, tokens, gain, key_weight, value_weight, halves):
    levels, patches, width = tokens.shape
    local = key_weight.shape[1]
    count = slots.size
    steps = (levels + 1) // 2
    whole = lambda i: (0, 0)
    return pl.pallas_call(
        functools.partial(project_kernel, halves),
        grid=(steps,),
        in_specs=[
            pl.BlockSpec(slots.shape, whole),
            pl.BlockSpec((1, width), whole),
            pl.BlockSpec((width, local), whole),
            pl.BlockSpec((width, local), whole),
            pl.BlockSpec((1, patches, width), lambda i: (2 * i, 0, 0)),
            pl.BlockSpec((1, patches, width), lambda i: (jnp.minimum(2 * i + 1, levels - 1), 0, 0)),
        ],
        out_specs=[pl.BlockSpec((count // BLOCK, 1, BLOCK, 2 * local), lambda i: (0, i, 0, 0))] * 2,
        out_shape=[jax.ShapeDtypeStruct((count // BLOCK, steps, BLOCK, 2 * local), jnp.bfloat16)] * 2,
        scratch_shapes=[
            pltpu.VMEM((2 * patches, width), jnp.bfloat16),
            pltpu.VMEM((count, patches), jnp.bfloat16),
            pltpu.VMEM((width, 2 * local), jnp.bfloat16),
        ],
        compiler_params=params(58),
        cost_estimate=pl.CostEstimate(
            flops=8 * levels * patches * (width + count) * local,
            bytes_accessed=2 * levels * patches * (width + 2 * local) + 4 * width * local,
            transcendentals=0,
        ),
        name="norm_project",
    )(slots, gain.reshape(1, width), key_weight, value_weight, tokens, tokens)


def attend_kernel(levels, query_ref, even_ref, odd_ref, *refs):
    out_ref = refs[-1]
    blocks, _, block, local = even_ref.shape
    slots, local = blocks * block, local // 2
    latents = out_ref.shape[0] // slots
    rows = GROUP * latents
    columns = levels * GROUP
    heads = LANES // HEAD_DIM
    lane_head = lax.broadcasted_iota(jnp.int32, (rows, LANES), 1) // HEAD_DIM
    row_slot = lax.broadcasted_iota(jnp.int32, (GROUP, heads * rows), 0)
    column_slot = (lax.broadcasted_iota(jnp.int32, (GROUP, heads * rows), 1) // latents) & (GROUP - 1)
    same = row_slot - column_slot == 0
    scale = math.log2(math.e) / math.sqrt(HEAD_DIM)
    queries = query_ref[...].reshape(slots * latents, local).astype(jnp.float32)

    def columns_of(start, lane):
        index = (start // block, slice(None), pl.ds(start % block, GROUP), pl.ds(lane, LANES))
        pieces = [even_ref[index], odd_ref[index][: levels // 2]]
        return jnp.concatenate(pieces, axis=0).reshape(columns, LANES)

    for first in range(0, slots, block):
        tasks = [(start, lane) for start in range(first, first + block, GROUP) for lane in range(0, local, LANES)]
        scores = []
        for start, lane in tasks:
            part = queries[start * latents : start * latents + rows, lane : lane + LANES]
            part = jnp.concatenate(
                [jnp.where(lane_head == head, part, 0.0).astype(jnp.bfloat16) for head in range(heads)], axis=0
            )
            keys = columns_of(start, lane)
            product = lax.dot_general(keys, part, (((1,), (1,)), ((), ())), preferred_element_type=jnp.float32)
            scores.append(product.reshape(levels, GROUP, heads * rows))
        softs = []
        for product in scores:
            expo = jnp.exp2((product - jnp.max(product, axis=0, keepdims=True)) * scale)
            inverse = jnp.where(same, 1.0 / jnp.sum(expo, axis=0), 0.0)
            softs.append((expo * inverse[None]).reshape(columns, heads * rows).astype(jnp.bfloat16))
        for (start, lane), soft in zip(tasks, softs):
            values = columns_of(start, local + lane)
            wide = lax.dot_general(soft, values, (((0,), (0,)), ((), ())), preferred_element_type=jnp.float32)
            mixed = wide[:rows]
            for head in range(1, heads):
                mixed = jnp.where(lane_head == head, wide[head * rows : (head + 1) * rows], mixed)
            out_ref[pl.ds(start * latents, rows), pl.ds(lane, LANES)] = mixed.astype(jnp.bfloat16)


def attend(queries, pairs, levels, index, after=()):
    stripes, halves, rows, local = queries.shape
    steps = pairs[0].shape[0] // halves // STEP_BLOCKS
    block = stripes * rows // steps
    pair_spec = pl.BlockSpec(
        (STEP_BLOCKS, pairs[0].shape[1], BLOCK, 2 * local), lambda i: (index * steps + i, 0, 0, 0)
    )
    return pl.pallas_call(
        functools.partial(attend_kernel, levels),
        grid=(steps,),
        in_specs=[
            pl.BlockSpec((stripes // steps, 1, rows, local), lambda i: (i, index, 0, 0)),
            pair_spec,
            pair_spec,
        ]
        + [pl.BlockSpec(memory_space=pl.ANY)] * len(after),
        out_specs=pl.BlockSpec((block, local), lambda i: (i, 0)),
        out_shape=jax.ShapeDtypeStruct((steps * block, local), jnp.bfloat16),
        compiler_params=params(55),
        cost_estimate=pl.CostEstimate(
            flops=64 * steps * block * levels * GROUP * local,
            bytes_accessed=4 * steps * (block + levels * STEP_BLOCKS * BLOCK) * local,
            transcendentals=0,
        ),
        name="attend_slots",
    )(queries, *pairs, *after)


def combine_rows(mixed_refs, weight_refs, part):
    total = None
    for mixed_ref, weight_ref in zip(mixed_refs, weight_refs):
        term = jnp.dot(mixed_ref[part, :], weight_ref[...], preferred_element_type=jnp.float32)
        term = term.astype(jnp.bfloat16).astype(jnp.float32)
        total = term if total is None else total + term
    return total.astype(jnp.bfloat16)


def combine_home_kernel(place_ref, *refs):
    for distance, out_ref in enumerate(refs[8:]):
        rows = out_ref.shape[0] * out_ref.shape[1]
        start = jnp.bitwise_xor(place_ref[0], distance) * rows
        part = pl.ds(pl.multiple_of(start, rows), rows)
        out_ref[...] = combine_rows(refs[:4], refs[4:8], part).reshape(out_ref.shape)


def combine_kernel(place_ref, *refs):
    out_ref = refs[-1]
    stripes, caps, latents, local = out_ref.shape
    rest = refs[8:-1]
    half = caps - sum(ref.shape[0] for ref in rest[:1])
    for distance, ref in enumerate(rest):
        out_ref[jnp.bitwise_xor(place_ref[0], distance), half:] = ref[...]
    for stripe in range(stripes):
        part = pl.ds(stripe * half * latents, half * latents)
        rows = combine_rows(refs[:4], refs[4:8], part)
        out_ref[stripe, :half] = rows.reshape(half, latents, local)


def combine(kernel, place, groups, weights, out_shape, rest=()):
    operands = (*groups, *weights, *rest)
    rows, local = groups[0].shape
    vmem = pl.BlockSpec(memory_space=pltpu.VMEM)
    return pl.pallas_call(
        kernel,
        in_specs=[pl.BlockSpec(memory_space=pltpu.SMEM)] + [vmem] * len(operands),
        out_specs=jax.tree.map(lambda _: vmem, out_shape),
        out_shape=out_shape,
        compiler_params=params(20),
        cost_estimate=pl.CostEstimate(
            flops=24 * rows * local * local, bytes_accessed=10 * rows * local, transcendentals=0
        ),
        name="combine_groups",
    )(place, *operands)


def swap(array, axis_name, distance):
    size = lax.axis_size(axis_name)
    return lax.ppermute(array, axis_name, [(i, i ^ distance) for i in range(size)])


def follow(array, *others):
    return lax.optimization_barrier((array, *others))[0]


def spread_heads(mixed, others=()):
    second = swap(mixed, "head", 2)
    return mixed, swap(mixed, "head", 1), second, swap(follow(second, *others), "head", 1)


def exchange(array, stripes):
    array = array.reshape(stripes, -1, *array.shape[1:])
    return lax.all_to_all(array, "lat", split_axis=0, concat_axis=0, tiled=True)


def spread_weight(out_weight, head):
    local = out_weight.shape[0]
    parts = []
    for distance in range(lax.axis_size("head")):
        start = jnp.bitwise_xor(head, distance) * local
        part = lax.dynamic_slice_in_dim(out_weight, start, local, 1)
        parts.append(swap(part, "head", distance) if distance else part)
    return parts


def shards(level_tokens, ln_gain, key_weight, value_weight, out_weight, ocean_queries, send_slots):
    stripes = lax.axis_size("lat")
    caps = send_slots.shape[2]
    shape = ocean_queries.shape
    slots, latents, local = shape
    place = lax.axis_index("lat").reshape(1)
    halves = 2 if caps == BLOCK else 1
    queries = exchange(ocean_queries, stripes).reshape(stripes, halves, -1, local)
    weights = spread_weight(out_weight, lax.axis_index("head"))
    tokens = jnp.transpose(level_tokens, (1, 0, 2))
    levels = tokens.shape[0]
    pairs = project(send_slots[0], tokens, ln_gain, key_weight, value_weight, halves)
    pairs, weights = lax.optimization_barrier((tuple(pairs), weights))
    whole = jax.ShapeDtypeStruct((stripes, caps, latents, local), jnp.bfloat16)
    if halves == 1:
        mixed = exchange(attend(queries, pairs, levels, 0), stripes).reshape(-1, local)
        return combine(combine_kernel, place, spread_heads(mixed), weights, whole).reshape(shape)
    late = attend(queries, pairs, levels, 1)
    early = attend(queries, pairs, levels, 0, (late,))
    chunks = [jax.ShapeDtypeStruct((caps // 2, latents, local), jnp.bfloat16)] * stripes
    chunks = combine(combine_home_kernel, place, spread_heads(late, (early,)), weights, chunks)
    chunks = [swap(chunk, "lat", distance) if distance else chunk for distance, chunk in enumerate(chunks)]
    near, far = chunks[: stripes // 2], chunks[stripes // 2 :]
    early = follow(exchange(early, stripes), *near).reshape(-1, local)
    return combine(combine_kernel, place, spread_heads(early, far), weights, whole, chunks).reshape(shape)


def solution(mesh):
    return jax.shard_map(
        shards,
        mesh=mesh,
        in_specs=(
            P("lat", None, None),
            P(),
            P(None, "head"),
            P(None, "head"),
            P("head", None),
            P("lat", None, "head"),
            P("lat", None, None),
        ),
        out_specs=P("lat", None, "head"),
        check_vma=False,
    )
```

```python
import functools
import math

import jax
import jax.numpy as jnp
from jax import lax
from jax.experimental import pallas as pl
from jax.experimental.pallas import tpu as pltpu
from jax.sharding import PartitionSpec as P

HEAD_DIM = 64
EPS = 1e-05
GROUP = 8
BLOCK = 64
STEP_BLOCKS = 2
ROWS = 32
MIB = 1024 * 1024


def params(mib):
    return pltpu.CompilerParams(vmem_limit_bytes=mib * MIB)


def normalize_rows(tokens, gain):
    width = tokens.shape[-1]
    tokens = tokens.astype(jnp.float32)
    center = jnp.sum(tokens, axis=-1, keepdims=True) * (1.0 / width)
    shifted = tokens - center
    spread = jnp.sum(shifted * shifted, axis=-1, keepdims=True) * (1.0 / width)
    return (shifted * lax.rsqrt(spread + EPS) * gain).astype(jnp.bfloat16)


def build_pick(slots_ref, pick_ref, halves):
    stripes, caps = slots_ref.shape
    half = caps // halves
    diagonal = lax.broadcasted_iota(jnp.int32, (caps, caps), 0) == lax.broadcasted_iota(jnp.int32, (caps, caps), 1)
    patch = lax.broadcasted_iota(jnp.int32, (caps, pick_ref.shape[1]), 1)
    for owner in range(stripes):
        row = jnp.broadcast_to(slots_ref[owner : owner + 1, :], (caps, caps))
        column = jnp.sum(jnp.where(diagonal, row, 0), axis=-1, keepdims=True)
        pick = jnp.where(patch == column, 1.0, 0.0).astype(jnp.bfloat16)
        for index in range(halves):
            start = (index * stripes + owner) * half
            pick_ref[start : start + half, :] = pick[index * half : (index + 1) * half]


def project_kernel(
    halves,
    slots_ref,
    gain_ref,
    key_weight_ref,
    value_weight_ref,
    even_ref,
    odd_ref,
    out_ref,
    normed_ref,
    pick_ref,
    weight_ref,
):
    patches = even_ref.shape[1]
    local = key_weight_ref.shape[1]

    @pl.when(pl.program_id(0) == 0)
    def _():
        build_pick(slots_ref, pick_ref, halves)
        weight_ref[:, :local] = key_weight_ref[...]
        weight_ref[:, local:] = value_weight_ref[...]

    gain = gain_ref[...]
    for index, tokens_ref in enumerate((even_ref, odd_ref)):
        for start in range(0, patches, ROWS):
            normed = normalize_rows(tokens_ref[0, pl.ds(start, ROWS), :], gain)
            normed_ref[pl.ds(index * patches + start, ROWS), :] = normed
    product = jnp.dot(normed_ref[...], weight_ref[...], preferred_element_type=jnp.float32).astype(jnp.bfloat16)
    product = jnp.concatenate([product[:patches], product[patches:]], axis=1)
    picked = jnp.dot(pick_ref[...], product, preferred_element_type=jnp.float32)
    groups = picked.shape[0] // GROUP
    picked = [
        picked[:, index * 2 * local : (index + 1) * 2 * local].reshape(groups, 1, GROUP, 2 * local) for index in range(2)
    ]
    picked = jnp.concatenate(picked, axis=1).reshape(out_ref.shape[0], 2 * BLOCK, 2 * local)
    out_ref[:, 0] = picked.astype(jnp.bfloat16)


def project(slots, tokens, gain, key_weight, value_weight, halves):
    levels, patches, width = tokens.shape
    local = key_weight.shape[1]
    count = slots.size
    steps = (levels + 1) // 2
    whole = lambda i: (0, 0)
    return pl.pallas_call(
        functools.partial(project_kernel, halves),
        grid=(steps,),
        in_specs=[
            pl.BlockSpec(slots.shape, whole),
            pl.BlockSpec((1, width), whole),
            pl.BlockSpec((width, local), whole),
            pl.BlockSpec((width, local), whole),
            pl.BlockSpec((1, patches, width), lambda i: (2 * i, 0, 0)),
            pl.BlockSpec((1, patches, width), lambda i: (jnp.minimum(2 * i + 1, levels - 1), 0, 0)),
        ],
        out_specs=pl.BlockSpec((count // BLOCK, 1, 2 * BLOCK, 2 * local), lambda i: (0, i, 0, 0)),
        out_shape=jax.ShapeDtypeStruct((count // BLOCK, steps, 2 * BLOCK, 2 * local), jnp.bfloat16),
        scratch_shapes=[
            pltpu.VMEM((2 * patches, width), jnp.bfloat16),
            pltpu.VMEM((count, patches), jnp.bfloat16),
            pltpu.VMEM((width, 2 * local), jnp.bfloat16),
        ],
        compiler_params=params(58),
        cost_estimate=pl.CostEstimate(
            flops=8 * levels * patches * (width + count) * local,
            bytes_accessed=2 * levels * patches * (width + 2 * local) + 4 * width * local,
            transcendentals=0,
        ),
        name="norm_project",
    )(slots, gain.reshape(1, width), key_weight, value_weight, tokens, tokens)


def attend_kernel(levels, query_ref, pair_ref, *refs):
    out_ref = refs[-1]
    blocks, level_pairs, block, local = pair_ref.shape
    block, local = block // 2, local // 2
    slots = blocks * block
    latents = out_ref.shape[0] // slots
    rows = GROUP * latents
    heads = local // HEAD_DIM
    columns = level_pairs * 2 * GROUP
    lane_head = lax.broadcasted_iota(jnp.int32, (rows, local), 1) // HEAD_DIM
    row_slot = lax.broadcasted_iota(jnp.int32, (GROUP, heads * rows), 0)
    column_slot = (lax.broadcasted_iota(jnp.int32, (GROUP, heads * rows), 1) // latents) & (GROUP - 1)
    same = row_slot - column_slot == 0
    scale = math.log2(math.e) / math.sqrt(HEAD_DIM)
    queries = query_ref[...].reshape(slots * latents, local).astype(jnp.float32)

    def columns_of(start, lane):
        part = pl.ds(start % block * 2, 2 * GROUP)
        return pair_ref[start // block, :, part, pl.ds(lane, local)].reshape(columns, local)

    for first in range(0, slots, block):
        tasks = range(first, first + block, GROUP)
        scores = []
        for start in tasks:
            part = queries[start * latents : start * latents + rows]
            part = jnp.concatenate(
                [jnp.where(lane_head == head, part, 0.0).astype(jnp.bfloat16) for head in range(heads)], axis=0
            )
            product = lax.dot_general(
                columns_of(start, 0), part, (((1,), (1,)), ((), ())), preferred_element_type=jnp.float32
            )
            scores.append(product.reshape(2 * level_pairs, GROUP, heads * rows))
        softs = []
        for product in scores:
            product = product[:levels]
            expo = jnp.exp2((product - jnp.max(product, axis=0, keepdims=True)) * scale)
            inverse = jnp.where(same, 1.0 / jnp.sum(expo, axis=0), 0.0)
            soft = expo * inverse[None]
            if levels < 2 * level_pairs:
                soft = jnp.concatenate([soft, jnp.zeros_like(soft[:1])], axis=0)
            softs.append(soft.reshape(columns, heads * rows).astype(jnp.bfloat16))
        for start, soft in zip(tasks, softs):
            wide = lax.dot_general(
                soft, columns_of(start, local), (((0,), (0,)), ((), ())), preferred_element_type=jnp.float32
            )
            mixed = wide[:rows]
            for head in range(1, heads):
                mixed = jnp.where(lane_head == head, wide[head * rows : (head + 1) * rows], mixed)
            out_ref[pl.ds(start * latents, rows), :] = mixed.astype(jnp.bfloat16)


def attend(queries, pairs, levels, index, after=()):
    stripes, halves, rows, local = queries.shape
    steps = pairs.shape[0] // halves // STEP_BLOCKS
    block = stripes * rows // steps
    pair_shape = (STEP_BLOCKS, *pairs.shape[1:])
    return pl.pallas_call(
        functools.partial(attend_kernel, levels),
        grid=(steps,),
        in_specs=[
            pl.BlockSpec((stripes // steps, 1, rows, local), lambda i: (i, index, 0, 0)),
            pl.BlockSpec(pair_shape, lambda i: (index * steps + i, 0, 0, 0)),
        ]
        + [pl.BlockSpec(memory_space=pl.ANY)] * len(after),
        out_specs=pl.BlockSpec((block, local), lambda i: (i, 0)),
        out_shape=jax.ShapeDtypeStruct((steps * block, local), jnp.bfloat16),
        compiler_params=params(55),
        cost_estimate=pl.CostEstimate(
            flops=1024 * steps * block * levels * local,
            bytes_accessed=4 * steps * (block + levels * STEP_BLOCKS * BLOCK) * local,
            transcendentals=0,
        ),
        name="attend_slots",
    )(queries, pairs, *after)


def combine_rows(mixed_refs, weight_refs, part):
    total = None
    for mixed_ref, weight_ref in zip(mixed_refs, weight_refs):
        term = jnp.dot(mixed_ref[part, :], weight_ref[...], preferred_element_type=jnp.float32)
        term = term.astype(jnp.bfloat16).astype(jnp.float32)
        total = term if total is None else total + term
    return total.astype(jnp.bfloat16)


def combine_home_kernel(place_ref, *refs):
    for distance, out_ref in enumerate(refs[8:]):
        rows = out_ref.shape[0] * out_ref.shape[1]
        start = jnp.bitwise_xor(place_ref[0], distance) * rows
        part = pl.ds(pl.multiple_of(start, rows), rows)
        out_ref[...] = combine_rows(refs[:4], refs[4:8], part).reshape(out_ref.shape)


def combine_kernel(place_ref, *refs):
    out_ref = refs[-1]
    stripes, caps, latents, local = out_ref.shape
    rest = refs[8:-1]
    half = caps - sum(ref.shape[0] for ref in rest[:1])
    for distance, ref in enumerate(rest):
        out_ref[jnp.bitwise_xor(place_ref[0], distance), half:] = ref[...]
    for stripe in range(stripes):
        part = pl.ds(stripe * half * latents, half * latents)
        rows = combine_rows(refs[:4], refs[4:8], part)
        out_ref[stripe, :half] = rows.reshape(half, latents, local)


def combine(kernel, place, groups, weights, out_shape, rest=()):
    operands = (*groups, *weights, *rest)
    rows, local = groups[0].shape
    vmem = pl.BlockSpec(memory_space=pltpu.VMEM)
    return pl.pallas_call(
        kernel,
        in_specs=[pl.BlockSpec(memory_space=pltpu.SMEM)] + [vmem] * len(operands),
        out_specs=jax.tree.map(lambda _: vmem, out_shape),
        out_shape=out_shape,
        compiler_params=params(20),
        cost_estimate=pl.CostEstimate(
            flops=24 * rows * local * local, bytes_accessed=10 * rows * local, transcendentals=0
        ),
        name="combine_groups",
    )(place, *operands)


def swap(array, axis_name, distance):
    size = lax.axis_size(axis_name)
    return lax.ppermute(array, axis_name, [(i, i ^ distance) for i in range(size)])


def follow(array, *others):
    return lax.optimization_barrier((array, *others))[0]


def spread_heads(mixed, others=()):
    second = swap(mixed, "head", 2)
    return mixed, swap(mixed, "head", 1), second, swap(follow(second, *others), "head", 1)


def exchange(array, stripes):
    array = array.reshape(stripes, -1, *array.shape[1:])
    return lax.all_to_all(array, "lat", split_axis=0, concat_axis=0, tiled=True)


def spread_weight(out_weight, head):
    local = out_weight.shape[0]
    parts = []
    for distance in range(lax.axis_size("head")):
        start = jnp.bitwise_xor(head, distance) * local
        part = lax.dynamic_slice_in_dim(out_weight, start, local, 1)
        parts.append(swap(part, "head", distance) if distance else part)
    return parts


def shards(level_tokens, ln_gain, key_weight, value_weight, out_weight, ocean_queries, send_slots):
    stripes = lax.axis_size("lat")
    caps = send_slots.shape[2]
    shape = ocean_queries.shape
    slots, latents, local = shape
    place = lax.axis_index("lat").reshape(1)
    halves = 2 if caps == BLOCK else 1
    queries = exchange(ocean_queries, stripes).reshape(stripes, halves, -1, local)
    weights = spread_weight(out_weight, lax.axis_index("head"))
    tokens = jnp.transpose(level_tokens, (1, 0, 2))
    levels = tokens.shape[0]
    pairs = project(send_slots[0], tokens, ln_gain, key_weight, value_weight, halves)
    pairs, weights = lax.optimization_barrier((pairs, weights))
    whole = jax.ShapeDtypeStruct((stripes, caps, latents, local), jnp.bfloat16)
    if halves == 1:
        mixed = exchange(attend(queries, pairs, levels, 0), stripes).reshape(-1, local)
        return combine(combine_kernel, place, spread_heads(mixed), weights, whole).reshape(shape)
    late = attend(queries, pairs, levels, 1)
    early = attend(queries, pairs, levels, 0, (late,))
    chunks = [jax.ShapeDtypeStruct((caps // 2, latents, local), jnp.bfloat16)] * stripes
    chunks = combine(combine_home_kernel, place, spread_heads(late, (early,)), weights, chunks)
    chunks = [swap(chunk, "lat", distance) if distance else chunk for distance, chunk in enumerate(chunks)]
    near, far = chunks[: stripes // 2], chunks[stripes // 2 :]
    early = follow(exchange(early, stripes), *near).reshape(-1, local)
    return combine(combine_kernel, place, spread_heads(early, far), weights, whole, chunks).reshape(shape)


def solution(mesh):
    return jax.shard_map(
        shards,
        mesh=mesh,
        in_specs=(
            P("lat", None, None),
            P(),
            P(None, "head"),
            P(None, "head"),
            P("head", None),
            P("lat", None, "head"),
            P("lat", None, None),
        ),
        out_specs=P("lat", None, "head"),
        check_vma=False,
    )
```

```python
import functools
import math

import jax
import jax.numpy as jnp
from jax import lax
from jax.experimental import pallas as pl
from jax.experimental.pallas import tpu as pltpu
from jax.sharding import PartitionSpec as P

HEAD_DIM = 64
EPS = 1e-05
GROUP = 8
BLOCK = 32
STEPS = 2
ROWS = 32
MIB = 1024 * 1024


def params(mib):
    return pltpu.CompilerParams(vmem_limit_bytes=mib * MIB)


def normalize_rows(tokens, gain):
    width = tokens.shape[-1]
    tokens = tokens.astype(jnp.float32)
    center = jnp.sum(tokens, axis=-1, keepdims=True) * (1.0 / width)
    shifted = tokens - center
    spread = jnp.sum(shifted * shifted, axis=-1, keepdims=True) * (1.0 / width)
    return (shifted * lax.rsqrt(spread + EPS) * gain).astype(jnp.bfloat16)


def build_pick(slots_ref, pick_ref, sizes):
    stripes, caps = slots_ref.shape
    diagonal = lax.broadcasted_iota(jnp.int32, (caps, caps), 0) == lax.broadcasted_iota(jnp.int32, (caps, caps), 1)
    patch = lax.broadcasted_iota(jnp.int32, (caps, pick_ref.shape[1]), 1)
    for owner in range(stripes):
        row = jnp.broadcast_to(slots_ref[owner : owner + 1, :], (caps, caps))
        column = jnp.sum(jnp.where(diagonal, row, 0), axis=-1, keepdims=True)
        pick = jnp.where(patch == column, 1.0, 0.0).astype(jnp.bfloat16)
        first = 0
        for size in sizes:
            start = first * stripes + owner * size
            pick_ref[start : start + size, :] = pick[first : first + size]
            first += size


def project_kernel(
    sizes,
    slots_ref,
    gain_ref,
    key_weight_ref,
    value_weight_ref,
    even_ref,
    odd_ref,
    *refs,
):
    out_refs, (normed_ref, pick_ref, weight_ref) = refs[: len(sizes)], refs[len(sizes) :]
    patches = even_ref.shape[1]
    local = key_weight_ref.shape[1]

    @pl.when(pl.program_id(0) == 0)
    def _():
        build_pick(slots_ref, pick_ref, sizes)
        weight_ref[:, :local] = key_weight_ref[...]
        weight_ref[:, local:] = value_weight_ref[...]

    gain = gain_ref[...]
    for index, tokens_ref in enumerate((even_ref, odd_ref)):
        for start in range(0, patches, ROWS):
            normed = normalize_rows(tokens_ref[0, pl.ds(start, ROWS), :], gain)
            normed_ref[pl.ds(index * patches + start, ROWS), :] = normed
    product = jnp.dot(normed_ref[...], weight_ref[...], preferred_element_type=jnp.float32).astype(jnp.bfloat16)
    product = jnp.concatenate([product[:patches], product[patches:]], axis=1)
    picked = jnp.dot(pick_ref[...], product, preferred_element_type=jnp.float32)
    groups = picked.shape[0] // GROUP
    picked = [
        picked[:, index * 2 * local : (index + 1) * 2 * local].reshape(groups, 1, GROUP, 2 * local) for index in range(2)
    ]
    picked = jnp.concatenate(picked, axis=1).reshape(-1, 2 * BLOCK, 2 * local).astype(jnp.bfloat16)
    first = 0
    for out_ref in out_refs:
        out_ref[:, 0] = picked[first : first + out_ref.shape[0]]
        first += out_ref.shape[0]


def project(slots, tokens, gain, key_weight, value_weight, sizes):
    levels, patches, width = tokens.shape
    local = key_weight.shape[1]
    count = slots.size
    counts = [slots.shape[0] * size // BLOCK for size in sizes]
    steps = (levels + 1) // 2
    whole = lambda i: (0, 0)
    return pl.pallas_call(
        functools.partial(project_kernel, sizes),
        grid=(steps,),
        in_specs=[
            pl.BlockSpec(slots.shape, whole),
            pl.BlockSpec((1, width), whole),
            pl.BlockSpec((width, local), whole),
            pl.BlockSpec((width, local), whole),
            pl.BlockSpec((1, patches, width), lambda i: (2 * i, 0, 0)),
            pl.BlockSpec((1, patches, width), lambda i: (jnp.minimum(2 * i + 1, levels - 1), 0, 0)),
        ],
        out_specs=[pl.BlockSpec((blocks, 1, 2 * BLOCK, 2 * local), lambda i: (0, i, 0, 0)) for blocks in counts],
        out_shape=[jax.ShapeDtypeStruct((blocks, steps, 2 * BLOCK, 2 * local), jnp.bfloat16) for blocks in counts],
        scratch_shapes=[
            pltpu.VMEM((2 * patches, width), jnp.bfloat16),
            pltpu.VMEM((count, patches), jnp.bfloat16),
            pltpu.VMEM((width, 2 * local), jnp.bfloat16),
        ],
        compiler_params=params(58),
        cost_estimate=pl.CostEstimate(
            flops=8 * levels * patches * (width + count) * local,
            bytes_accessed=2 * levels * patches * (width + 2 * local) + 4 * width * local,
            transcendentals=0,
        ),
        name="norm_project",
    )(slots, gain.reshape(1, width), key_weight, value_weight, tokens, tokens)


def attend_kernel(levels, query_ref, pair_ref, *refs):
    out_ref = refs[-1]
    blocks, level_pairs, block, local = pair_ref.shape
    block, local = block // 2, local // 2
    slots = blocks * block
    latents = out_ref.shape[0] // slots
    rows = GROUP * latents
    heads = local // HEAD_DIM
    columns = level_pairs * 2 * GROUP
    lane_head = lax.broadcasted_iota(jnp.int32, (rows, local), 1) // HEAD_DIM
    row_slot = lax.broadcasted_iota(jnp.int32, (GROUP, heads * rows), 0)
    column_slot = (lax.broadcasted_iota(jnp.int32, (GROUP, heads * rows), 1) // latents) & (GROUP - 1)
    same = row_slot - column_slot == 0
    scale = math.log2(math.e) / math.sqrt(HEAD_DIM)
    queries = query_ref[...].astype(jnp.float32)

    def columns_of(start, lane):
        part = pl.ds(start % block * 2, 2 * GROUP)
        return pair_ref[start // block, :, part, pl.ds(lane, local)].reshape(columns, local)

    for first in range(0, slots, block):
        tasks = range(first, first + block, GROUP)
        scores = []
        for start in tasks:
            part = queries[start * latents : start * latents + rows]
            part = jnp.concatenate(
                [jnp.where(lane_head == head, part, 0.0).astype(jnp.bfloat16) for head in range(heads)], axis=0
            )
            product = lax.dot_general(
                columns_of(start, 0), part, (((1,), (1,)), ((), ())), preferred_element_type=jnp.float32
            )
            scores.append(product.reshape(2 * level_pairs, GROUP, heads * rows))
        softs = []
        for product in scores:
            product = product[:levels]
            expo = jnp.exp2((product - jnp.max(product, axis=0, keepdims=True)) * scale)
            inverse = jnp.where(same, 1.0 / jnp.sum(expo, axis=0), 0.0)
            soft = expo * inverse[None]
            if levels < 2 * level_pairs:
                soft = jnp.concatenate([soft, jnp.zeros_like(soft[:1])], axis=0)
            softs.append(soft.reshape(columns, heads * rows).astype(jnp.bfloat16))
        for start, soft in zip(tasks, softs):
            wide = lax.dot_general(
                soft, columns_of(start, local), (((0,), (0,)), ((), ())), preferred_element_type=jnp.float32
            )
            mixed = wide[:rows]
            for head in range(1, heads):
                mixed = jnp.where(lane_head == head, wide[head * rows : (head + 1) * rows], mixed)
            out_ref[pl.ds(start * latents, rows), :] = mixed.astype(jnp.bfloat16)


def attend(queries, pairs, levels, after=()):
    rows, local = queries.shape
    blocks = pairs.shape[0] // STEPS
    query_spec = pl.BlockSpec((rows // STEPS, local), lambda i: (i, 0))
    return pl.pallas_call(
        functools.partial(attend_kernel, levels),
        grid=(STEPS,),
        in_specs=[query_spec, pl.BlockSpec((blocks, *pairs.shape[1:]), lambda i: (i, 0, 0, 0))]
        + [pl.BlockSpec(memory_space=pl.ANY)] * len(after),
        out_specs=query_spec,
        out_shape=jax.ShapeDtypeStruct((rows, local), jnp.bfloat16),
        compiler_params=params(55),
        cost_estimate=pl.CostEstimate(
            flops=1024 * rows * levels * local, bytes_accessed=4 * rows * (levels + 1) * local, transcendentals=0
        ),
        name="attend_slots",
    )(queries, pairs, *after)


def combine_rows(mixed_refs, weight_refs, part):
    total = None
    for mixed_ref, weight_ref in zip(mixed_refs, weight_refs):
        term = jnp.dot(mixed_ref[part, :], weight_ref[...], preferred_element_type=jnp.float32)
        term = term.astype(jnp.bfloat16).astype(jnp.float32)
        total = term if total is None else total + term
    return total.astype(jnp.bfloat16)


def combine_home_kernel(place_ref, *refs):
    for distance, out_ref in enumerate(refs[8:]):
        rows = out_ref.shape[0] * out_ref.shape[1]
        start = jnp.bitwise_xor(place_ref[0], distance) * rows
        part = pl.ds(pl.multiple_of(start, rows), rows)
        out_ref[...] = combine_rows(refs[:4], refs[4:8], part).reshape(out_ref.shape)


def combine_kernel(place_ref, *refs):
    out_ref = refs[-1]
    stripes, caps, latents, local = out_ref.shape
    rest = refs[8:-1]
    half = caps - sum(ref.shape[0] for ref in rest[:1])
    for distance, ref in enumerate(rest):
        out_ref[jnp.bitwise_xor(place_ref[0], distance), half:] = ref[...]
    for stripe in range(stripes):
        part = pl.ds(stripe * half * latents, half * latents)
        rows = combine_rows(refs[:4], refs[4:8], part)
        out_ref[stripe, :half] = rows.reshape(half, latents, local)


def combine(kernel, place, groups, weights, out_shape, rest=()):
    operands = (*groups, *weights, *rest)
    rows, local = groups[0].shape
    vmem = pl.BlockSpec(memory_space=pltpu.VMEM)
    return pl.pallas_call(
        kernel,
        in_specs=[pl.BlockSpec(memory_space=pltpu.SMEM)] + [vmem] * len(operands),
        out_specs=jax.tree.map(lambda _: vmem, out_shape),
        out_shape=out_shape,
        compiler_params=params(20),
        cost_estimate=pl.CostEstimate(
            flops=24 * rows * local * local, bytes_accessed=10 * rows * local, transcendentals=0
        ),
        name="combine_groups",
    )(place, *operands)


def swap(array, axis_name, distance):
    size = lax.axis_size(axis_name)
    return lax.ppermute(array, axis_name, [(i, i ^ distance) for i in range(size)])


def follow(array, *others):
    return lax.optimization_barrier((array, *others))[0]


def spread_heads(mixed, others=()):
    second = swap(mixed, "head", 2)
    return mixed, swap(mixed, "head", 1), second, swap(follow(second, *others), "head", 1)


def exchange(array, stripes):
    array = array.reshape(stripes, -1, *array.shape[1:])
    return lax.all_to_all(array, "lat", split_axis=0, concat_axis=0, tiled=True)


def spread_weight(out_weight, head):
    local = out_weight.shape[0]
    parts = []
    for distance in range(lax.axis_size("head")):
        start = jnp.bitwise_xor(head, distance) * local
        part = lax.dynamic_slice_in_dim(out_weight, start, local, 1)
        parts.append(swap(part, "head", distance) if distance else part)
    return parts


def shards(level_tokens, ln_gain, key_weight, value_weight, out_weight, ocean_queries, send_slots):
    stripes = lax.axis_size("lat")
    caps = send_slots.shape[2]
    shape = ocean_queries.shape
    slots, latents, local = shape
    place = lax.axis_index("lat").reshape(1)
    split = caps * 3 // 8 if caps % (2 * BLOCK) == 0 else caps
    sizes = (split, caps - split) if split < caps else (caps,)
    queries = exchange(ocean_queries, stripes)
    weights = spread_weight(out_weight, lax.axis_index("head"))
    tokens = jnp.transpose(level_tokens, (1, 0, 2))
    levels = tokens.shape[0]
    pairs = project(send_slots[0], tokens, ln_gain, key_weight, value_weight, sizes)
    pairs, weights = lax.optimization_barrier((tuple(pairs), weights))
    whole = jax.ShapeDtypeStruct((stripes, caps, latents, local), jnp.bfloat16)
    early_queries = queries[:, :split].reshape(-1, local)
    if split == caps:
        mixed = exchange(attend(early_queries, pairs[0], levels), stripes).reshape(-1, local)
        return combine(combine_kernel, place, spread_heads(mixed), weights, whole).reshape(shape)
    late = attend(queries[:, split:].reshape(-1, local), pairs[1], levels)
    early = attend(early_queries, pairs[0], levels, (late,))
    chunks = [jax.ShapeDtypeStruct((caps - split, latents, local), jnp.bfloat16)] * stripes
    chunks = combine(combine_home_kernel, place, spread_heads(late, (early,)), weights, chunks)
    chunks = [swap(chunk, "lat", distance) if distance else chunk for distance, chunk in enumerate(chunks)]
    near, far = chunks[: stripes // 2], chunks[stripes // 2 :]
    early = follow(exchange(early, stripes), *near).reshape(-1, local)
    return combine(combine_kernel, place, spread_heads(early, far), weights, whole, chunks).reshape(shape)


def solution(mesh):
    return jax.shard_map(
        shards,
        mesh=mesh,
        in_specs=(
            P("lat", None, None),
            P(),
            P(None, "head"),
            P(None, "head"),
            P("head", None),
            P("lat", None, "head"),
            P("lat", None, None),
        ),
        out_specs=P("lat", None, "head"),
        check_vma=False,
    )
```

```python
import functools
import math

import jax
import jax.numpy as jnp
from jax import lax
from jax.experimental import pallas as pl
from jax.experimental.pallas import tpu as pltpu
from jax.sharding import PartitionSpec as P

HEAD_DIM = 64
EPS = 1e-05
GROUP = 8
BLOCK = 64
STEP_BLOCKS = 2
STAGE = 128
ROWS = 32
MIB = 1024 * 1024


def params(mib):
    return pltpu.CompilerParams(vmem_limit_bytes=mib * MIB)


def normalize_rows(tokens, gain):
    width = tokens.shape[-1]
    tokens = tokens.astype(jnp.float32)
    center = jnp.sum(tokens, axis=-1, keepdims=True) * (1.0 / width)
    shifted = tokens - center
    spread = jnp.sum(shifted * shifted, axis=-1, keepdims=True) * (1.0 / width)
    return (shifted * lax.rsqrt(spread + EPS) * gain).astype(jnp.bfloat16)


def build_pick(slots_ref, pick_ref, halves):
    stripes, caps = slots_ref.shape
    half = caps // halves
    diagonal = lax.broadcasted_iota(jnp.int32, (caps, caps), 0) == lax.broadcasted_iota(jnp.int32, (caps, caps), 1)
    patch = lax.broadcasted_iota(jnp.int32, (caps, pick_ref.shape[1]), 1)
    for owner in range(stripes):
        row = jnp.broadcast_to(slots_ref[owner : owner + 1, :], (caps, caps))
        column = jnp.sum(jnp.where(diagonal, row, 0), axis=-1, keepdims=True)
        pick = jnp.where(patch == column, 1.0, 0.0).astype(jnp.bfloat16)
        for index in range(halves):
            start = (index * stripes + owner) * half
            pick_ref[start : start + half, :] = pick[index * half : (index + 1) * half]


def project_kernel(
    halves,
    slots_ref,
    gain_ref,
    key_weight_ref,
    value_weight_ref,
    even_ref,
    odd_ref,
    out_ref,
    normed_ref,
    pick_ref,
    weight_ref,
):
    patches = even_ref.shape[1]
    local = key_weight_ref.shape[1]

    @pl.when(pl.program_id(0) == 0)
    def _():
        build_pick(slots_ref, pick_ref, halves)
        weight_ref[:, :local] = key_weight_ref[...]
        weight_ref[:, local:] = value_weight_ref[...]

    gain = gain_ref[...]
    for index, tokens_ref in enumerate((even_ref, odd_ref)):
        for start in range(0, patches, ROWS):
            normed = normalize_rows(tokens_ref[0, pl.ds(start, ROWS), :], gain)
            normed_ref[pl.ds(index * patches + start, ROWS), :] = normed
    product = jnp.dot(normed_ref[...], weight_ref[...], preferred_element_type=jnp.float32).astype(jnp.bfloat16)
    product = jnp.concatenate([product[:patches], product[patches:]], axis=1)
    picked = jnp.dot(pick_ref[...], product, preferred_element_type=jnp.float32)
    groups = picked.shape[0] // GROUP
    picked = [
        picked[:, index * 2 * local : (index + 1) * 2 * local].reshape(groups, 1, GROUP, 2 * local) for index in range(2)
    ]
    picked = jnp.concatenate(picked, axis=1).reshape(out_ref.shape[0], 2 * BLOCK, 2 * local)
    out_ref[:, 0] = picked.astype(jnp.bfloat16)


def project(slots, tokens, gain, key_weight, value_weight, halves):
    levels, patches, width = tokens.shape
    local = key_weight.shape[1]
    count = slots.size
    steps = (levels + 1) // 2
    whole = lambda i: (0, 0)
    return pl.pallas_call(
        functools.partial(project_kernel, halves),
        grid=(steps,),
        in_specs=[
            pl.BlockSpec(slots.shape, whole),
            pl.BlockSpec((1, width), whole),
            pl.BlockSpec((width, local), whole),
            pl.BlockSpec((width, local), whole),
            pl.BlockSpec((1, patches, width), lambda i: (2 * i, 0, 0)),
            pl.BlockSpec((1, patches, width), lambda i: (jnp.minimum(2 * i + 1, levels - 1), 0, 0)),
        ],
        out_specs=pl.BlockSpec((count // BLOCK, 1, 2 * BLOCK, 2 * local), lambda i: (0, i, 0, 0)),
        out_shape=jax.ShapeDtypeStruct((count // BLOCK, steps, 2 * BLOCK, 2 * local), jnp.bfloat16),
        scratch_shapes=[
            pltpu.VMEM((2 * patches, width), jnp.bfloat16),
            pltpu.VMEM((count, patches), jnp.bfloat16),
            pltpu.VMEM((width, 2 * local), jnp.bfloat16),
        ],
        compiler_params=params(58),
        cost_estimate=pl.CostEstimate(
            flops=8 * levels * patches * (width + count) * local,
            bytes_accessed=2 * levels * patches * (width + 2 * local) + 4 * width * local,
            transcendentals=0,
        ),
        name="norm_project",
    )(slots, gain.reshape(1, width), key_weight, value_weight, tokens, tokens)


def attend_kernel(levels, query_ref, pair_ref, *refs):
    out_ref = refs[-1]
    blocks, level_pairs, block, local = pair_ref.shape
    block, local = block // 2, local // 2
    slots = blocks * block
    latents = out_ref.shape[0] // slots
    rows = GROUP * latents
    heads = local // HEAD_DIM
    columns = level_pairs * 2 * GROUP
    lane_head = lax.broadcasted_iota(jnp.int32, (rows, local), 1) // HEAD_DIM
    row_slot = lax.broadcasted_iota(jnp.int32, (GROUP, heads * rows), 0)
    column_slot = (lax.broadcasted_iota(jnp.int32, (GROUP, heads * rows), 1) // latents) & (GROUP - 1)
    same = row_slot - column_slot == 0
    scale = math.log2(math.e) / math.sqrt(HEAD_DIM)
    queries = query_ref[...].reshape(slots * latents, local).astype(jnp.float32)

    def columns_of(start, lane):
        part = pl.ds(start % block * 2, 2 * GROUP)
        return pair_ref[start // block, :, part, pl.ds(lane, local)].reshape(columns, local)

    for first in range(0, slots, STAGE):
        tasks = range(first, first + STAGE, GROUP)
        scores = []
        for start in tasks:
            part = queries[start * latents : start * latents + rows]
            part = jnp.concatenate(
                [jnp.where(lane_head == head, part, 0.0).astype(jnp.bfloat16) for head in range(heads)], axis=0
            )
            product = lax.dot_general(
                columns_of(start, 0), part, (((1,), (1,)), ((), ())), preferred_element_type=jnp.float32
            )
            scores.append(product.reshape(2 * level_pairs, GROUP, heads * rows))
        softs = []
        for product in scores:
            product = product[:levels]
            expo = jnp.exp2((product - jnp.max(product, axis=0, keepdims=True)) * scale)
            inverse = jnp.where(same, 1.0 / jnp.sum(expo, axis=0), 0.0)
            soft = expo * inverse[None]
            if levels < 2 * level_pairs:
                soft = jnp.concatenate([soft, jnp.zeros_like(soft[:1])], axis=0)
            softs.append(soft.reshape(columns, heads * rows).astype(jnp.bfloat16))
        for start, soft in zip(tasks, softs):
            wide = lax.dot_general(
                soft, columns_of(start, local), (((0,), (0,)), ((), ())), preferred_element_type=jnp.float32
            )
            mixed = wide[:rows]
            for head in range(1, heads):
                mixed = jnp.where(lane_head == head, wide[head * rows : (head + 1) * rows], mixed)
            out_ref[pl.ds(start * latents, rows), :] = mixed.astype(jnp.bfloat16)


def attend(queries, pairs, levels, index, after=()):
    stripes, halves, rows, local = queries.shape
    steps = pairs.shape[0] // halves // STEP_BLOCKS
    block = stripes * rows // steps
    pair_shape = (STEP_BLOCKS, *pairs.shape[1:])
    return pl.pallas_call(
        functools.partial(attend_kernel, levels),
        grid=(steps,),
        in_specs=[
            pl.BlockSpec((stripes // steps, 1, rows, local), lambda i: (i, index, 0, 0)),
            pl.BlockSpec(pair_shape, lambda i: (index * steps + i, 0, 0, 0)),
        ]
        + [pl.BlockSpec(memory_space=pl.ANY)] * len(after),
        out_specs=pl.BlockSpec((block, local), lambda i: (i, 0)),
        out_shape=jax.ShapeDtypeStruct((steps * block, local), jnp.bfloat16),
        compiler_params=params(55),
        cost_estimate=pl.CostEstimate(
            flops=1024 * steps * block * levels * local,
            bytes_accessed=4 * steps * (block + levels * STEP_BLOCKS * BLOCK) * local,
            transcendentals=0,
        ),
        name="attend_slots",
    )(queries, pairs, *after)


def combine_rows(mixed_refs, weight_refs, part):
    total = None
    for mixed_ref, weight_ref in zip(mixed_refs, weight_refs):
        term = jnp.dot(mixed_ref[part, :], weight_ref[...], preferred_element_type=jnp.float32)
        term = term.astype(jnp.bfloat16).astype(jnp.float32)
        total = term if total is None else total + term
    return total.astype(jnp.bfloat16)


def combine_home_kernel(place_ref, *refs):
    for distance, out_ref in enumerate(refs[8:]):
        rows = out_ref.shape[0] * out_ref.shape[1]
        start = jnp.bitwise_xor(place_ref[0], distance) * rows
        part = pl.ds(pl.multiple_of(start, rows), rows)
        out_ref[...] = combine_rows(refs[:4], refs[4:8], part).reshape(out_ref.shape)


def combine_kernel(place_ref, *refs):
    out_ref = refs[-1]
    stripes, caps, latents, local = out_ref.shape
    rest = refs[8:-1]
    half = caps - sum(ref.shape[0] for ref in rest[:1])
    for distance, ref in enumerate(rest):
        out_ref[jnp.bitwise_xor(place_ref[0], distance), half:] = ref[...]
    for stripe in range(stripes):
        part = pl.ds(stripe * half * latents, half * latents)
        rows = combine_rows(refs[:4], refs[4:8], part)
        out_ref[stripe, :half] = rows.reshape(half, latents, local)


def combine(kernel, place, groups, weights, out_shape, rest=()):
    operands = (*groups, *weights, *rest)
    rows, local = groups[0].shape
    vmem = pl.BlockSpec(memory_space=pltpu.VMEM)
    return pl.pallas_call(
        kernel,
        in_specs=[pl.BlockSpec(memory_space=pltpu.SMEM)] + [vmem] * len(operands),
        out_specs=jax.tree.map(lambda _: vmem, out_shape),
        out_shape=out_shape,
        compiler_params=params(20),
        cost_estimate=pl.CostEstimate(
            flops=24 * rows * local * local, bytes_accessed=10 * rows * local, transcendentals=0
        ),
        name="combine_groups",
    )(place, *operands)


def swap(array, axis_name, distance):
    size = lax.axis_size(axis_name)
    return lax.ppermute(array, axis_name, [(i, i ^ distance) for i in range(size)])


def follow(array, *others):
    return lax.optimization_barrier((array, *others))[0]


def spread_heads(mixed, others=()):
    second = swap(mixed, "head", 2)
    return mixed, swap(mixed, "head", 1), second, swap(follow(second, *others), "head", 1)


def exchange(array, stripes):
    array = array.reshape(stripes, -1, *array.shape[1:])
    return lax.all_to_all(array, "lat", split_axis=0, concat_axis=0, tiled=True)


def spread_weight(out_weight, head):
    local = out_weight.shape[0]
    parts = []
    for distance in range(lax.axis_size("head")):
        start = jnp.bitwise_xor(head, distance) * local
        part = lax.dynamic_slice_in_dim(out_weight, start, local, 1)
        parts.append(swap(part, "head", distance) if distance else part)
    return parts


def shards(level_tokens, ln_gain, key_weight, value_weight, out_weight, ocean_queries, send_slots):
    stripes = lax.axis_size("lat")
    caps = send_slots.shape[2]
    shape = ocean_queries.shape
    slots, latents, local = shape
    place = lax.axis_index("lat").reshape(1)
    halves = 2 if caps == BLOCK else 1
    queries = exchange(ocean_queries, stripes).reshape(stripes, halves, -1, local)
    weights = spread_weight(out_weight, lax.axis_index("head"))
    tokens = jnp.transpose(level_tokens, (1, 0, 2))
    levels = tokens.shape[0]
    pairs = project(send_slots[0], tokens, ln_gain, key_weight, value_weight, halves)
    pairs, weights = lax.optimization_barrier((pairs, weights))
    whole = jax.ShapeDtypeStruct((stripes, caps, latents, local), jnp.bfloat16)
    if halves == 1:
        mixed = exchange(attend(queries, pairs, levels, 0), stripes).reshape(-1, local)
        return combine(combine_kernel, place, spread_heads(mixed), weights, whole).reshape(shape)
    late = attend(queries, pairs, levels, 1)
    early = attend(queries, pairs, levels, 0, (late,))
    chunks = [jax.ShapeDtypeStruct((caps // 2, latents, local), jnp.bfloat16)] * stripes
    chunks = combine(combine_home_kernel, place, spread_heads(late, (early,)), weights, chunks)
    chunks = [swap(chunk, "lat", distance) if distance else chunk for distance, chunk in enumerate(chunks)]
    near, far = chunks[: stripes // 2], chunks[stripes // 2 :]
    early = follow(exchange(early, stripes), *near).reshape(-1, local)
    return combine(combine_kernel, place, spread_heads(early, far), weights, whole, chunks).reshape(shape)


def solution(mesh):
    return jax.shard_map(
        shards,
        mesh=mesh,
        in_specs=(
            P("lat", None, None),
            P(),
            P(None, "head"),
            P(None, "head"),
            P("head", None),
            P("lat", None, "head"),
            P("lat", None, None),
        ),
        out_specs=P("lat", None, "head"),
        check_vma=False,
    )
```

```python
import functools
import math

import jax
import jax.numpy as jnp
from jax import lax
from jax.experimental import pallas as pl
from jax.experimental.pallas import tpu as pltpu
from jax.sharding import PartitionSpec as P

HEAD_DIM = 64
EPS = 1e-05
GROUP = 8
BLOCK = 64
STEP_BLOCKS = 2
STAGE = 128
ROWS = 32
MIB = 1024 * 1024


def params(mib):
    return pltpu.CompilerParams(vmem_limit_bytes=mib * MIB)


def normalize_rows(tokens, gain):
    width = tokens.shape[-1]
    tokens = tokens.astype(jnp.float32)
    center = jnp.sum(tokens, axis=-1, keepdims=True) * (1.0 / width)
    shifted = tokens - center
    spread = jnp.sum(shifted * shifted, axis=-1, keepdims=True) * (1.0 / width)
    return (shifted * lax.rsqrt(spread + EPS) * gain).astype(jnp.bfloat16)


def build_pick(slots_ref, pick_ref, halves):
    stripes, caps = slots_ref.shape
    half = caps // halves
    diagonal = lax.broadcasted_iota(jnp.int32, (caps, caps), 0) == lax.broadcasted_iota(jnp.int32, (caps, caps), 1)
    patch = lax.broadcasted_iota(jnp.int32, (caps, pick_ref.shape[1]), 1)
    for owner in range(stripes):
        row = jnp.broadcast_to(slots_ref[owner : owner + 1, :], (caps, caps))
        column = jnp.sum(jnp.where(diagonal, row, 0), axis=-1, keepdims=True)
        pick = jnp.where(patch == column, 1.0, 0.0).astype(jnp.bfloat16)
        for index in range(halves):
            start = (index * stripes + owner) * half
            pick_ref[start : start + half, :] = pick[index * half : (index + 1) * half]


def project_kernel(
    halves,
    slots_ref,
    gain_ref,
    key_weight_ref,
    value_weight_ref,
    even_ref,
    odd_ref,
    out_ref,
    normed_ref,
    pick_ref,
    weight_ref,
):
    patches = even_ref.shape[1]
    local = key_weight_ref.shape[1]

    @pl.when(pl.program_id(0) == 0)
    def _():
        build_pick(slots_ref, pick_ref, halves)
        weight_ref[:, :local] = key_weight_ref[...]
        weight_ref[:, local:] = value_weight_ref[...]

    gain = gain_ref[...]
    for index, tokens_ref in enumerate((even_ref, odd_ref)):
        for start in range(0, patches, ROWS):
            normed = normalize_rows(tokens_ref[0, pl.ds(start, ROWS), :], gain)
            normed_ref[pl.ds(index * patches + start, ROWS), :] = normed
    product = jnp.dot(normed_ref[...], weight_ref[...], preferred_element_type=jnp.float32).astype(jnp.bfloat16)
    product = jnp.concatenate([product[:patches], product[patches:]], axis=1)
    picked = jnp.dot(pick_ref[...], product, preferred_element_type=jnp.float32)
    groups = picked.shape[0] // GROUP
    picked = [
        picked[:, index * 2 * local : (index + 1) * 2 * local].reshape(groups, 1, GROUP, 2 * local) for index in range(2)
    ]
    picked = jnp.concatenate(picked, axis=1).reshape(out_ref.shape[0], 2 * BLOCK, 2 * local)
    out_ref[:, 0] = picked.astype(jnp.bfloat16)


def project(slots, tokens, gain, key_weight, value_weight, halves):
    levels, patches, width = tokens.shape
    local = key_weight.shape[1]
    count = slots.size
    steps = (levels + 1) // 2
    whole = lambda i: (0, 0)
    return pl.pallas_call(
        functools.partial(project_kernel, halves),
        grid=(steps,),
        in_specs=[
            pl.BlockSpec(slots.shape, whole),
            pl.BlockSpec((1, width), whole),
            pl.BlockSpec((width, local), whole),
            pl.BlockSpec((width, local), whole),
            pl.BlockSpec((1, patches, width), lambda i: (2 * i, 0, 0)),
            pl.BlockSpec((1, patches, width), lambda i: (jnp.minimum(2 * i + 1, levels - 1), 0, 0)),
        ],
        out_specs=pl.BlockSpec((count // BLOCK, 1, 2 * BLOCK, 2 * local), lambda i: (0, i, 0, 0)),
        out_shape=jax.ShapeDtypeStruct((count // BLOCK, steps, 2 * BLOCK, 2 * local), jnp.bfloat16),
        scratch_shapes=[
            pltpu.VMEM((2 * patches, width), jnp.bfloat16),
            pltpu.VMEM((count, patches), jnp.bfloat16),
            pltpu.VMEM((width, 2 * local), jnp.bfloat16),
        ],
        compiler_params=params(58),
        cost_estimate=pl.CostEstimate(
            flops=8 * levels * patches * (width + count) * local,
            bytes_accessed=2 * levels * patches * (width + 2 * local) + 4 * width * local,
            transcendentals=0,
        ),
        name="norm_project",
    )(slots, gain.reshape(1, width), key_weight, value_weight, tokens, tokens)


def attend_kernel(levels, query_ref, pair_ref, *refs):
    out_ref = refs[-1]
    blocks, level_pairs, block, local = pair_ref.shape
    block, local = block // 2, local // 2
    slots = blocks * block
    latents = out_ref.shape[0] // slots
    rows = GROUP * latents
    heads = local // HEAD_DIM
    columns = level_pairs * 2 * GROUP
    lane_head = lax.broadcasted_iota(jnp.int32, (rows, local), 1) // HEAD_DIM
    row_slot = lax.broadcasted_iota(jnp.int32, (GROUP, heads * rows), 0)
    column_slot = (lax.broadcasted_iota(jnp.int32, (GROUP, heads * rows), 1) // latents) & (GROUP - 1)
    same = row_slot - column_slot == 0
    scale = math.log2(math.e) / math.sqrt(HEAD_DIM)
    queries = query_ref[...].reshape(slots * latents, local).astype(jnp.float32)

    def columns_of(start, lane):
        part = pl.ds(start % block * 2, 2 * GROUP)
        return pair_ref[start // block, :, part, pl.ds(lane, local)].reshape(columns, local)

    for first in range(0, slots, STAGE):
        tasks = range(first, first + STAGE, GROUP)
        scores = []
        for start in tasks:
            part = queries[start * latents : start * latents + rows]
            part = jnp.concatenate(
                [jnp.where(lane_head == head, part, 0.0).astype(jnp.bfloat16) for head in range(heads)], axis=0
            )
            product = lax.dot_general(
                columns_of(start, 0), part, (((1,), (1,)), ((), ())), preferred_element_type=jnp.float32
            )
            scores.append(product.reshape(2 * level_pairs, GROUP, heads * rows))
        softs = []
        for product in scores:
            product = product[:levels]
            expo = jnp.exp2((product - jnp.max(product, axis=0, keepdims=True)) * scale)
            inverse = jnp.where(same, 1.0 / jnp.sum(expo, axis=0), 0.0)
            soft = expo * inverse[None]
            if levels < 2 * level_pairs:
                soft = jnp.concatenate([soft, jnp.zeros_like(soft[:1])], axis=0)
            softs.append(soft.reshape(columns, heads * rows).astype(jnp.bfloat16))
        for start, soft in zip(tasks, softs):
            wide = lax.dot_general(
                soft, columns_of(start, local), (((0,), (0,)), ((), ())), preferred_element_type=jnp.float32
            )
            mixed = wide[:rows]
            for head in range(1, heads):
                mixed = jnp.where(lane_head == head, wide[head * rows : (head + 1) * rows], mixed)
            out_ref[pl.ds(start * latents, rows), :] = mixed.astype(jnp.bfloat16)


def attend(queries, pairs, levels, index, after=()):
    stripes, halves, rows, local = queries.shape
    steps = pairs.shape[0] // halves // STEP_BLOCKS
    block = stripes * rows // steps
    pair_shape = (STEP_BLOCKS, *pairs.shape[1:])
    return pl.pallas_call(
        functools.partial(attend_kernel, levels),
        grid=(steps,),
        in_specs=[
            pl.BlockSpec((stripes // steps, 1, rows, local), lambda i: (i, index, 0, 0)),
            pl.BlockSpec(pair_shape, lambda i: (index * steps + i, 0, 0, 0)),
        ]
        + [pl.BlockSpec(memory_space=pl.ANY)] * len(after),
        out_specs=pl.BlockSpec((block, local), lambda i: (i, 0)),
        out_shape=jax.ShapeDtypeStruct((steps * block, local), jnp.bfloat16),
        compiler_params=params(55),
        cost_estimate=pl.CostEstimate(
            flops=1024 * steps * block * levels * local,
            bytes_accessed=4 * steps * (block + levels * STEP_BLOCKS * BLOCK) * local,
            transcendentals=0,
        ),
        name="attend_slots",
    )(queries, pairs, *after)


def combine_rows(mixed_refs, weight_refs, part):
    total = None
    for mixed_ref, weight_ref in zip(mixed_refs, weight_refs):
        term = jnp.dot(mixed_ref[part, :], weight_ref[...], preferred_element_type=jnp.float32)
        term = term.astype(jnp.bfloat16).astype(jnp.float32)
        total = term if total is None else total + term
    return total.astype(jnp.bfloat16)


def combine_home_kernel(place_ref, *refs):
    for distance, out_ref in enumerate(refs[8:]):
        rows = out_ref.shape[0] * out_ref.shape[1]
        start = jnp.bitwise_xor(place_ref[0], distance) * rows
        part = pl.ds(pl.multiple_of(start, rows), rows)
        out_ref[...] = combine_rows(refs[:4], refs[4:8], part).reshape(out_ref.shape)


def combine_kernel(place_ref, *refs):
    out_ref = refs[-1]
    stripes, caps, latents, local = out_ref.shape
    for stripe in range(stripes):
        part = pl.ds(stripe * caps * latents, caps * latents)
        rows = combine_rows(refs[:4], refs[4:8], part)
        out_ref[stripe] = rows.reshape(caps, latents, local)


def term_of(mixed_ref, weight_ref, part):
    term = jnp.dot(mixed_ref[part, :], weight_ref[...], preferred_element_type=jnp.float32)
    return term.astype(jnp.bfloat16).astype(jnp.float32)


def combine_most_kernel(place_ref, *refs):
    out_ref, total_ref = refs[-2:]
    rest = refs[6:-2]
    stripes = out_ref.shape[0]
    half = out_ref.shape[1] - rest[0].shape[0]
    for distance, ref in enumerate(rest):
        out_ref[jnp.bitwise_xor(place_ref[0], distance), half:] = ref[...]
    rows = total_ref.shape[0] // stripes
    for stripe in range(stripes):
        part = pl.ds(stripe * rows, rows)
        first, second, third = (term_of(mixed, weight, part) for mixed, weight in zip(refs[:3], refs[3:6]))
        total_ref[part, :] = first + second + third


def combine_last_kernel(mixed_ref, weight_ref, total_ref, whole_ref, out_ref):
    stripes, half, latents, local = out_ref.shape
    rows = half * latents
    for stripe in range(stripes):
        part = pl.ds(stripe * rows, rows)
        total = total_ref[part, :] + term_of(mixed_ref, weight_ref, part)
        out_ref[stripe] = total.astype(jnp.bfloat16).reshape(half, latents, local)


def combine_last(mixed, weight, total, whole):
    stripes, caps, latents, local = whole.shape
    half = mixed.shape[0] // stripes // latents
    specs = [pl.BlockSpec(array.shape, lambda i: (0, 0)) for array in (mixed, weight, total)]
    return pl.pallas_call(
        combine_last_kernel,
        grid=(1,),
        in_specs=specs + [pl.BlockSpec(memory_space=pl.ANY)],
        out_specs=pl.BlockSpec((stripes, half, latents, local), lambda i: (0, 0, 0, 0)),
        out_shape=jax.ShapeDtypeStruct(whole.shape, whole.dtype),
        input_output_aliases={3: 0},
        compiler_params=params(20),
        cost_estimate=pl.CostEstimate(flops=6 * mixed.size * local, bytes_accessed=8 * mixed.size, transcendentals=0),
        name="combine_last",
    )(mixed, weight, total, whole)


def combine(kernel, place, groups, weights, out_shape, rest=()):
    operands = (*groups, *weights, *rest)
    rows, local = groups[0].shape
    vmem = pl.BlockSpec(memory_space=pltpu.VMEM)
    return pl.pallas_call(
        kernel,
        in_specs=[pl.BlockSpec(memory_space=pltpu.SMEM)] + [vmem] * len(operands),
        out_specs=jax.tree.map(lambda _: vmem, out_shape),
        out_shape=out_shape,
        compiler_params=params(20),
        cost_estimate=pl.CostEstimate(
            flops=24 * rows * local * local, bytes_accessed=10 * rows * local, transcendentals=0
        ),
        name="combine_groups",
    )(place, *operands)


def swap(array, axis_name, distance):
    size = lax.axis_size(axis_name)
    return lax.ppermute(array, axis_name, [(i, i ^ distance) for i in range(size)])


def follow(array, *others):
    return lax.optimization_barrier((array, *others))[0]


def spread_heads(mixed, others=()):
    second = swap(mixed, "head", 2)
    return mixed, swap(mixed, "head", 1), second, swap(follow(second, *others), "head", 1)


def exchange(array, stripes):
    array = array.reshape(stripes, -1, *array.shape[1:])
    return lax.all_to_all(array, "lat", split_axis=0, concat_axis=0, tiled=True)


def spread_weight(out_weight, head):
    local = out_weight.shape[0]
    parts = []
    for distance in range(lax.axis_size("head")):
        start = jnp.bitwise_xor(head, distance) * local
        part = lax.dynamic_slice_in_dim(out_weight, start, local, 1)
        parts.append(swap(part, "head", distance) if distance else part)
    return parts


def shards(level_tokens, ln_gain, key_weight, value_weight, out_weight, ocean_queries, send_slots):
    stripes = lax.axis_size("lat")
    caps = send_slots.shape[2]
    shape = ocean_queries.shape
    slots, latents, local = shape
    place = lax.axis_index("lat").reshape(1)
    halves = 2 if caps == BLOCK else 1
    queries = exchange(ocean_queries, stripes).reshape(stripes, halves, -1, local)
    weights = spread_weight(out_weight, lax.axis_index("head"))
    tokens = jnp.transpose(level_tokens, (1, 0, 2))
    levels = tokens.shape[0]
    pairs = project(send_slots[0], tokens, ln_gain, key_weight, value_weight, halves)
    pairs, weights = lax.optimization_barrier((pairs, weights))
    whole = jax.ShapeDtypeStruct((stripes, caps, latents, local), jnp.bfloat16)
    if halves == 1:
        mixed = exchange(attend(queries, pairs, levels, 0), stripes).reshape(-1, local)
        return combine(combine_kernel, place, spread_heads(mixed), weights, whole).reshape(shape)
    late = attend(queries, pairs, levels, 1)
    early = attend(queries, pairs, levels, 0, (late,))
    chunks = [jax.ShapeDtypeStruct((caps // 2, latents, local), jnp.bfloat16)] * stripes
    chunks = combine(combine_home_kernel, place, spread_heads(late, (early,)), weights, chunks)
    chunks = [swap(chunk, "lat", distance) if distance else chunk for distance, chunk in enumerate(chunks)]
    near, far = chunks[: stripes // 2], chunks[stripes // 2 :]
    early = follow(exchange(early, stripes), *near).reshape(-1, local)
    *most, last = spread_heads(early, far)
    most_shape = (whole, jax.ShapeDtypeStruct(early.shape, jnp.float32))
    out, total = combine(combine_most_kernel, place, most, weights[:3], most_shape, chunks)
    return combine_last(last, weights[3], total, out).reshape(shape)


def solution(mesh):
    return jax.shard_map(
        shards,
        mesh=mesh,
        in_specs=(
            P("lat", None, None),
            P(),
            P(None, "head"),
            P(None, "head"),
            P("head", None),
            P("lat", None, "head"),
            P("lat", None, None),
        ),
        out_specs=P("lat", None, "head"),
        check_vma=False,
    )
```

```python
import functools
import math

import jax
import jax.numpy as jnp
from jax import lax
from jax.experimental import pallas as pl
from jax.experimental.pallas import tpu as pltpu
from jax.sharding import PartitionSpec as P

HEAD_DIM = 64
EPS = 1e-05
GROUP = 8
BLOCK = 64
STEP_BLOCKS = 2
STAGE = 128
ROWS = 32
MIB = 1024 * 1024


def params(mib):
    return pltpu.CompilerParams(vmem_limit_bytes=mib * MIB)


def normalize_rows(tokens, gain):
    width = tokens.shape[-1]
    tokens = tokens.astype(jnp.float32)
    center = jnp.sum(tokens, axis=-1, keepdims=True) * (1.0 / width)
    shifted = tokens - center
    spread = jnp.sum(shifted * shifted, axis=-1, keepdims=True) * (1.0 / width)
    return (shifted * lax.rsqrt(spread + EPS) * gain).astype(jnp.bfloat16)


def build_pick(slots_ref, pick_ref, halves):
    stripes, caps = slots_ref.shape
    half = caps // halves
    diagonal = lax.broadcasted_iota(jnp.int32, (caps, caps), 0) == lax.broadcasted_iota(jnp.int32, (caps, caps), 1)
    patch = lax.broadcasted_iota(jnp.int32, (caps, pick_ref.shape[1]), 1)
    for owner in range(stripes):
        row = jnp.broadcast_to(slots_ref[owner : owner + 1, :], (caps, caps))
        column = jnp.sum(jnp.where(diagonal, row, 0), axis=-1, keepdims=True)
        pick = jnp.where(patch == column, 1.0, 0.0).astype(jnp.bfloat16)
        for index in range(halves):
            start = (index * stripes + owner) * half
            pick_ref[start : start + half, :] = pick[index * half : (index + 1) * half]


def project_kernel(
    halves,
    slots_ref,
    gain_ref,
    key_weight_ref,
    value_weight_ref,
    even_ref,
    odd_ref,
    out_ref,
    normed_ref,
    pick_ref,
    weight_ref,
):
    patches = even_ref.shape[1]
    local = key_weight_ref.shape[1]

    @pl.when(pl.program_id(0) == 0)
    def _():
        build_pick(slots_ref, pick_ref, halves)
        weight_ref[:, :local] = key_weight_ref[...]
        weight_ref[:, local:] = value_weight_ref[...]

    gain = gain_ref[...]
    for index, tokens_ref in enumerate((even_ref, odd_ref)):
        for start in range(0, patches, ROWS):
            normed = normalize_rows(tokens_ref[0, pl.ds(start, ROWS), :], gain)
            normed_ref[pl.ds(index * patches + start, ROWS), :] = normed
    product = jnp.dot(normed_ref[...], weight_ref[...], preferred_element_type=jnp.float32).astype(jnp.bfloat16)
    product = jnp.concatenate([product[:patches], product[patches:]], axis=1)
    picked = jnp.dot(pick_ref[...], product, preferred_element_type=jnp.float32)
    groups = picked.shape[0] // GROUP
    picked = [
        picked[:, index * 2 * local : (index + 1) * 2 * local].reshape(groups, 1, GROUP, 2 * local) for index in range(2)
    ]
    picked = jnp.concatenate(picked, axis=1).reshape(out_ref.shape[0], 2 * BLOCK, 2 * local)
    out_ref[:, 0] = picked.astype(jnp.bfloat16)


def project(slots, tokens, gain, key_weight, value_weight, halves):
    levels, patches, width = tokens.shape
    local = key_weight.shape[1]
    count = slots.size
    steps = (levels + 1) // 2
    whole = lambda i: (0, 0)
    return pl.pallas_call(
        functools.partial(project_kernel, halves),
        grid=(steps,),
        in_specs=[
            pl.BlockSpec(slots.shape, whole),
            pl.BlockSpec((1, width), whole),
            pl.BlockSpec((width, local), whole),
            pl.BlockSpec((width, local), whole),
            pl.BlockSpec((1, patches, width), lambda i: (2 * i, 0, 0)),
            pl.BlockSpec((1, patches, width), lambda i: (jnp.minimum(2 * i + 1, levels - 1), 0, 0)),
        ],
        out_specs=pl.BlockSpec((count // BLOCK, 1, 2 * BLOCK, 2 * local), lambda i: (0, i, 0, 0)),
        out_shape=jax.ShapeDtypeStruct((count // BLOCK, steps, 2 * BLOCK, 2 * local), jnp.bfloat16),
        scratch_shapes=[
            pltpu.VMEM((2 * patches, width), jnp.bfloat16),
            pltpu.VMEM((count, patches), jnp.bfloat16),
            pltpu.VMEM((width, 2 * local), jnp.bfloat16),
        ],
        compiler_params=params(58),
        cost_estimate=pl.CostEstimate(
            flops=8 * levels * patches * (width + count) * local,
            bytes_accessed=2 * levels * patches * (width + 2 * local) + 4 * width * local,
            transcendentals=0,
        ),
        name="norm_project",
    )(slots, gain.reshape(1, width), key_weight, value_weight, tokens, tokens)


def attend_kernel(levels, query_ref, pair_ref, *refs):
    out_ref = refs[-1]
    blocks, level_pairs, block, local = pair_ref.shape
    block, local = block // 2, local // 2
    slots = blocks * block
    latents = out_ref.shape[0] // slots
    rows = GROUP * latents
    heads = local // HEAD_DIM
    columns = level_pairs * 2 * GROUP
    lane_head = lax.broadcasted_iota(jnp.int32, (rows, local), 1) // HEAD_DIM
    row_slot = lax.broadcasted_iota(jnp.int32, (GROUP, heads * rows), 0)
    column_slot = (lax.broadcasted_iota(jnp.int32, (GROUP, heads * rows), 1) // latents) & (GROUP - 1)
    same = row_slot - column_slot == 0
    scale = math.log2(math.e) / math.sqrt(HEAD_DIM)
    queries = query_ref[...].reshape(slots * latents, local).astype(jnp.float32)

    def columns_of(start, lane):
        part = pl.ds(start % block * 2, 2 * GROUP)
        return pair_ref[start // block, :, part, pl.ds(lane, local)].reshape(columns, local)

    for first in range(0, slots, STAGE):
        tasks = range(first, first + STAGE, GROUP)
        scores = []
        for start in tasks:
            part = queries[start * latents : start * latents + rows]
            part = jnp.concatenate(
                [jnp.where(lane_head == head, part, 0.0).astype(jnp.bfloat16) for head in range(heads)], axis=0
            )
            product = lax.dot_general(
                columns_of(start, 0), part, (((1,), (1,)), ((), ())), preferred_element_type=jnp.float32
            )
            scores.append(product.reshape(2 * level_pairs, GROUP, heads * rows))
        softs = []
        for product in scores:
            product = product[:levels]
            expo = jnp.exp2((product - jnp.max(product, axis=0, keepdims=True)) * scale)
            inverse = jnp.where(same, 1.0 / jnp.sum(expo, axis=0), 0.0)
            soft = expo * inverse[None]
            if levels < 2 * level_pairs:
                soft = jnp.concatenate([soft, jnp.zeros_like(soft[:1])], axis=0)
            softs.append(soft.reshape(columns, heads * rows).astype(jnp.bfloat16))
        for start, soft in zip(tasks, softs):
            wide = lax.dot_general(
                soft, columns_of(start, local), (((0,), (0,)), ((), ())), preferred_element_type=jnp.float32
            )
            mixed = wide[:rows]
            for head in range(1, heads):
                mixed = jnp.where(lane_head == head, wide[head * rows : (head + 1) * rows], mixed)
            out_ref[pl.ds(start * latents, rows), :] = mixed.astype(jnp.bfloat16)


def attend(queries, pairs, levels, index, after=()):
    stripes, halves, rows, local = queries.shape
    steps = pairs.shape[0] // halves // STEP_BLOCKS
    block = stripes * rows // steps
    pair_shape = (STEP_BLOCKS, *pairs.shape[1:])
    return pl.pallas_call(
        functools.partial(attend_kernel, levels),
        grid=(steps,),
        in_specs=[
            pl.BlockSpec((stripes // steps, 1, rows, local), lambda i: (i, index, 0, 0)),
            pl.BlockSpec(pair_shape, lambda i: (index * steps + i, 0, 0, 0)),
        ]
        + [pl.BlockSpec(memory_space=pl.ANY)] * len(after),
        out_specs=pl.BlockSpec((block, local), lambda i: (i, 0)),
        out_shape=jax.ShapeDtypeStruct((steps * block, local), jnp.bfloat16),
        compiler_params=params(55),
        cost_estimate=pl.CostEstimate(
            flops=1024 * steps * block * levels * local,
            bytes_accessed=4 * steps * (block + levels * STEP_BLOCKS * BLOCK) * local,
            transcendentals=0,
        ),
        name="attend_slots",
    )(queries, pairs, *after)


def combine_rows(mixed_refs, weight_refs, part):
    total = None
    for mixed_ref, weight_ref in zip(mixed_refs, weight_refs):
        term = jnp.dot(mixed_ref[part, :], weight_ref[...], preferred_element_type=jnp.float32)
        term = term.astype(jnp.bfloat16).astype(jnp.float32)
        total = term if total is None else total + term
    return total.astype(jnp.bfloat16)


def combine_home_kernel(place_ref, *refs):
    for distance, out_ref in enumerate(refs[8:]):
        rows = out_ref.shape[0] * out_ref.shape[1]
        start = jnp.bitwise_xor(place_ref[0], distance) * rows
        part = pl.ds(pl.multiple_of(start, rows), rows)
        out_ref[...] = combine_rows(refs[:4], refs[4:8], part).reshape(out_ref.shape)


def combine_kernel(place_ref, *refs):
    out_ref = refs[-1]
    stripes, caps, latents, local = out_ref.shape
    for stripe in range(stripes):
        part = pl.ds(stripe * caps * latents, caps * latents)
        rows = combine_rows(refs[:4], refs[4:8], part)
        out_ref[stripe] = rows.reshape(caps, latents, local)


def term_of(mixed_ref, weight_ref, part):
    term = jnp.dot(mixed_ref[part, :], weight_ref[...], preferred_element_type=jnp.float32)
    return term.astype(jnp.bfloat16).astype(jnp.float32)


def combine_most_kernel(place_ref, *refs):
    out_ref, total_ref = refs[-2:]
    rest = refs[4:-2]
    stripes = out_ref.shape[0]
    half = out_ref.shape[1] - rest[0].shape[0]
    for distance, ref in enumerate(rest):
        out_ref[jnp.bitwise_xor(place_ref[0], distance), half:] = ref[...]
    rows = total_ref.shape[0] // stripes
    for stripe in range(stripes):
        part = pl.ds(stripe * rows, rows)
        total_ref[part, :] = term_of(refs[0], refs[2], part) + term_of(refs[1], refs[3], part)


def combine_last_kernel(first_ref, second_ref, first_weight_ref, second_weight_ref, total_ref, whole_ref, out_ref):
    stripes, half, latents, local = out_ref.shape
    rows = half * latents
    for stripe in range(stripes):
        part = pl.ds(stripe * rows, rows)
        total = total_ref[part, :] + term_of(first_ref, first_weight_ref, part)
        total = total + term_of(second_ref, second_weight_ref, part)
        out_ref[stripe] = total.astype(jnp.bfloat16).reshape(half, latents, local)


def combine_last(mixed, weights, total, whole):
    stripes, caps, latents, local = whole.shape
    half = total.shape[0] // stripes // latents
    operands = (*mixed, *weights, total)
    specs = [pl.BlockSpec(array.shape, lambda i: (0, 0)) for array in operands]
    return pl.pallas_call(
        combine_last_kernel,
        grid=(1,),
        in_specs=specs + [pl.BlockSpec(memory_space=pl.ANY)],
        out_specs=pl.BlockSpec((stripes, half, latents, local), lambda i: (0, 0, 0, 0)),
        out_shape=jax.ShapeDtypeStruct(whole.shape, whole.dtype),
        input_output_aliases={len(operands): 0},
        compiler_params=params(20),
        cost_estimate=pl.CostEstimate(flops=12 * total.size * local, bytes_accessed=10 * total.size, transcendentals=0),
        name="combine_last",
    )(*operands, whole)


def combine(kernel, place, groups, weights, out_shape, rest=()):
    operands = (*groups, *weights, *rest)
    rows, local = groups[0].shape
    vmem = pl.BlockSpec(memory_space=pltpu.VMEM)
    return pl.pallas_call(
        kernel,
        in_specs=[pl.BlockSpec(memory_space=pltpu.SMEM)] + [vmem] * len(operands),
        out_specs=jax.tree.map(lambda _: vmem, out_shape),
        out_shape=out_shape,
        compiler_params=params(20),
        cost_estimate=pl.CostEstimate(
            flops=24 * rows * local * local, bytes_accessed=10 * rows * local, transcendentals=0
        ),
        name="combine_groups",
    )(place, *operands)


def swap(array, axis_name, distance):
    size = lax.axis_size(axis_name)
    return lax.ppermute(array, axis_name, [(i, i ^ distance) for i in range(size)])


def follow(array, *others):
    return lax.optimization_barrier((array, *others))[0]


def spread_heads(mixed, others=()):
    second = swap(mixed, "head", 2)
    return mixed, swap(mixed, "head", 1), second, swap(follow(second, *others), "head", 1)


def exchange(array, stripes):
    array = array.reshape(stripes, -1, *array.shape[1:])
    return lax.all_to_all(array, "lat", split_axis=0, concat_axis=0, tiled=True)


def spread_weight(out_weight, head):
    local = out_weight.shape[0]
    parts = []
    for distance in range(lax.axis_size("head")):
        start = jnp.bitwise_xor(head, distance) * local
        part = lax.dynamic_slice_in_dim(out_weight, start, local, 1)
        parts.append(swap(part, "head", distance) if distance else part)
    return parts


def shards(level_tokens, ln_gain, key_weight, value_weight, out_weight, ocean_queries, send_slots):
    stripes = lax.axis_size("lat")
    caps = send_slots.shape[2]
    shape = ocean_queries.shape
    slots, latents, local = shape
    place = lax.axis_index("lat").reshape(1)
    halves = 2 if caps == BLOCK else 1
    queries = exchange(ocean_queries, stripes).reshape(stripes, halves, -1, local)
    weights = spread_weight(out_weight, lax.axis_index("head"))
    tokens = jnp.transpose(level_tokens, (1, 0, 2))
    levels = tokens.shape[0]
    pairs = project(send_slots[0], tokens, ln_gain, key_weight, value_weight, halves)
    pairs, weights = lax.optimization_barrier((pairs, weights))
    whole = jax.ShapeDtypeStruct((stripes, caps, latents, local), jnp.bfloat16)
    if halves == 1:
        mixed = exchange(attend(queries, pairs, levels, 0), stripes).reshape(-1, local)
        return combine(combine_kernel, place, spread_heads(mixed), weights, whole).reshape(shape)
    late = attend(queries, pairs, levels, 1)
    early = attend(queries, pairs, levels, 0, (late,))
    chunks = [jax.ShapeDtypeStruct((caps // 2, latents, local), jnp.bfloat16)] * stripes
    chunks = combine(combine_home_kernel, place, spread_heads(late, (early,)), weights, chunks)
    chunks = [swap(chunk, "lat", distance) if distance else chunk for distance, chunk in enumerate(chunks)]
    near, far = chunks[: stripes // 2], chunks[stripes // 2 :]
    early = follow(exchange(early, stripes), *near).reshape(-1, local)
    own, across, second, third = spread_heads(early, far)
    most_shape = (whole, jax.ShapeDtypeStruct(early.shape, jnp.float32))
    out, total = combine(combine_most_kernel, place, (own, second), weights[::2], most_shape, chunks)
    return combine_last((across, third), weights[1::2], total, out).reshape(shape)


def solution(mesh):
    return jax.shard_map(
        shards,
        mesh=mesh,
        in_specs=(
            P("lat", None, None),
            P(),
            P(None, "head"),
            P(None, "head"),
            P("head", None),
            P("lat", None, "head"),
            P("lat", None, None),
        ),
        out_specs=P("lat", None, "head"),
        check_vma=False,
    )
```

```python
import functools
import math

import jax
import jax.numpy as jnp
from jax import lax
from jax.experimental import pallas as pl
from jax.experimental.pallas import tpu as pltpu
from jax.sharding import PartitionSpec as P

HEAD_DIM = 64
EPS = 1e-05
GROUP = 8
BLOCK = 64
STEP_BLOCKS = 2
STAGE = 128
ROWS = 32
MIB = 1024 * 1024


def params(mib):
    return pltpu.CompilerParams(vmem_limit_bytes=mib * MIB)


def normalize_rows(tokens, gain):
    width = tokens.shape[-1]
    tokens = tokens.astype(jnp.float32)
    center = jnp.sum(tokens, axis=-1, keepdims=True) * (1.0 / width)
    shifted = tokens - center
    spread = jnp.sum(shifted * shifted, axis=-1, keepdims=True) * (1.0 / width)
    return (shifted * lax.rsqrt(spread + EPS) * gain).astype(jnp.bfloat16)


def build_pick(slots_ref, pick_ref, halves):
    stripes, caps = slots_ref.shape
    half = caps // halves
    diagonal = lax.broadcasted_iota(jnp.int32, (caps, caps), 0) == lax.broadcasted_iota(jnp.int32, (caps, caps), 1)
    patch = lax.broadcasted_iota(jnp.int32, (caps, pick_ref.shape[1]), 1)
    for owner in range(stripes):
        row = jnp.broadcast_to(slots_ref[owner : owner + 1, :], (caps, caps))
        column = jnp.sum(jnp.where(diagonal, row, 0), axis=-1, keepdims=True)
        pick = jnp.where(patch == column, 1.0, 0.0).astype(jnp.bfloat16)
        for index in range(halves):
            start = (index * stripes + owner) * half
            pick_ref[start : start + half, :] = pick[index * half : (index + 1) * half]


def project_kernel(
    halves,
    slots_ref,
    gain_ref,
    key_weight_ref,
    value_weight_ref,
    even_ref,
    odd_ref,
    out_ref,
    normed_ref,
    pick_ref,
    weight_ref,
):
    patches = even_ref.shape[1]
    local = key_weight_ref.shape[1]

    @pl.when(pl.program_id(0) == 0)
    def _():
        build_pick(slots_ref, pick_ref, halves)
        weight_ref[:, :local] = key_weight_ref[...]
        weight_ref[:, local:] = value_weight_ref[...]

    gain = gain_ref[...]
    for index, tokens_ref in enumerate((even_ref, odd_ref)):
        for start in range(0, patches, ROWS):
            normed = normalize_rows(tokens_ref[0, pl.ds(start, ROWS), :], gain)
            normed_ref[pl.ds(index * patches + start, ROWS), :] = normed
    product = jnp.dot(normed_ref[...], weight_ref[...], preferred_element_type=jnp.float32).astype(jnp.bfloat16)
    product = jnp.concatenate([product[:patches], product[patches:]], axis=1)
    picked = jnp.dot(pick_ref[...], product, preferred_element_type=jnp.float32)
    groups = picked.shape[0] // GROUP
    picked = [
        picked[:, index * 2 * local : (index + 1) * 2 * local].reshape(groups, 1, GROUP, 2 * local) for index in range(2)
    ]
    picked = jnp.concatenate(picked, axis=1).reshape(out_ref.shape[0], 2 * BLOCK, 2 * local)
    out_ref[:, 0] = picked.astype(jnp.bfloat16)


def project(slots, tokens, gain, key_weight, value_weight, halves):
    levels, patches, width = tokens.shape
    local = key_weight.shape[1]
    count = slots.size
    steps = (levels + 1) // 2
    whole = lambda i: (0, 0)
    return pl.pallas_call(
        functools.partial(project_kernel, halves),
        grid=(steps,),
        in_specs=[
            pl.BlockSpec(slots.shape, whole),
            pl.BlockSpec((1, width), whole),
            pl.BlockSpec((width, local), whole),
            pl.BlockSpec((width, local), whole),
            pl.BlockSpec((1, patches, width), lambda i: (2 * i, 0, 0)),
            pl.BlockSpec((1, patches, width), lambda i: (jnp.minimum(2 * i + 1, levels - 1), 0, 0)),
        ],
        out_specs=pl.BlockSpec((count // BLOCK, 1, 2 * BLOCK, 2 * local), lambda i: (0, i, 0, 0)),
        out_shape=jax.ShapeDtypeStruct((count // BLOCK, steps, 2 * BLOCK, 2 * local), jnp.bfloat16),
        scratch_shapes=[
            pltpu.VMEM((2 * patches, width), jnp.bfloat16),
            pltpu.VMEM((count, patches), jnp.bfloat16),
            pltpu.VMEM((width, 2 * local), jnp.bfloat16),
        ],
        compiler_params=params(58),
        cost_estimate=pl.CostEstimate(
            flops=8 * levels * patches * (width + count) * local,
            bytes_accessed=2 * levels * patches * (width + 2 * local) + 4 * width * local,
            transcendentals=0,
        ),
        name="norm_project",
    )(slots, gain.reshape(1, width), key_weight, value_weight, tokens, tokens)


def attend_kernel(levels, query_ref, pair_ref, *refs):
    out_refs, out_ref = refs[:-1], refs[-1]
    blocks, level_pairs, block, local = pair_ref.shape
    block, local = block // 2, local // 2
    slots = blocks * block
    latents = out_ref.shape[0] // slots
    rows = GROUP * latents
    heads = local // HEAD_DIM
    columns = level_pairs * 2 * GROUP
    lane_head = lax.broadcasted_iota(jnp.int32, (rows, local), 1) // HEAD_DIM
    row_slot = lax.broadcasted_iota(jnp.int32, (GROUP, heads * rows), 0)
    column_slot = (lax.broadcasted_iota(jnp.int32, (GROUP, heads * rows), 1) // latents) & (GROUP - 1)
    same = row_slot - column_slot == 0
    scale = math.log2(math.e) / math.sqrt(HEAD_DIM)
    queries = query_ref[...].reshape(slots * latents, local).astype(jnp.float32)

    def columns_of(start, lane):
        part = pl.ds(start % block * 2, 2 * GROUP)
        return pair_ref[start // block, :, part, pl.ds(lane, local)].reshape(columns, local)

    for first in range(0, slots, STAGE):
        tasks = range(first, first + STAGE, GROUP)
        scores = []
        for start in tasks:
            part = queries[start * latents : start * latents + rows]
            part = jnp.concatenate(
                [jnp.where(lane_head == head, part, 0.0).astype(jnp.bfloat16) for head in range(heads)], axis=0
            )
            product = lax.dot_general(
                columns_of(start, 0), part, (((1,), (1,)), ((), ())), preferred_element_type=jnp.float32
            )
            scores.append(product.reshape(2 * level_pairs, GROUP, heads * rows))
        softs = []
        for product in scores:
            product = product[:levels]
            expo = jnp.exp2((product - jnp.max(product, axis=0, keepdims=True)) * scale)
            inverse = jnp.where(same, 1.0 / jnp.sum(expo, axis=0), 0.0)
            soft = expo * inverse[None]
            if levels < 2 * level_pairs:
                soft = jnp.concatenate([soft, jnp.zeros_like(soft[:1])], axis=0)
            softs.append(soft.reshape(columns, heads * rows).astype(jnp.bfloat16))
        for start, soft in zip(tasks, softs):
            wide = lax.dot_general(
                soft, columns_of(start, local), (((0,), (0,)), ((), ())), preferred_element_type=jnp.float32
            )
            mixed = wide[:rows]
            for head in range(1, heads):
                mixed = jnp.where(lane_head == head, wide[head * rows : (head + 1) * rows], mixed)
            out_ref[pl.ds(start * latents, rows), :] = mixed.astype(jnp.bfloat16)
    steps = pl.num_programs(0) // len(out_refs)
    for index, half_ref in enumerate(out_refs):

        @pl.when(pl.program_id(0) // steps == index)
        def _(half_ref=half_ref):
            half_ref[...] = out_ref[...]


def attend(queries, pairs, levels):
    stripes, halves, rows, local = queries.shape
    steps = pairs.shape[0] // halves // STEP_BLOCKS
    block = stripes * rows // steps
    pair_shape = (STEP_BLOCKS, *pairs.shape[1:])

    def out_spec(index):
        return pl.BlockSpec((block, local), lambda i: (jnp.clip(i - index * steps, 0, steps - 1), 0))

    return pl.pallas_call(
        functools.partial(attend_kernel, levels),
        grid=(halves * steps,),
        in_specs=[
            pl.BlockSpec((stripes // steps, 1, rows, local), lambda i: (i % steps, i // steps, 0, 0)),
            pl.BlockSpec(pair_shape, lambda i: (i, 0, 0, 0)),
        ],
        out_specs=[out_spec(index) for index in range(halves)],
        out_shape=[jax.ShapeDtypeStruct((steps * block, local), jnp.bfloat16)] * halves,
        scratch_shapes=[pltpu.VMEM((block, local), jnp.bfloat16)],
        compiler_params=params(55),
        cost_estimate=pl.CostEstimate(
            flops=1024 * halves * steps * block * levels * local,
            bytes_accessed=4 * halves * steps * (block + levels * STEP_BLOCKS * BLOCK) * local,
            transcendentals=0,
        ),
        name="attend_slots",
    )(queries, pairs)


def combine_rows(mixed_refs, weight_refs, part):
    total = None
    for mixed_ref, weight_ref in zip(mixed_refs, weight_refs):
        term = jnp.dot(mixed_ref[part, :], weight_ref[...], preferred_element_type=jnp.float32)
        term = term.astype(jnp.bfloat16).astype(jnp.float32)
        total = term if total is None else total + term
    return total.astype(jnp.bfloat16)


def combine_home_kernel(place_ref, *refs):
    for distance, out_ref in enumerate(refs[8:]):
        rows = out_ref.shape[0] * out_ref.shape[1]
        start = jnp.bitwise_xor(place_ref[0], distance) * rows
        part = pl.ds(pl.multiple_of(start, rows), rows)
        out_ref[...] = combine_rows(refs[:4], refs[4:8], part).reshape(out_ref.shape)


def combine_kernel(place_ref, *refs):
    out_ref = refs[-1]
    stripes, caps, latents, local = out_ref.shape
    for stripe in range(stripes):
        part = pl.ds(stripe * caps * latents, caps * latents)
        rows = combine_rows(refs[:4], refs[4:8], part)
        out_ref[stripe] = rows.reshape(caps, latents, local)


def term_of(mixed_ref, weight_ref, part):
    term = jnp.dot(mixed_ref[part, :], weight_ref[...], preferred_element_type=jnp.float32)
    return term.astype(jnp.bfloat16).astype(jnp.float32)


def combine_most_kernel(place_ref, *refs):
    out_ref, total_ref = refs[-2:]
    rest = refs[4:-2]
    stripes = out_ref.shape[0]
    half = out_ref.shape[1] - rest[0].shape[0]
    for distance, ref in enumerate(rest):
        out_ref[jnp.bitwise_xor(place_ref[0], distance), half:] = ref[...]
    rows = total_ref.shape[0] // stripes
    for stripe in range(stripes):
        part = pl.ds(stripe * rows, rows)
        total_ref[part, :] = term_of(refs[0], refs[2], part) + term_of(refs[1], refs[3], part)


def combine_last_kernel(first_ref, second_ref, first_weight_ref, second_weight_ref, total_ref, whole_ref, out_ref):
    stripes, half, latents, local = out_ref.shape
    rows = half * latents
    for stripe in range(stripes):
        part = pl.ds(stripe * rows, rows)
        total = total_ref[part, :] + term_of(first_ref, first_weight_ref, part)
        total = total + term_of(second_ref, second_weight_ref, part)
        out_ref[stripe] = total.astype(jnp.bfloat16).reshape(half, latents, local)


def combine_last(mixed, weights, total, whole):
    stripes, caps, latents, local = whole.shape
    half = total.shape[0] // stripes // latents
    operands = (*mixed, *weights, total)
    specs = [pl.BlockSpec(array.shape, lambda i: (0, 0)) for array in operands]
    return pl.pallas_call(
        combine_last_kernel,
        grid=(1,),
        in_specs=specs + [pl.BlockSpec(memory_space=pl.ANY)],
        out_specs=pl.BlockSpec((stripes, half, latents, local), lambda i: (0, 0, 0, 0)),
        out_shape=jax.ShapeDtypeStruct(whole.shape, whole.dtype),
        input_output_aliases={len(operands): 0},
        compiler_params=params(20),
        cost_estimate=pl.CostEstimate(flops=12 * total.size * local, bytes_accessed=10 * total.size, transcendentals=0),
        name="combine_last",
    )(*operands, whole)


def combine(kernel, place, groups, weights, out_shape, rest=()):
    operands = (*groups, *weights, *rest)
    rows, local = groups[0].shape
    vmem = pl.BlockSpec(memory_space=pltpu.VMEM)
    return pl.pallas_call(
        kernel,
        in_specs=[pl.BlockSpec(memory_space=pltpu.SMEM)] + [vmem] * len(operands),
        out_specs=jax.tree.map(lambda _: vmem, out_shape),
        out_shape=out_shape,
        compiler_params=params(20),
        cost_estimate=pl.CostEstimate(
            flops=0, bytes_accessed=0, transcendentals=0
        ),
        name="combine_groups",
    )(place, *operands)


def swap(array, axis_name, distance):
    size = lax.axis_size(axis_name)
    return lax.ppermute(array, axis_name, [(i, i ^ distance) for i in range(size)])


def follow(array, *others):
    return lax.optimization_barrier((array, *others))[0]


def spread_heads(mixed, others=()):
    second = swap(mixed, "head", 2)
    return mixed, swap(mixed, "head", 1), second, swap(follow(second, *others), "head", 1)


def exchange(array, stripes):
    array = array.reshape(stripes, -1, *array.shape[1:])
    return lax.all_to_all(array, "lat", split_axis=0, concat_axis=0, tiled=True)


def spread_weight(out_weight, head):
    local = out_weight.shape[0]
    parts = []
    for distance in range(lax.axis_size("head")):
        start = jnp.bitwise_xor(head, distance) * local
        part = lax.dynamic_slice_in_dim(out_weight, start, local, 1)
        parts.append(swap(part, "head", distance) if distance else part)
    return parts


def shards(level_tokens, ln_gain, key_weight, value_weight, out_weight, ocean_queries, send_slots):
    stripes = lax.axis_size("lat")
    caps = send_slots.shape[2]
    shape = ocean_queries.shape
    slots, latents, local = shape
    place = lax.axis_index("lat").reshape(1)
    halves = 2 if caps == BLOCK else 1
    queries = exchange(ocean_queries, stripes).reshape(stripes, halves, -1, local)
    weights = spread_weight(out_weight, lax.axis_index("head"))
    tokens = jnp.transpose(level_tokens, (1, 0, 2))
    levels = tokens.shape[0]
    pairs = project(send_slots[0], tokens, ln_gain, key_weight, value_weight, halves)
    pairs, weights = lax.optimization_barrier((pairs, weights))
    whole = jax.ShapeDtypeStruct((stripes, caps, latents, local), jnp.bfloat16)
    if halves == 1:
        mixed = exchange(attend(queries, pairs, levels)[0], stripes).reshape(-1, local)
        return combine(combine_kernel, place, spread_heads(mixed), weights, whole).reshape(shape)
    early, late = attend(queries, pairs, levels)
    chunks = [jax.ShapeDtypeStruct((caps // 2, latents, local), jnp.bfloat16)] * stripes
    chunks = combine(combine_home_kernel, place, spread_heads(late), weights, chunks)
    chunks = [swap(chunk, "lat", distance) if distance else chunk for distance, chunk in enumerate(chunks)]
    near, far = chunks[: stripes // 2], chunks[stripes // 2 :]
    early = follow(exchange(early, stripes), *near).reshape(-1, local)
    own, across, second, third = spread_heads(early, far)
    most_shape = (whole, jax.ShapeDtypeStruct(early.shape, jnp.float32))
    out, total = combine(combine_most_kernel, place, (own, second), weights[::2], most_shape, chunks)
    return combine_last((across, third), weights[1::2], total, out).reshape(shape)


def solution(mesh):
    return jax.shard_map(
        shards,
        mesh=mesh,
        in_specs=(
            P("lat", None, None),
            P(),
            P(None, "head"),
            P(None, "head"),
            P("head", None),
            P("lat", None, "head"),
            P("lat", None, None),
        ),
        out_specs=P("lat", None, "head"),
        check_vma=False,
    )
```

```python
import functools
import math

import jax
import jax.numpy as jnp
from jax import lax
from jax.experimental import pallas as pl
from jax.experimental.pallas import tpu as pltpu
from jax.sharding import PartitionSpec as P

HEAD_DIM = 64
EPS = 1e-05
GROUP = 8
BLOCK = 64
STEP_BLOCKS = 2
STAGE = 128
ROWS = 32
MIB = 1024 * 1024


def params(mib):
    return pltpu.CompilerParams(vmem_limit_bytes=mib * MIB)


def normalize_rows(tokens, gain):
    width = tokens.shape[-1]
    tokens = tokens.astype(jnp.float32)
    center = jnp.sum(tokens, axis=-1, keepdims=True) * (1.0 / width)
    shifted = tokens - center
    spread = jnp.sum(shifted * shifted, axis=-1, keepdims=True) * (1.0 / width)
    return (shifted * lax.rsqrt(spread + EPS) * gain).astype(jnp.bfloat16)


def build_pick(slots_ref, pick_ref, halves):
    stripes, caps = slots_ref.shape
    half = caps // halves
    diagonal = lax.broadcasted_iota(jnp.int32, (caps, caps), 0) == lax.broadcasted_iota(jnp.int32, (caps, caps), 1)
    patch = lax.broadcasted_iota(jnp.int32, (caps, pick_ref.shape[1]), 1)
    for owner in range(stripes):
        row = jnp.broadcast_to(slots_ref[owner : owner + 1, :], (caps, caps))
        column = jnp.sum(jnp.where(diagonal, row, 0), axis=-1, keepdims=True)
        pick = jnp.where(patch == column, 1.0, 0.0).astype(jnp.bfloat16)
        for index in range(halves):
            start = (index * stripes + owner) * half
            pick_ref[start : start + half, :] = pick[index * half : (index + 1) * half]


def project_kernel(
    halves,
    slots_ref,
    gain_ref,
    key_weight_ref,
    value_weight_ref,
    even_ref,
    odd_ref,
    out_ref,
    normed_ref,
    pick_ref,
    weight_ref,
):
    patches = even_ref.shape[1]
    local = key_weight_ref.shape[1]

    @pl.when(pl.program_id(0) == 0)
    def _():
        build_pick(slots_ref, pick_ref, halves)
        weight_ref[:, :local] = key_weight_ref[...]
        weight_ref[:, local:] = value_weight_ref[...]

    gain = gain_ref[...]
    for index, tokens_ref in enumerate((even_ref, odd_ref)):
        for start in range(0, patches, ROWS):
            normed = normalize_rows(tokens_ref[0, pl.ds(start, ROWS), :], gain)
            normed_ref[pl.ds(index * patches + start, ROWS), :] = normed
    product = jnp.dot(normed_ref[...], weight_ref[...], preferred_element_type=jnp.float32).astype(jnp.bfloat16)
    product = jnp.concatenate([product[:patches], product[patches:]], axis=1)
    picked = jnp.dot(pick_ref[...], product, preferred_element_type=jnp.float32)
    groups = picked.shape[0] // GROUP
    picked = [
        picked[:, index * 2 * local : (index + 1) * 2 * local].reshape(groups, 1, GROUP, 2 * local) for index in range(2)
    ]
    picked = jnp.concatenate(picked, axis=1).reshape(out_ref.shape[0], 2 * BLOCK, 2 * local)
    out_ref[:, 0] = picked.astype(jnp.bfloat16)


def project(slots, tokens, gain, key_weight, value_weight, halves):
    levels, patches, width = tokens.shape
    local = key_weight.shape[1]
    count = slots.size
    steps = (levels + 1) // 2
    whole = lambda i: (0, 0)
    return pl.pallas_call(
        functools.partial(project_kernel, halves),
        grid=(steps,),
        in_specs=[
            pl.BlockSpec(slots.shape, whole),
            pl.BlockSpec((1, width), whole),
            pl.BlockSpec((width, local), whole),
            pl.BlockSpec((width, local), whole),
            pl.BlockSpec((1, patches, width), lambda i: (2 * i, 0, 0)),
            pl.BlockSpec((1, patches, width), lambda i: (jnp.minimum(2 * i + 1, levels - 1), 0, 0)),
        ],
        out_specs=pl.BlockSpec((count // BLOCK, 1, 2 * BLOCK, 2 * local), lambda i: (0, i, 0, 0)),
        out_shape=jax.ShapeDtypeStruct((count // BLOCK, steps, 2 * BLOCK, 2 * local), jnp.bfloat16),
        scratch_shapes=[
            pltpu.VMEM((2 * patches, width), jnp.bfloat16),
            pltpu.VMEM((count, patches), jnp.bfloat16),
            pltpu.VMEM((width, 2 * local), jnp.bfloat16),
        ],
        compiler_params=params(58),
        cost_estimate=pl.CostEstimate(
            flops=8 * levels * patches * (width + count) * local,
            bytes_accessed=2 * levels * patches * (width + 2 * local) + 4 * width * local,
            transcendentals=0,
        ),
        name="norm_project",
    )(slots, gain.reshape(1, width), key_weight, value_weight, tokens, tokens)


def attend_kernel(levels, query_ref, pair_ref, *refs):
    out_ref = refs[-1]
    blocks, level_pairs, block, local = pair_ref.shape
    block, local = block // 2, local // 2
    slots = blocks * block
    latents = out_ref.shape[0] // slots
    rows = GROUP * latents
    heads = local // HEAD_DIM
    columns = level_pairs * 2 * GROUP
    lane_head = lax.broadcasted_iota(jnp.int32, (rows, local), 1) // HEAD_DIM
    row_slot = lax.broadcasted_iota(jnp.int32, (GROUP, heads * rows), 0)
    column_slot = (lax.broadcasted_iota(jnp.int32, (GROUP, heads * rows), 1) // latents) & (GROUP - 1)
    same = row_slot - column_slot == 0
    scale = math.log2(math.e) / math.sqrt(HEAD_DIM)
    queries = query_ref[...].reshape(slots * latents, local).astype(jnp.float32)

    def columns_of(start, lane):
        part = pl.ds(start % block * 2, 2 * GROUP)
        return pair_ref[start // block, :, part, pl.ds(lane, local)].reshape(columns, local)

    for first in range(0, slots, STAGE):
        tasks = range(first, first + STAGE, GROUP)
        scores = []
        for start in tasks:
            part = queries[start * latents : start * latents + rows]
            part = jnp.concatenate(
                [jnp.where(lane_head == head, part, 0.0).astype(jnp.bfloat16) for head in range(heads)], axis=0
            )
            product = lax.dot_general(
                columns_of(start, 0), part, (((1,), (1,)), ((), ())), preferred_element_type=jnp.float32
            )
            scores.append(product.reshape(2 * level_pairs, GROUP, heads * rows))
        softs = []
        for product in scores:
            product = product[:levels]
            expo = jnp.exp2((product - jnp.max(product, axis=0, keepdims=True)) * scale)
            inverse = jnp.where(same, 1.0 / jnp.sum(expo, axis=0), 0.0)
            soft = expo * inverse[None]
            if levels < 2 * level_pairs:
                soft = jnp.concatenate([soft, jnp.zeros_like(soft[:1])], axis=0)
            softs.append(soft.reshape(columns, heads * rows).astype(jnp.bfloat16))
        for start, soft in zip(tasks, softs):
            wide = lax.dot_general(
                soft, columns_of(start, local), (((0,), (0,)), ((), ())), preferred_element_type=jnp.float32
            )
            mixed = wide[:rows]
            for head in range(1, heads):
                mixed = jnp.where(lane_head == head, wide[head * rows : (head + 1) * rows], mixed)
            out_ref[pl.ds(start * latents, rows), :] = mixed.astype(jnp.bfloat16)


def attend(queries, pairs, levels, index, after=()):
    stripes, halves, rows, local = queries.shape
    steps = pairs.shape[0] // halves // STEP_BLOCKS
    block = stripes * rows // steps
    pair_shape = (STEP_BLOCKS, *pairs.shape[1:])
    return pl.pallas_call(
        functools.partial(attend_kernel, levels),
        grid=(steps,),
        in_specs=[
            pl.BlockSpec((stripes // steps, 1, rows, local), lambda i: (i, index, 0, 0)),
            pl.BlockSpec(pair_shape, lambda i: (index * steps + i, 0, 0, 0)),
        ]
        + [pl.BlockSpec(memory_space=pl.ANY)] * len(after),
        out_specs=pl.BlockSpec((block, local), lambda i: (i, 0)),
        out_shape=jax.ShapeDtypeStruct((steps * block, local), jnp.bfloat16),
        compiler_params=params(55),
        cost_estimate=pl.CostEstimate(
            flops=1024 * steps * block * levels * local,
            bytes_accessed=4 * steps * (block + levels * STEP_BLOCKS * BLOCK) * local,
            transcendentals=0,
        ),
        name="attend_slots",
    )(queries, pairs, *after)


def combine_rows(mixed_refs, weight_refs, part):
    total = None
    for mixed_ref, weight_ref in zip(mixed_refs, weight_refs):
        term = jnp.dot(mixed_ref[part, :], weight_ref[...], preferred_element_type=jnp.float32)
        term = term.astype(jnp.bfloat16).astype(jnp.float32)
        total = term if total is None else total + term
    return total.astype(jnp.bfloat16)


def combine_home_kernel(place_ref, *refs):
    for distance, out_ref in enumerate(refs[8:]):
        rows = out_ref.shape[0] * out_ref.shape[1]
        start = jnp.bitwise_xor(place_ref[0], distance) * rows
        part = pl.ds(pl.multiple_of(start, rows), rows)
        out_ref[...] = combine_rows(refs[:4], refs[4:8], part).reshape(out_ref.shape)


def combine_kernel(place_ref, *refs):
    out_ref = refs[-1]
    stripes, caps, latents, local = out_ref.shape
    for stripe in range(stripes):
        part = pl.ds(stripe * caps * latents, caps * latents)
        rows = combine_rows(refs[:4], refs[4:8], part)
        out_ref[stripe] = rows.reshape(caps, latents, local)


def term_of(mixed_ref, weight_ref, part):
    term = jnp.dot(mixed_ref[part, :], weight_ref[...], preferred_element_type=jnp.float32)
    return term.astype(jnp.bfloat16).astype(jnp.float32)


def combine_most_kernel(place_ref, *refs):
    out_ref, total_ref = refs[-2:]
    rest = refs[4:-2]
    stripes = out_ref.shape[0]
    half = out_ref.shape[1] - rest[0].shape[0]
    for distance, ref in enumerate(rest):
        out_ref[jnp.bitwise_xor(place_ref[0], distance), half:] = ref[...]
    rows = total_ref.shape[0] // stripes
    for stripe in range(stripes):
        part = pl.ds(stripe * rows, rows)
        total_ref[part, :] = term_of(refs[0], refs[2], part) + term_of(refs[1], refs[3], part)


def combine_last_kernel(first_ref, second_ref, first_weight_ref, second_weight_ref, total_ref, whole_ref, out_ref):
    stripes, half, latents, local = out_ref.shape
    rows = half * latents
    for stripe in range(stripes):
        part = pl.ds(stripe * rows, rows)
        total = total_ref[part, :] + term_of(first_ref, first_weight_ref, part)
        total = total + term_of(second_ref, second_weight_ref, part)
        out_ref[stripe] = total.astype(jnp.bfloat16).reshape(half, latents, local)


def combine_last(mixed, weights, total, whole):
    stripes, caps, latents, local = whole.shape
    half = total.shape[0] // stripes // latents
    operands = (*mixed, *weights, total)
    specs = [pl.BlockSpec(array.shape, lambda i: (0, 0)) for array in operands]
    return pl.pallas_call(
        combine_last_kernel,
        grid=(1,),
        in_specs=specs + [pl.BlockSpec(memory_space=pl.ANY)],
        out_specs=pl.BlockSpec((stripes, half, latents, local), lambda i: (0, 0, 0, 0)),
        out_shape=jax.ShapeDtypeStruct(whole.shape, whole.dtype),
        input_output_aliases={len(operands): 0},
        compiler_params=params(20),
        cost_estimate=pl.CostEstimate(flops=12 * total.size * local, bytes_accessed=10 * total.size, transcendentals=0),
        name="combine_last",
    )(*operands, whole)


def combine(kernel, place, groups, weights, out_shape, rest=()):
    operands = (*groups, *weights, *rest)
    rows, local = groups[0].shape
    vmem = pl.BlockSpec(memory_space=pltpu.VMEM)
    return pl.pallas_call(
        kernel,
        in_specs=[pl.BlockSpec(memory_space=pltpu.SMEM)] + [vmem] * len(operands),
        out_specs=jax.tree.map(lambda _: vmem, out_shape),
        out_shape=out_shape,
        compiler_params=params(20),
        cost_estimate=pl.CostEstimate(
            flops=24 * rows * local * local, bytes_accessed=10 * rows * local, transcendentals=0
        ),
        name="combine_groups",
    )(place, *operands)


def swap(array, axis_name, distance):
    size = lax.axis_size(axis_name)
    return lax.ppermute(array, axis_name, [(i, i ^ distance) for i in range(size)])


def follow(array, *others):
    return lax.optimization_barrier((array, *others))[0]


def spread_heads(mixed, others=()):
    second = swap(mixed, "head", 2)
    return mixed, swap(mixed, "head", 1), second, swap(follow(second, *others), "head", 1)


def exchange(array, stripes):
    array = array.reshape(stripes, -1, *array.shape[1:])
    return lax.all_to_all(array, "lat", split_axis=0, concat_axis=0, tiled=True)


def spread_weight(out_weight, head):
    local = out_weight.shape[0]
    parts = []
    for distance in range(lax.axis_size("head")):
        start = jnp.bitwise_xor(head, distance) * local
        part = lax.dynamic_slice_in_dim(out_weight, start, local, 1)
        parts.append(swap(part, "head", distance) if distance else part)
    return parts


def shards(level_tokens, ln_gain, key_weight, value_weight, out_weight, ocean_queries, send_slots):
    stripes = lax.axis_size("lat")
    caps = send_slots.shape[2]
    shape = ocean_queries.shape
    slots, latents, local = shape
    place = lax.axis_index("lat").reshape(1)
    halves = 2 if caps == BLOCK else 1
    queries = exchange(ocean_queries, stripes).reshape(stripes, halves, -1, local)
    weights = spread_weight(out_weight, lax.axis_index("head"))
    tokens = jnp.transpose(level_tokens, (1, 0, 2))
    levels = tokens.shape[0]
    pairs = project(send_slots[0], tokens, ln_gain, key_weight, value_weight, halves)
    pairs, weights = lax.optimization_barrier((pairs, weights))
    whole = jax.ShapeDtypeStruct((stripes, caps, latents, local), jnp.bfloat16)
    if halves == 1:
        mixed = exchange(attend(queries, pairs, levels, 0), stripes).reshape(-1, local)
        return combine(combine_kernel, place, spread_heads(mixed), weights, whole).reshape(shape)
    late = attend(queries, pairs, levels, 1)
    early = attend(queries, pairs, levels, 0, (late,))
    chunks = [jax.ShapeDtypeStruct((caps // 2, latents, local), jnp.bfloat16)] * stripes
    chunks = combine(combine_home_kernel, place, spread_heads(late, (early,)), weights, chunks)
    order = [*range(stripes // 2 - 1, 0, -1), *range(stripes // 2, stripes)]
    moved = {distance: swap(chunks[distance], "lat", distance) for distance in order}
    near = [moved[distance] for distance in order[: stripes // 2 - 1]]
    far = [moved[distance] for distance in order[stripes // 2 - 1 :]]
    chunks = [chunks[0], *(moved[distance] for distance in range(1, stripes))]
    early = follow(exchange(early, stripes), *near).reshape(-1, local)
    own, across, second, third = spread_heads(early, far)
    most_shape = (whole, jax.ShapeDtypeStruct(early.shape, jnp.float32))
    out, total = combine(combine_most_kernel, place, (own, second), weights[::2], most_shape, chunks)
    return combine_last((across, third), weights[1::2], total, out).reshape(shape)


def solution(mesh):
    return jax.shard_map(
        shards,
        mesh=mesh,
        in_specs=(
            P("lat", None, None),
            P(),
            P(None, "head"),
            P(None, "head"),
            P("head", None),
            P("lat", None, "head"),
            P("lat", None, None),
        ),
        out_specs=P("lat", None, "head"),
        check_vma=False,
    )
```

```python
import functools
import math

import jax
import jax.numpy as jnp
from jax import lax
from jax.experimental import pallas as pl
from jax.experimental.pallas import tpu as pltpu
from jax.sharding import PartitionSpec as P

HEAD_DIM = 64
EPS = 1e-05
GROUP = 8
BLOCK = 64
STEP_BLOCKS = 2
STAGE = 128
ROWS = 32
MIB = 1024 * 1024


def params(mib):
    return pltpu.CompilerParams(vmem_limit_bytes=mib * MIB)


def normalize_rows(tokens, gain):
    width = tokens.shape[-1]
    tokens = tokens.astype(jnp.float32)
    center = jnp.sum(tokens, axis=-1, keepdims=True) * (1.0 / width)
    shifted = tokens - center
    spread = jnp.sum(shifted * shifted, axis=-1, keepdims=True) * (1.0 / width)
    return (shifted * lax.rsqrt(spread + EPS) * gain).astype(jnp.bfloat16)


def build_pick(slots_ref, pick_ref, halves):
    stripes, caps = slots_ref.shape
    half = caps // halves
    diagonal = lax.broadcasted_iota(jnp.int32, (caps, caps), 0) == lax.broadcasted_iota(jnp.int32, (caps, caps), 1)
    patch = lax.broadcasted_iota(jnp.int32, (caps, pick_ref.shape[1]), 1)
    for owner in range(stripes):
        row = jnp.broadcast_to(slots_ref[owner : owner + 1, :], (caps, caps))
        column = jnp.sum(jnp.where(diagonal, row, 0), axis=-1, keepdims=True)
        pick = jnp.where(patch == column, 1.0, 0.0).astype(jnp.bfloat16)
        for index in range(halves):
            start = (index * stripes + owner) * half
            pick_ref[start : start + half, :] = pick[index * half : (index + 1) * half]


def project_kernel(
    halves,
    levels,
    slots_ref,
    gain_ref,
    key_weight_ref,
    value_weight_ref,
    even_ref,
    odd_ref,
    out_ref,
    normed_ref,
    pick_ref,
    weight_ref,
):
    patches = even_ref.shape[1]
    local = key_weight_ref.shape[1]

    @pl.when(pl.program_id(0) == 0)
    def _():
        build_pick(slots_ref, pick_ref, halves)
        weight_ref[:, :local] = key_weight_ref[...]
        weight_ref[:, local:] = value_weight_ref[...]

    def multiply(tokens_refs):
        gain = gain_ref[...]
        count = len(tokens_refs)
        for index, tokens_ref in enumerate(tokens_refs):
            for start in range(0, patches, ROWS):
                normed = normalize_rows(tokens_ref[0, pl.ds(start, ROWS), :], gain)
                normed_ref[pl.ds(index * patches + start, ROWS), :] = normed
        normed = normed_ref[pl.ds(0, count * patches), :]
        product = jnp.dot(normed, weight_ref[...], preferred_element_type=jnp.float32).astype(jnp.bfloat16)
        product = jnp.concatenate([product[i * patches : (i + 1) * patches] for i in range(count)], axis=1)
        picked = jnp.dot(pick_ref[...], product, preferred_element_type=jnp.float32)
        groups = picked.shape[0] // GROUP
        picked = [
            picked[:, i * 2 * local : (i + 1) * 2 * local].reshape(groups, 1, GROUP, 2 * local) for i in range(count)
        ]
        if count == 1:
            picked.append(jnp.zeros_like(picked[0]))
        picked = jnp.concatenate(picked, axis=1).reshape(out_ref.shape[0], 2 * BLOCK, 2 * local)
        out_ref[:, 0] = picked.astype(jnp.bfloat16)

    single = levels % 2 == 1
    last = pl.num_programs(0) - 1

    @pl.when((pl.program_id(0) < last) | (not single))
    def _():
        multiply((even_ref, odd_ref))

    if single:

        @pl.when(pl.program_id(0) == last)
        def _():
            multiply((even_ref,))


def project(slots, tokens, gain, key_weight, value_weight, halves):
    levels, patches, width = tokens.shape
    local = key_weight.shape[1]
    count = slots.size
    steps = (levels + 1) // 2
    whole = lambda i: (0, 0)
    return pl.pallas_call(
        functools.partial(project_kernel, halves, levels),
        grid=(steps,),
        in_specs=[
            pl.BlockSpec(slots.shape, whole),
            pl.BlockSpec((1, width), whole),
            pl.BlockSpec((width, local), whole),
            pl.BlockSpec((width, local), whole),
            pl.BlockSpec((1, patches, width), lambda i: (2 * i, 0, 0)),
            pl.BlockSpec((1, patches, width), lambda i: (jnp.minimum(2 * i + 1, levels - 1), 0, 0)),
        ],
        out_specs=pl.BlockSpec((count // BLOCK, 1, 2 * BLOCK, 2 * local), lambda i: (0, i, 0, 0)),
        out_shape=jax.ShapeDtypeStruct((count // BLOCK, steps, 2 * BLOCK, 2 * local), jnp.bfloat16),
        scratch_shapes=[
            pltpu.VMEM((2 * patches, width), jnp.bfloat16),
            pltpu.VMEM((count, patches), jnp.bfloat16),
            pltpu.VMEM((width, 2 * local), jnp.bfloat16),
        ],
        compiler_params=params(58),
        cost_estimate=pl.CostEstimate(
            flops=8 * levels * patches * (width + count) * local,
            bytes_accessed=2 * levels * patches * (width + 2 * local) + 4 * width * local,
            transcendentals=0,
        ),
        name="norm_project",
    )(slots, gain.reshape(1, width), key_weight, value_weight, tokens, tokens)


def attend_kernel(levels, query_ref, pair_ref, *refs):
    out_ref = refs[-1]
    blocks, level_pairs, block, local = pair_ref.shape
    block, local = block // 2, local // 2
    slots = blocks * block
    latents = out_ref.shape[0] // slots
    rows = GROUP * latents
    heads = local // HEAD_DIM
    columns = level_pairs * 2 * GROUP
    lane_head = lax.broadcasted_iota(jnp.int32, (rows, local), 1) // HEAD_DIM
    row_slot = lax.broadcasted_iota(jnp.int32, (GROUP, heads * rows), 0)
    column_slot = (lax.broadcasted_iota(jnp.int32, (GROUP, heads * rows), 1) // latents) & (GROUP - 1)
    same = row_slot - column_slot == 0
    scale = math.log2(math.e) / math.sqrt(HEAD_DIM)
    queries = query_ref[...].reshape(slots * latents, local).astype(jnp.float32)

    def columns_of(start, lane):
        part = pl.ds(start % block * 2, 2 * GROUP)
        return pair_ref[start // block, :, part, pl.ds(lane, local)].reshape(columns, local)

    for first in range(0, slots, STAGE):
        tasks = range(first, first + STAGE, GROUP)
        scores = []
        for start in tasks:
            part = queries[start * latents : start * latents + rows]
            part = jnp.concatenate(
                [jnp.where(lane_head == head, part, 0.0).astype(jnp.bfloat16) for head in range(heads)], axis=0
            )
            product = lax.dot_general(
                columns_of(start, 0), part, (((1,), (1,)), ((), ())), preferred_element_type=jnp.float32
            )
            scores.append(product.reshape(2 * level_pairs, GROUP, heads * rows))
        softs = []
        for product in scores:
            product = product[:levels]
            expo = jnp.exp2((product - jnp.max(product, axis=0, keepdims=True)) * scale)
            inverse = jnp.where(same, 1.0 / jnp.sum(expo, axis=0), 0.0)
            soft = expo * inverse[None]
            if levels < 2 * level_pairs:
                soft = jnp.concatenate([soft, jnp.zeros_like(soft[:1])], axis=0)
            softs.append(soft.reshape(columns, heads * rows).astype(jnp.bfloat16))
        for start, soft in zip(tasks, softs):
            wide = lax.dot_general(
                soft, columns_of(start, local), (((0,), (0,)), ((), ())), preferred_element_type=jnp.float32
            )
            mixed = wide[:rows]
            for head in range(1, heads):
                mixed = jnp.where(lane_head == head, wide[head * rows : (head + 1) * rows], mixed)
            out_ref[pl.ds(start * latents, rows), :] = mixed.astype(jnp.bfloat16)


def attend(queries, pairs, levels, index, after=()):
    stripes, halves, rows, local = queries.shape
    steps = pairs.shape[0] // halves // STEP_BLOCKS
    block = stripes * rows // steps
    pair_shape = (STEP_BLOCKS, *pairs.shape[1:])
    return pl.pallas_call(
        functools.partial(attend_kernel, levels),
        grid=(steps,),
        in_specs=[
            pl.BlockSpec((stripes // steps, 1, rows, local), lambda i: (i, index, 0, 0)),
            pl.BlockSpec(pair_shape, lambda i: (index * steps + i, 0, 0, 0)),
        ]
        + [pl.BlockSpec(memory_space=pl.ANY)] * len(after),
        out_specs=pl.BlockSpec((block, local), lambda i: (i, 0)),
        out_shape=jax.ShapeDtypeStruct((steps * block, local), jnp.bfloat16),
        compiler_params=params(55),
        cost_estimate=pl.CostEstimate(
            flops=1024 * steps * block * levels * local,
            bytes_accessed=4 * steps * (block + levels * STEP_BLOCKS * BLOCK) * local,
            transcendentals=0,
        ),
        name="attend_slots",
    )(queries, pairs, *after)


def combine_rows(mixed_refs, weight_refs, part):
    total = None
    for mixed_ref, weight_ref in zip(mixed_refs, weight_refs):
        term = jnp.dot(mixed_ref[part, :], weight_ref[...], preferred_element_type=jnp.float32)
        term = term.astype(jnp.bfloat16).astype(jnp.float32)
        total = term if total is None else total + term
    return total.astype(jnp.bfloat16)


def combine_home_kernel(place_ref, *refs):
    for distance, out_ref in enumerate(refs[8:]):
        rows = out_ref.shape[0] * out_ref.shape[1]
        start = jnp.bitwise_xor(place_ref[0], distance) * rows
        part = pl.ds(pl.multiple_of(start, rows), rows)
        out_ref[...] = combine_rows(refs[:4], refs[4:8], part).reshape(out_ref.shape)


def combine_kernel(place_ref, *refs):
    out_ref = refs[-1]
    stripes, caps, latents, local = out_ref.shape
    for stripe in range(stripes):
        part = pl.ds(stripe * caps * latents, caps * latents)
        rows = combine_rows(refs[:4], refs[4:8], part)
        out_ref[stripe] = rows.reshape(caps, latents, local)


def term_of(mixed_ref, weight_ref, part):
    term = jnp.dot(mixed_ref[part, :], weight_ref[...], preferred_element_type=jnp.float32)
    return term.astype(jnp.bfloat16).astype(jnp.float32)


def combine_most_kernel(place_ref, *refs):
    out_ref, total_ref = refs[-2:]
    rest = refs[4:-2]
    stripes = out_ref.shape[0]
    half = out_ref.shape[1] - rest[0].shape[0]
    for distance, ref in enumerate(rest):
        out_ref[jnp.bitwise_xor(place_ref[0], distance), half:] = ref[...]
    rows = total_ref.shape[0] // stripes
    for stripe in range(stripes):
        part = pl.ds(stripe * rows, rows)
        total_ref[part, :] = term_of(refs[0], refs[2], part) + term_of(refs[1], refs[3], part)


def combine_last_kernel(first_ref, second_ref, first_weight_ref, second_weight_ref, total_ref, whole_ref, out_ref):
    stripes, half, latents, local = out_ref.shape
    rows = half * latents
    for stripe in range(stripes):
        part = pl.ds(stripe * rows, rows)
        total = total_ref[part, :] + term_of(first_ref, first_weight_ref, part)
        total = total + term_of(second_ref, second_weight_ref, part)
        out_ref[stripe] = total.astype(jnp.bfloat16).reshape(half, latents, local)


def combine_last(mixed, weights, total, whole):
    stripes, caps, latents, local = whole.shape
    half = total.shape[0] // stripes // latents
    operands = (*mixed, *weights, total)
    specs = [pl.BlockSpec(array.shape, lambda i: (0, 0)) for array in operands]
    return pl.pallas_call(
        combine_last_kernel,
        grid=(1,),
        in_specs=specs + [pl.BlockSpec(memory_space=pl.ANY)],
        out_specs=pl.BlockSpec((stripes, half, latents, local), lambda i: (0, 0, 0, 0)),
        out_shape=jax.ShapeDtypeStruct(whole.shape, whole.dtype),
        input_output_aliases={len(operands): 0},
        compiler_params=params(20),
        cost_estimate=pl.CostEstimate(flops=12 * total.size * local, bytes_accessed=10 * total.size, transcendentals=0),
        name="combine_last",
    )(*operands, whole)


def combine(kernel, place, groups, weights, out_shape, rest=()):
    operands = (*groups, *weights, *rest)
    rows, local = groups[0].shape
    vmem = pl.BlockSpec(memory_space=pltpu.VMEM)
    return pl.pallas_call(
        kernel,
        in_specs=[pl.BlockSpec(memory_space=pltpu.SMEM)] + [vmem] * len(operands),
        out_specs=jax.tree.map(lambda _: vmem, out_shape),
        out_shape=out_shape,
        compiler_params=params(20),
        cost_estimate=pl.CostEstimate(
            flops=24 * rows * local * local, bytes_accessed=10 * rows * local, transcendentals=0
        ),
        name="combine_groups",
    )(place, *operands)


def swap(array, axis_name, distance):
    size = lax.axis_size(axis_name)
    return lax.ppermute(array, axis_name, [(i, i ^ distance) for i in range(size)])


def follow(array, *others):
    return lax.optimization_barrier((array, *others))[0]


def spread_heads(mixed, others=()):
    second = swap(mixed, "head", 2)
    return mixed, swap(mixed, "head", 1), second, swap(follow(second, *others), "head", 1)


def exchange(array, stripes):
    array = array.reshape(stripes, -1, *array.shape[1:])
    return lax.all_to_all(array, "lat", split_axis=0, concat_axis=0, tiled=True)


def spread_weight(out_weight, head):
    local = out_weight.shape[0]
    parts = []
    for distance in range(lax.axis_size("head")):
        start = jnp.bitwise_xor(head, distance) * local
        part = lax.dynamic_slice_in_dim(out_weight, start, local, 1)
        parts.append(swap(part, "head", distance) if distance else part)
    return parts


def shards(level_tokens, ln_gain, key_weight, value_weight, out_weight, ocean_queries, send_slots):
    stripes = lax.axis_size("lat")
    caps = send_slots.shape[2]
    shape = ocean_queries.shape
    slots, latents, local = shape
    place = lax.axis_index("lat").reshape(1)
    halves = 2 if caps == BLOCK else 1
    queries = exchange(ocean_queries, stripes).reshape(stripes, halves, -1, local)
    weights = spread_weight(out_weight, lax.axis_index("head"))
    tokens = jnp.transpose(level_tokens, (1, 0, 2))
    levels = tokens.shape[0]
    pairs = project(send_slots[0], tokens, ln_gain, key_weight, value_weight, halves)
    pairs, weights = lax.optimization_barrier((pairs, weights))
    whole = jax.ShapeDtypeStruct((stripes, caps, latents, local), jnp.bfloat16)
    if halves == 1:
        mixed = exchange(attend(queries, pairs, levels, 0), stripes).reshape(-1, local)
        return combine(combine_kernel, place, spread_heads(mixed), weights, whole).reshape(shape)
    late = attend(queries, pairs, levels, 1)
    early = attend(queries, pairs, levels, 0, (late,))
    chunks = [jax.ShapeDtypeStruct((caps // 2, latents, local), jnp.bfloat16)] * stripes
    chunks = combine(combine_home_kernel, place, spread_heads(late, (early,)), weights, chunks)
    order = [*range(1, stripes // 2), *range(stripes - 1, stripes // 2 - 1, -1)]
    moved = {distance: swap(chunks[distance], "lat", distance) for distance in order}
    chunks = [chunks[0], *(moved[distance] for distance in range(1, stripes))]
    near, far = chunks[: stripes // 2], [moved[distance] for distance in order[stripes // 2 - 1 :]]
    early = follow(exchange(early, stripes), *near).reshape(-1, local)
    own, across, second, third = spread_heads(early, far)
    most_shape = (whole, jax.ShapeDtypeStruct(early.shape, jnp.float32))
    out, total = combine(combine_most_kernel, place, (own, second), weights[::2], most_shape, chunks)
    return combine_last((across, third), weights[1::2], total, out).reshape(shape)


def solution(mesh):
    return jax.shard_map(
        shards,
        mesh=mesh,
        in_specs=(
            P("lat", None, None),
            P(),
            P(None, "head"),
            P(None, "head"),
            P("head", None),
            P("lat", None, "head"),
            P("lat", None, None),
        ),
        out_specs=P("lat", None, "head"),
        check_vma=False,
    )
```

```python
import functools
import math

import jax
import jax.numpy as jnp
from jax import lax
from jax.experimental import pallas as pl
from jax.experimental.pallas import tpu as pltpu
from jax.sharding import PartitionSpec as P

HEAD_DIM = 64
EPS = 1e-05
GROUP = 8
BLOCK = 64
STEP_BLOCKS = 2
STAGE = 128
ROWS = 32
MIB = 1024 * 1024


def params(mib):
    return pltpu.CompilerParams(vmem_limit_bytes=mib * MIB)


def normalize_rows(tokens, gain):
    width = tokens.shape[-1]
    tokens = tokens.astype(jnp.float32)
    center = jnp.sum(tokens, axis=-1, keepdims=True) * (1.0 / width)
    shifted = tokens - center
    spread = jnp.sum(shifted * shifted, axis=-1, keepdims=True) * (1.0 / width)
    return (shifted * lax.rsqrt(spread + EPS) * gain).astype(jnp.bfloat16)


def build_pick(slots_ref, pick_ref, halves):
    stripes, caps = slots_ref.shape
    half = caps // halves
    diagonal = lax.broadcasted_iota(jnp.int32, (caps, caps), 0) == lax.broadcasted_iota(jnp.int32, (caps, caps), 1)
    patch = lax.broadcasted_iota(jnp.int32, (caps, pick_ref.shape[1]), 1)
    for owner in range(stripes):
        row = jnp.broadcast_to(slots_ref[owner : owner + 1, :], (caps, caps))
        column = jnp.sum(jnp.where(diagonal, row, 0), axis=-1, keepdims=True)
        pick = jnp.where(patch == column, 1.0, 0.0).astype(jnp.bfloat16)
        for index in range(halves):
            start = (index * stripes + owner) * half
            pick_ref[start : start + half, :] = pick[index * half : (index + 1) * half]


def project_kernel(
    halves,
    slots_ref,
    gain_ref,
    key_weight_ref,
    value_weight_ref,
    even_ref,
    odd_ref,
    out_ref,
    normed_ref,
    pick_ref,
    weight_ref,
):
    patches = even_ref.shape[1]
    local = key_weight_ref.shape[1]

    @pl.when(pl.program_id(0) == 0)
    def _():
        build_pick(slots_ref, pick_ref, halves)
        weight_ref[:, :local] = key_weight_ref[...]
        weight_ref[:, local:] = value_weight_ref[...]

    gain = gain_ref[...]
    for index, tokens_ref in enumerate((even_ref, odd_ref)):
        for start in range(0, patches, ROWS):
            normed = normalize_rows(tokens_ref[0, pl.ds(start, ROWS), :], gain)
            normed_ref[pl.ds(index * patches + start, ROWS), :] = normed
    product = jnp.dot(normed_ref[...], weight_ref[...], preferred_element_type=jnp.float32).astype(jnp.bfloat16)
    product = jnp.concatenate([product[:patches], product[patches:]], axis=1)
    picked = jnp.dot(pick_ref[...], product, preferred_element_type=jnp.float32)
    groups = picked.shape[0] // GROUP
    picked = [
        picked[:, index * 2 * local : (index + 1) * 2 * local].reshape(groups, 1, GROUP, 2 * local) for index in range(2)
    ]
    picked = jnp.concatenate(picked, axis=1).reshape(out_ref.shape[0], 2 * BLOCK, 2 * local)
    out_ref[:, 0] = picked.astype(jnp.bfloat16)


def project(slots, tokens, gain, key_weight, value_weight, halves):
    levels, patches, width = tokens.shape
    local = key_weight.shape[1]
    count = slots.size
    steps = (levels + 1) // 2
    whole = lambda i: (0, 0)
    return pl.pallas_call(
        functools.partial(project_kernel, halves),
        grid=(steps,),
        in_specs=[
            pl.BlockSpec(slots.shape, whole),
            pl.BlockSpec((1, width), whole),
            pl.BlockSpec((width, local), whole),
            pl.BlockSpec((width, local), whole),
            pl.BlockSpec((1, patches, width), lambda i: (2 * i, 0, 0)),
            pl.BlockSpec((1, patches, width), lambda i: (jnp.minimum(2 * i + 1, levels - 1), 0, 0)),
        ],
        out_specs=pl.BlockSpec((count // BLOCK, 1, 2 * BLOCK, 2 * local), lambda i: (0, i, 0, 0)),
        out_shape=jax.ShapeDtypeStruct((count // BLOCK, steps, 2 * BLOCK, 2 * local), jnp.bfloat16),
        scratch_shapes=[
            pltpu.VMEM((2 * patches, width), jnp.bfloat16),
            pltpu.VMEM((count, patches), jnp.bfloat16),
            pltpu.VMEM((width, 2 * local), jnp.bfloat16),
        ],
        compiler_params=params(58),
        cost_estimate=pl.CostEstimate(
            flops=8 * levels * patches * (width + count) * local,
            bytes_accessed=2 * levels * patches * (width + 2 * local) + 4 * width * local,
            transcendentals=0,
        ),
        name="norm_project",
    )(slots, gain.reshape(1, width), key_weight, value_weight, tokens, tokens)


def attend_kernel(levels, query_ref, pair_ref, *refs):
    out_ref = refs[-1]
    blocks, level_pairs, block, local = pair_ref.shape
    block, local = block // 2, local // 2
    slots = blocks * block
    latents = out_ref.shape[0] // slots
    rows = GROUP * latents
    heads = local // HEAD_DIM
    columns = level_pairs * 2 * GROUP
    lane_head = lax.broadcasted_iota(jnp.int32, (rows, local), 1) // HEAD_DIM
    row_slot = lax.broadcasted_iota(jnp.int32, (GROUP, heads * rows), 0)
    column_slot = (lax.broadcasted_iota(jnp.int32, (GROUP, heads * rows), 1) // latents) & (GROUP - 1)
    same = row_slot - column_slot == 0
    scale = math.log2(math.e) / math.sqrt(HEAD_DIM)
    queries = query_ref[...].reshape(slots * latents, local).astype(jnp.float32)

    def columns_of(start, lane):
        part = pl.ds(start % block * 2, 2 * GROUP)
        return pair_ref[start // block, :, part, pl.ds(lane, local)].reshape(columns, local)

    for first in range(0, slots, STAGE):
        tasks = range(first, first + STAGE, GROUP)
        scores = []
        for start in tasks:
            part = queries[start * latents : start * latents + rows]
            part = jnp.concatenate(
                [jnp.where(lane_head == head, part, 0.0).astype(jnp.bfloat16) for head in range(heads)], axis=0
            )
            product = lax.dot_general(
                columns_of(start, 0), part, (((1,), (1,)), ((), ())), preferred_element_type=jnp.float32
            )
            scores.append(product.reshape(2 * level_pairs, GROUP, heads * rows))
        softs = []
        for product in scores:
            product = product[:levels]
            expo = jnp.exp2((product - jnp.max(product, axis=0, keepdims=True)) * scale)
            inverse = jnp.where(same, 1.0 / jnp.sum(expo, axis=0), 0.0)
            soft = expo * inverse[None]
            if levels < 2 * level_pairs:
                soft = jnp.concatenate([soft, jnp.zeros_like(soft[:1])], axis=0)
            softs.append(soft.reshape(columns, heads * rows).astype(jnp.bfloat16))
        for start, soft in zip(tasks, softs):
            wide = lax.dot_general(
                soft, columns_of(start, local), (((0,), (0,)), ((), ())), preferred_element_type=jnp.float32
            )
            mixed = wide[:rows]
            for head in range(1, heads):
                mixed = jnp.where(lane_head == head, wide[head * rows : (head + 1) * rows], mixed)
            out_ref[pl.ds(start * latents, rows), :] = mixed.astype(jnp.bfloat16)


def attend(queries, pairs, levels, index, after=()):
    stripes, halves, rows, local = queries.shape
    steps = pairs.shape[0] // halves // STEP_BLOCKS
    block = stripes * rows // steps
    pair_shape = (STEP_BLOCKS, *pairs.shape[1:])
    return pl.pallas_call(
        functools.partial(attend_kernel, levels),
        grid=(steps,),
        in_specs=[
            pl.BlockSpec((stripes // steps, 1, rows, local), lambda i: (i, index, 0, 0)),
            pl.BlockSpec(pair_shape, lambda i: (index * steps + i, 0, 0, 0)),
        ]
        + [pl.BlockSpec(memory_space=pl.ANY)] * len(after),
        out_specs=pl.BlockSpec((block, local), lambda i: (i, 0)),
        out_shape=jax.ShapeDtypeStruct((steps * block, local), jnp.bfloat16),
        compiler_params=params(55),
        cost_estimate=pl.CostEstimate(
            flops=1024 * steps * block * levels * local,
            bytes_accessed=4 * steps * (block + levels * STEP_BLOCKS * BLOCK) * local,
            transcendentals=0,
        ),
        name="attend_slots",
    )(queries, pairs, *after)


def combine_rows(mixed_refs, weight_refs, part):
    total = None
    for mixed_ref, weight_ref in zip(mixed_refs, weight_refs):
        term = jnp.dot(mixed_ref[part, :], weight_ref[...], preferred_element_type=jnp.float32)
        term = term.astype(jnp.bfloat16).astype(jnp.float32)
        total = term if total is None else total + term
    return total.astype(jnp.bfloat16)


def combine_home_kernel(place_ref, *refs):
    for distance, out_ref in enumerate(refs[8:]):
        rows = out_ref.shape[0] * out_ref.shape[1]
        start = jnp.bitwise_xor(place_ref[0], distance) * rows
        part = pl.ds(pl.multiple_of(start, rows), rows)
        out_ref[...] = combine_rows(refs[:4], refs[4:8], part).reshape(out_ref.shape)


def combine_kernel(place_ref, *refs):
    out_ref = refs[-1]
    stripes, caps, latents, local = out_ref.shape
    for stripe in range(stripes):
        part = pl.ds(stripe * caps * latents, caps * latents)
        rows = combine_rows(refs[:4], refs[4:8], part)
        out_ref[stripe] = rows.reshape(caps, latents, local)


def term_of(mixed_ref, weight_ref, part):
    term = jnp.dot(mixed_ref[part, :], weight_ref[...], preferred_element_type=jnp.float32)
    return term.astype(jnp.bfloat16).astype(jnp.float32)


def combine_most_kernel(place_ref, *refs):
    out_ref, total_ref = refs[-2:]
    rest = refs[4:-2]
    stripes = out_ref.shape[0]
    half = out_ref.shape[1] - rest[0].shape[0]
    for distance, ref in enumerate(rest):
        out_ref[jnp.bitwise_xor(place_ref[0], distance), half:] = ref[...]
    rows = total_ref.shape[0] // stripes
    for stripe in range(stripes):
        part = pl.ds(stripe * rows, rows)
        total_ref[part, :] = term_of(refs[0], refs[2], part) + term_of(refs[1], refs[3], part)


def combine_last_kernel(first_ref, second_ref, first_weight_ref, second_weight_ref, total_ref, whole_ref, out_ref):
    stripes, half, latents, local = out_ref.shape
    rows = half * latents
    for stripe in range(stripes):
        part = pl.ds(stripe * rows, rows)
        total = total_ref[part, :] + term_of(first_ref, first_weight_ref, part)
        total = total + term_of(second_ref, second_weight_ref, part)
        out_ref[stripe] = total.astype(jnp.bfloat16).reshape(half, latents, local)


def combine_last(mixed, weights, total, whole):
    stripes, caps, latents, local = whole.shape
    half = total.shape[0] // stripes // latents
    operands = (*mixed, *weights, total)
    specs = [pl.BlockSpec(array.shape, lambda i: (0, 0)) for array in operands]
    return pl.pallas_call(
        combine_last_kernel,
        grid=(1,),
        in_specs=specs + [pl.BlockSpec(memory_space=pl.ANY)],
        out_specs=pl.BlockSpec((stripes, half, latents, local), lambda i: (0, 0, 0, 0)),
        out_shape=jax.ShapeDtypeStruct(whole.shape, whole.dtype),
        input_output_aliases={len(operands): 0},
        compiler_params=params(20),
        cost_estimate=pl.CostEstimate(flops=12 * total.size * local, bytes_accessed=10 * total.size, transcendentals=0),
        name="combine_last",
    )(*operands, whole)


def combine(kernel, place, groups, weights, out_shape, rest=()):
    operands = (*groups, *weights, *rest)
    rows, local = groups[0].shape

    def block(array):
        return pl.BlockSpec(array.shape, lambda i: (0,) * len(array.shape))

    return pl.pallas_call(
        kernel,
        grid=(1,),
        in_specs=[pl.BlockSpec(memory_space=pltpu.SMEM)] + [block(array) for array in operands],
        out_specs=jax.tree.map(block, out_shape),
        out_shape=out_shape,
        compiler_params=params(20),
        cost_estimate=pl.CostEstimate(
            flops=24 * rows * local * local, bytes_accessed=10 * rows * local, transcendentals=0
        ),
        name="combine_groups",
    )(place, *operands)


def swap(array, axis_name, distance):
    size = lax.axis_size(axis_name)
    return lax.ppermute(array, axis_name, [(i, i ^ distance) for i in range(size)])


def follow(array, *others):
    return lax.optimization_barrier((array, *others))[0]


def spread_heads(mixed, others=()):
    second = swap(mixed, "head", 2)
    return mixed, swap(mixed, "head", 1), second, swap(follow(second, *others), "head", 1)


def exchange(array, stripes):
    array = array.reshape(stripes, -1, *array.shape[1:])
    return lax.all_to_all(array, "lat", split_axis=0, concat_axis=0, tiled=True)


def spread_weight(out_weight, head):
    local = out_weight.shape[0]
    parts = []
    for distance in range(lax.axis_size("head")):
        start = jnp.bitwise_xor(head, distance) * local
        part = lax.dynamic_slice_in_dim(out_weight, start, local, 1)
        parts.append(swap(part, "head", distance) if distance else part)
    return parts


def shards(level_tokens, ln_gain, key_weight, value_weight, out_weight, ocean_queries, send_slots):
    stripes = lax.axis_size("lat")
    caps = send_slots.shape[2]
    shape = ocean_queries.shape
    slots, latents, local = shape
    place = lax.axis_index("lat").reshape(1)
    halves = 2 if caps == BLOCK else 1
    queries = exchange(ocean_queries, stripes).reshape(stripes, halves, -1, local)
    weights = spread_weight(out_weight, lax.axis_index("head"))
    tokens = jnp.transpose(level_tokens, (1, 0, 2))
    levels = tokens.shape[0]
    pairs = project(send_slots[0], tokens, ln_gain, key_weight, value_weight, halves)
    pairs, weights = lax.optimization_barrier((pairs, weights))
    whole = jax.ShapeDtypeStruct((stripes, caps, latents, local), jnp.bfloat16)
    if halves == 1:
        mixed = exchange(attend(queries, pairs, levels, 0), stripes).reshape(-1, local)
        return combine(combine_kernel, place, spread_heads(mixed), weights, whole).reshape(shape)
    late = attend(queries, pairs, levels, 1)
    early = attend(queries, pairs, levels, 0, (late,))
    chunks = [jax.ShapeDtypeStruct((caps // 2, latents, local), jnp.bfloat16)] * stripes
    chunks = combine(combine_home_kernel, place, spread_heads(late, (early,)), weights, chunks)
    chunks = [swap(chunk, "lat", distance) if distance else chunk for distance, chunk in enumerate(chunks)]
    near, far = chunks[: stripes // 2], chunks[stripes // 2 :]
    early = follow(exchange(early, stripes), *near).reshape(-1, local)
    own, across, second, third = spread_heads(early, far)
    most_shape = (whole, jax.ShapeDtypeStruct(early.shape, jnp.float32))
    out, total = combine(combine_most_kernel, place, (own, second), weights[::2], most_shape, chunks)
    return combine_last((across, third), weights[1::2], total, out).reshape(shape)


def solution(mesh):
    return jax.shard_map(
        shards,
        mesh=mesh,
        in_specs=(
            P("lat", None, None),
            P(),
            P(None, "head"),
            P(None, "head"),
            P("head", None),
            P("lat", None, "head"),
            P("lat", None, None),
        ),
        out_specs=P("lat", None, "head"),
        check_vma=False,
    )
```
